32 devices in a mesh: lev: 2 (over x), tile: 16 (over z, y, core).
Axes of the slice: x: 2, y: 2, z: 4, core: 2. Of those that a mesh axis runs over, the one named last changes fastest.
Arguments:
- adjoint: float32 [5, 16, 256, 256], P(None, 'lev', 'tile'), may hold values from -6 to 6
- courant: float32 [2, 16, 256, 256], P(None, 'lev', 'tile'), may hold values from -0.6 to 0.6
- metric: float32 [2, 16, 256, 256], P(None, 'lev', 'tile'), may hold values from 0.5 to 2
- pivot_inverse: float32 [4, 16, 256, 256], P(None, 'lev', 'tile'), may hold values from -0.06 to 0.2
- lower_gain: float32 [4, 16, 256, 256], P(None, 'lev', 'tile'), may hold values from -0.5 to 1
- upper_gain: float32 [4, 16, 256, 256], P(None, 'lev', 'tile'), may hold values from -0.5 to 1
Outputs:
- stepped: float32 [5, 16, 256, 256], P(None, 'lev', 'tile')
The draws below stay inside these ranges and needn't reach their ends.
All inputs are finite; a program needn't handle non-finite values.
Results may differ from the reference program's by a relative error of at most 0.00002.
Values sent between devices are 32-bit elements; how exact they have to be, the bound alone decides.
No kernel may reach another device: no remote copies, remote signals or barrier semaphores. Data moves between devices by JAX's collectives and lax.ppermute only.
A program may use at most 64 MiB of HBM per device.

```python
import math
import jax
import jax.numpy as jnp
from jax import lax

CY = 256
LEVELS = 16
NX = 256


def draw_pivot_inverse(key, part):
    domain_extent = (2, LEVELS, NX, CY)
    first_key, second_random_key = jax.random.split(key)
    main_diagonal = jnp.exp(jax.random.uniform(first_key, domain_extent, jnp.float32, math.log(0.05), math.log(0.2)))
    crossing = jax.random.uniform(second_random_key, domain_extent, jnp.float32, -0.06, 0.06)
    return jnp.stack([main_diagonal[0], crossing[0], crossing[1], main_diagonal[1]])


def gain_draw(key, marker):
    seeded = jax.random.fold_in(key, marker)
    first_key, second_random_key, third_key = jax.random.split(seeded, 3)
    domain_extent = (2, LEVELS, NX, CY)
    rate = jnp.exp(jax.random.uniform(first_key, domain_extent, jnp.float32, min(math.log(0.3 / LEVELS), math.log(1.0 / 40.0)), math.log(1.0 / 30.0)))
    main_diagonal = jnp.exp(-rate)
    pulse_groups = jax.random.bernoulli(second_random_key, 1.0 / 32.0, domain_extent)
    main_diagonal = jnp.where(pulse_groups, 0.6 * main_diagonal, main_diagonal)
    crossing = jax.random.uniform(third_key, domain_extent, jnp.float32, -1.0, 1.0) * 0.5 * (1.0 - main_diagonal)
    return jnp.stack([main_diagonal[0], crossing[0], crossing[1], main_diagonal[1]])


def draw_lower_gain(key, part):
    return gain_draw(key, 11)


def draw_upper_gain(key, part):
    return gain_draw(key, 23)


def block_scale(key, shape, shards, low, largest):
    def one(position, blocks):
        steps = jax.random.uniform(jax.random.fold_in(jax.random.fold_in(key, 6), position), (blocks,), jnp.float32, low / len(shards), largest / len(shards))
        return jnp.repeat(jnp.exp(steps), shape[position] // blocks).reshape((-1,) + (1,) * (len(shape) - position - 1))

    gain = one(*shards[0])
    for cut in shards[1:]:
        gain = gain * one(*cut)
    return gain


def centred(rng, dims, scale, limit, shards=(), kind=jnp.bfloat16):
    result = scale * jax.random.normal(rng, dims, jnp.float32)
    if shards:
        result = result * block_scale(rng, dims, shards, -0.22, 0.18)
    return jnp.clip(result, -limit, limit).astype(kind)


def setup_inputs(seed: int = 0) -> dict:
    key_of = jax.random.split(jax.random.key(seed), 7)
    adjoint = centred(key_of[0], (5, LEVELS, NX, CY), 1.0, 6.0, ((1, 2), (2, 16)), jnp.float32)
    courant = jnp.clip(jax.random.uniform(key_of[1], (2, LEVELS, NX, CY), jnp.float32, -0.6, 0.6) * block_scale(key_of[1], (2, LEVELS, NX, CY), ((1, 2), (2, 16)), -0.4, 0.0), -0.6, 0.6)
    metric = jnp.clip(jnp.exp(math.log(2.0) - 1.3862944 * jax.random.uniform(key_of[2], (2, LEVELS, NX, CY), jnp.float32) ** block_scale(key_of[2], (2, LEVELS, NX, CY), ((1, 2), (2, 16)), -0.2, 0.2)), 0.5, 2.0)
    pivot_inverse = draw_pivot_inverse(jax.random.fold_in(key_of[6], 71), 0)
    lower_gain = draw_lower_gain(jax.random.fold_in(key_of[6], 71), 0)
    upper_gain = draw_upper_gain(jax.random.fold_in(key_of[6], 71), 0)
    return {"adjoint": adjoint, "courant": courant, "metric": metric, "pivot_inverse": pivot_inverse, "lower_gain": lower_gain, "upper_gain": upper_gain}


def centered_roll(values, axis_id):
    ahead_one = jnp.roll(values, -1, axis_id)
    behind_one = jnp.roll(values, 1, axis_id)
    ahead_two = jnp.roll(values, -2, axis_id)
    behind_two = jnp.roll(values, 2, axis_id)
    return (8.0 * (ahead_one - behind_one) - (ahead_two - behind_two)) / 12.0


def mat_vec(system_matrix, vector):
    return jnp.stack([system_matrix[0] * vector[0] + system_matrix[1] * vector[1],
                      system_matrix[2] * vector[0] + system_matrix[3] * vector[1]])


def chain_run(coupling, forcing, initial, backward):
    def advance(state, inputs):
        fresh = mat_vec(inputs[0], state) + inputs[1]
        return fresh, fresh

    final_state, states = lax.scan(advance, initial,
                                   (jnp.moveaxis(coupling, 1, 0), jnp.moveaxis(forcing, 1, 0)),
                                   reverse=backward)
    return jnp.moveaxis(states, 0, 1)


def reference(adjoint, courant, metric, pivot_inverse, lower_gain, upper_gain):
    advected = adjoint + centered_roll(courant[0] * adjoint, 2) + centered_roll(courant[1] * adjoint, 3)
    pressure_field = advected[4] + centered_roll(metric[0] * adjoint[0], 1) + centered_roll(metric[1] * adjoint[1], 2)
    forcing = mat_vec(pivot_inverse, jnp.stack([advected[2], pressure_field]))
    initial = jnp.zeros((2,) + adjoint.shape[2:], jnp.float32)
    lowered = chain_run(lower_gain, forcing, initial, False)
    solved = chain_run(upper_gain, lowered, initial, True)
    return jnp.stack([advected[0], advected[1], solved[0], advected[3], solved[1]])
```

```python
import jax
import jax.numpy as jnp
from jax import lax
from jax.experimental import pallas as pl
from jax.experimental.pallas import tpu as pltpu
from jax.sharding import PartitionSpec as P

F32 = jnp.float32
VMEM_LIMIT = 24 * 1024 * 1024


def held(shape):
    return pltpu.VMEM(shape, F32)


def whole():
    return pl.BlockSpec(memory_space=pltpu.VMEM)


def params():
    return pltpu.CompilerParams(vmem_limit_bytes=VMEM_LIMIT)


def mul(m, v):
    return (m[0] * v[0] + m[1] * v[1], m[2] * v[0] + m[3] * v[1])


def matmul(m, n):
    return (
        m[0] * n[0] + m[1] * n[2],
        m[0] * n[1] + m[1] * n[3],
        m[2] * n[0] + m[3] * n[2],
        m[2] * n[1] + m[3] * n[3],
    )


def add(a, b):
    return tuple(x + y for x, y in zip(a, b, strict=True))


def at(ref, level):
    return tuple(ref[k, level] for k in range(ref.shape[0]))


def even_tile():
    return lax.rem(lax.axis_index("tile"), 2) == 0


def edges_body(adj, courant, metric, chip, far):
    rows = adj.shape[2]

    def emit(out, first):
        for r in range(2):
            wind = courant[0, :, first + r, :]
            for k in range(4):
                out[k, r] = wind * adj[k, :, first + r, :]
            out[4, r] = (
                wind * adj[4, :, first + r, :]
                + metric[0, :, first + r, :] * adj[0, :, first + r, :]
            )

    @pl.when(even_tile())
    def _():
        emit(chip, rows - 2)
        emit(far, 0)

    @pl.when(jnp.logical_not(even_tile()))
    def _():
        emit(chip, 0)
        emit(far, rows - 2)


def across(q):
    rows = q.shape[0]
    spot = lax.broadcasted_iota(jnp.int32, q.shape, 0)
    out = None
    for step, weight in ((1, 8.0 / 12.0), (2, -1.0 / 12.0)):
        ahead = jnp.where(spot < rows - step, pltpu.roll(q, rows - step, 0), 0.0)
        behind = jnp.where(spot >= step, pltpu.roll(q, step, 0), 0.0)
        term = weight * (ahead - behind)
        out = term if out is None else out + term
    return out


def along(q):
    cols = q.shape[1]
    near = pltpu.roll(q, cols - 1, 1) - pltpu.roll(q, 1, 1)
    wide = pltpu.roll(q, cols - 2, 1) - pltpu.roll(q, 2, 1)
    return (8.0 / 12.0) * near - (1.0 / 12.0) * wide


def inner_body(adj, courant, metric, lower, upper, passive, active, response):
    levels = adj.shape[1]

    def one(l, _):
        c0, c1 = courant[0, l], courant[1, l]
        for k, slot in ((0, 0), (1, 1), (3, 2)):
            x = adj[k, l]
            passive[slot, l] = x + across(c0 * x) + along(c1 * x)
        x = adj[2, l]
        active[0, l] = x + across(c0 * x) + along(c1 * x)
        x = adj[4, l]
        active[1, l] = (
            x
            + across(c0 * x + metric[0, l] * adj[0, l])
            + along(c1 * x + metric[1, l] * adj[1, l])
        )
        return 0

    lax.fori_loop(0, levels, one, 0)
    chain = [at(lower, 0)]
    for l in range(1, levels):
        chain.append(matmul(at(lower, l), chain[-1]))
    total = chain[-1]
    for l in range(levels - 2, -1, -1):
        total = add(matmul(at(upper, l), total), chain[l])
    for k in range(4):
        response[k] = total[k]


def halo_rows(chip, far, field):
    even = even_tile()
    got_chip = [chip[field, r] for r in range(2)]
    got_far = [far[field, r] for r in range(2)]
    low = [jnp.where(even, b, a) for a, b in zip(got_chip, got_far, strict=True)]
    high = [jnp.where(even, a, b) for a, b in zip(got_chip, got_far, strict=True)]
    return low, high


def add_halo(ref, slot, low, high):
    rows = ref.shape[2]
    near, wide = 8.0 / 12.0, 1.0 / 12.0
    ref[slot, :, 0, :] = ref[slot, :, 0, :] + (wide * low[0] - near * low[1])
    ref[slot, :, 1, :] = ref[slot, :, 1, :] + wide * low[1]
    ref[slot, :, rows - 2, :] = ref[slot, :, rows - 2, :] - wide * high[0]
    ref[slot, :, rows - 1, :] = ref[slot, :, rows - 1, :] + (
        near * high[0] - wide * high[1]
    )


def sweep_body(active, pivot, lower, upper, response, chip, far, lowered, summary, held_active):
    levels = active.shape[1]
    held_active[...] = active[...]
    for slot, field in ((0, 2), (1, 4)):
        add_halo(held_active, slot, *halo_rows(chip, far, field))
    states = []
    for l in range(levels):
        fresh = mul(at(pivot, l), at(held_active, l))
        if states:
            fresh = add(mul(at(lower, l), states[-1]), fresh)
        states.append(fresh)
        for k in range(2):
            lowered[k, l] = fresh[k]

    @pl.when(lax.axis_index("lev") == 0)
    def _():
        for k in range(2):
            summary[k] = states[-1][k]

    @pl.when(lax.axis_index("lev") == 1)
    def _():
        state = at(lowered, levels - 1)
        for l in range(levels - 2, -1, -1):
            state = add(mul(at(upper, l), state), at(lowered, l))
        for k in range(2):
            summary[k] = state[k]
        for k in range(4):
            summary[2 + k] = response[k]


def passive_body(passive, chip, far, out, held_passive, sems):
    held_passive[...] = passive[...]
    copies = []
    for slot, field in ((0, 0), (1, 1), (2, 3)):
        add_halo(held_passive, slot, *halo_rows(chip, far, field))
        copies.append(
            pltpu.make_async_copy(held_passive.at[slot], out.at[field], sems.at[slot])
        )
        copies[-1].start()
    for copy in copies:
        copy.wait()


def solve_body(lowered, lower, upper, mine, summary, partial, out, solved, sems):
    del partial
    levels = lowered.shape[1]

    @pl.when(lax.axis_index("lev") == 0)
    def _():
        state = (mine[0], mine[1])
        gain = tuple(summary[2 + k] for k in range(4))
        state = add(mul(gain, state), (summary[0], summary[1]))
        for l in range(levels - 1, -1, -1):
            state = add(mul(at(upper, l), state), at(lowered, l))
            for k in range(2):
                solved[k, l] = state[k]

    @pl.when(lax.axis_index("lev") == 1)
    def _():
        entering = (summary[0], summary[1])
        full = []
        for l in range(levels):
            entering = mul(at(lower, l), entering)
            full.append(add(entering, at(lowered, l)))
        state = full[-1]
        for l in range(levels - 1, -1, -1):
            if l < levels - 1:
                state = add(mul(at(upper, l), state), full[l])
            for k in range(2):
                solved[k, l] = state[k]

    copies = [
        pltpu.make_async_copy(solved.at[k], out.at[field], sems.at[k])
        for k, field in ((0, 2), (1, 4))
    ]
    for copy in copies:
        copy.start()
    for copy in copies:
        copy.wait()


def local_pair(adjoint, courant, metric, pivot_inverse, lower_gain, upper_gain):
    fields, levels, rows, cols = adjoint.shape
    tiles = lax.axis_size("tile")
    chip, far = pl.pallas_call(
        edges_body,
        name="edges",
        in_specs=[whole()] * 3,
        out_specs=[whole()] * 2,
        out_shape=[held((fields, 2, levels, cols))] * 2,
        compiler_params=params(),
    )(adjoint, courant, metric)
    with_chip = [(i, i ^ 1) for i in range(tiles)]
    with_far = [(i, (i - 1 if i % 2 == 0 else i + 1) % tiles) for i in range(tiles)]
    got_far = lax.ppermute(far, "tile", with_far)
    got_chip = lax.ppermute(chip, "tile", with_chip)
    passive, active, response = pl.pallas_call(
        inner_body,
        name="inner",
        in_specs=[whole()] * 5,
        out_specs=[whole()] * 3,
        out_shape=[
            held((3, levels, rows, cols)),
            held((2, levels, rows, cols)),
            held((4, rows, cols)),
        ],
        compiler_params=params(),
    )(adjoint, courant, metric, lower_gain, upper_gain)
    lowered, summary = pl.pallas_call(
        sweep_body,
        name="sweep",
        in_specs=[whole()] * 7,
        out_specs=[whole()] * 2,
        out_shape=[held((2, levels, rows, cols)), held((6, rows, cols))],
        scratch_shapes=[pltpu.VMEM((2, levels, rows, cols), F32)],
        compiler_params=params(),
    )(active, pivot_inverse, lower_gain, upper_gain, response, got_chip, got_far)
    received = lax.ppermute(summary, "lev", [(0, 1), (1, 0)])
    partial = pl.pallas_call(
        passive_body,
        name="passive",
        in_specs=[whole()] * 3,
        out_specs=pl.BlockSpec(memory_space=pl.ANY),
        out_shape=jax.ShapeDtypeStruct(adjoint.shape, F32),
        scratch_shapes=[
            pltpu.VMEM((3, levels, rows, cols), F32),
            pltpu.SemaphoreType.DMA((3,)),
        ],
        compiler_params=params(),
    )(passive, got_chip, got_far)
    return pl.pallas_call(
        solve_body,
        name="solve",
        in_specs=[whole()] * 5 + [pl.BlockSpec(memory_space=pl.ANY)],
        out_specs=pl.BlockSpec(memory_space=pl.ANY),
        out_shape=jax.ShapeDtypeStruct(adjoint.shape, F32),
        scratch_shapes=[
            pltpu.VMEM((2, levels, rows, cols), F32),
            pltpu.SemaphoreType.DMA((2,)),
        ],
        input_output_aliases={5: 0},
        compiler_params=params(),
    )(lowered, lower_gain, upper_gain, summary, received, partial)


LEVEL_UNROLL = 16


def with_halo(block, sides, width):
    for axis, dim in sides:
        count = lax.axis_size(axis)
        forward = [(i, i + 1) for i in range(count - 1)]
        forward.append((count - 1, 0))
        backward = [(target, source) for source, target in forward]
        low = lax.ppermute(
            lax.slice_in_dim(block, block.shape[dim] - width, None, axis=dim), axis, forward
        )
        high = lax.ppermute(lax.slice_in_dim(block, 0, width, axis=dim), axis, backward)
        block = jnp.concatenate([low, block, high], axis=dim)
    return block


def centered_roll(values, axis_id):
    ahead_one = jnp.roll(values, -1, axis_id)
    behind_one = jnp.roll(values, 1, axis_id)
    ahead_two = jnp.roll(values, -2, axis_id)
    behind_two = jnp.roll(values, 2, axis_id)
    return (8.0 * (ahead_one - behind_one) - (ahead_two - behind_two)) / 12.0


def centered_padded(padded):
    ahead_one = padded[:, :, 3:-1, :]
    behind_one = padded[:, :, 1:-3, :]
    ahead_two = padded[:, :, 4:, :]
    behind_two = padded[:, :, :-4, :]
    return (8.0 * (ahead_one - behind_one) - (ahead_two - behind_two)) / 12.0


def mat_vec(system_matrix, vector):
    return jnp.stack(
        [
            system_matrix[0] * vector[0] + system_matrix[1] * vector[1],
            system_matrix[2] * vector[0] + system_matrix[3] * vector[1],
        ]
    )


def chain_run(coupling, forcing, initial, backward):

    def advance(state, inputs):
        fresh = mat_vec(inputs[0], state) + inputs[1]
        return (fresh, fresh)

    final_state, states = lax.scan(
        advance,
        initial,
        (jnp.moveaxis(coupling, 1, 0), jnp.moveaxis(forcing, 1, 0)),
        reverse=backward,
        unroll=min(LEVEL_UNROLL, coupling.shape[1]),
    )
    return jnp.moveaxis(states, 0, 1)


def column_solve(pieces):
    forcing, lower_part, upper_part = pieces
    initial = jnp.zeros((2,) + forcing.shape[2:], jnp.float32)
    lowered = chain_run(lower_part, forcing, initial, False)
    solved = chain_run(upper_part, lowered, initial, True)
    return lax.all_to_all(solved, "lev", split_axis=1, concat_axis=2, tiled=True)


def local_any(adjoint, courant, metric, pivot_inverse, lower_gain, upper_gain):
    weighted = jnp.concatenate([courant[0] * adjoint, (metric[0] * adjoint[0])[None]], 0)
    padded = with_halo(weighted, (("tile", 2),), 2)
    across = centered_padded(padded)
    advected = adjoint + across[:5] + centered_roll(courant[1] * adjoint, 3)
    pressure_field = advected[4] + across[5] + centered_roll(metric[1] * adjoint[1], 2)
    forcing = mat_vec(pivot_inverse, jnp.stack([advected[2], pressure_field]))
    solved = column_solve(
        (
            lax.all_to_all(forcing, "lev", split_axis=2, concat_axis=1, tiled=True),
            lax.all_to_all(lower_gain, "lev", split_axis=2, concat_axis=1, tiled=True),
            lax.all_to_all(upper_gain, "lev", split_axis=2, concat_axis=1, tiled=True),
        )
    )
    return jnp.stack([advected[0], advected[1], solved[0], advected[3], solved[1]])


def solution(mesh):
    placed = (P(None, "lev", "tile", None),) * 6
    pair = mesh.shape["lev"] == 2 and mesh.shape["tile"] % 2 == 0
    return jax.shard_map(
        local_pair if pair else local_any,
        mesh=mesh,
        in_specs=placed,
        out_specs=P(None, "lev", "tile", None),
        check_vma=False,
    )
```

```python
import functools

import jax
import jax.numpy as jnp
from jax import lax
from jax.experimental import pallas as pl
from jax.experimental.pallas import tpu as pltpu
from jax.sharding import PartitionSpec as P

F32 = jnp.float32
VMEM_LIMIT = 24 * 1024 * 1024


def held(shape):
    return pltpu.VMEM(shape, F32)


def whole():
    return pl.BlockSpec(memory_space=pltpu.VMEM)


def in_hbm():
    return pl.BlockSpec(memory_space=pltpu.HBM)


def from_hbm(x):
    return pltpu.with_memory_space_constraint(x, pltpu.HBM)


def params():
    return pltpu.CompilerParams(vmem_limit_bytes=VMEM_LIMIT)


def mul(m, v):
    return (m[0] * v[0] + m[1] * v[1], m[2] * v[0] + m[3] * v[1])


def matmul(m, n):
    return (
        m[0] * n[0] + m[1] * n[2],
        m[0] * n[1] + m[1] * n[3],
        m[2] * n[0] + m[3] * n[2],
        m[2] * n[1] + m[3] * n[3],
    )


def add(a, b):
    return tuple(x + y for x, y in zip(a, b, strict=True))


def at(ref, level):
    return tuple(ref[k, level] for k in range(ref.shape[0]))


def edge_rows(rows):
    return (0, 1, rows - 2, rows - 1)


def emit_edges(adj, courant, metric, out, first):
    for r in range(2):
        wind = courant[0, :, first + r, :]
        for k in range(4):
            out[k, r] = wind * adj[k, :, first + r, :]
        out[4, r] = wind * adj[4, :, first + r, :]
        out[5, r] = metric[0, :, first + r, :] * adj[0, :, first + r, :]


def fetch_all(sources, targets, sems):
    copies = [
        pltpu.make_async_copy(source, target, sems.at[i])
        for i, (source, target) in enumerate(zip(sources, targets, strict=True))
    ]
    for copy in copies:
        copy.start()
    return copies


def edges_body(
    adj_in, courant_in, metric_in, ahead, adj, courant, metric, sems
):
    for copy in fetch_all(
        (adj_in, courant_in, metric_in), (adj, courant, metric), sems
    ):
        copy.wait()
    emit_edges(adj, courant, metric, ahead, adj.shape[2] - 2)


def across(q):
    rows = q.shape[0]
    spot = lax.broadcasted_iota(jnp.int32, q.shape, 0)
    out = None
    for step, weight in ((1, 8.0 / 12.0), (2, -1.0 / 12.0)):
        ahead = jnp.where(spot < rows - step, pltpu.roll(q, rows - step, 0), 0.0)
        behind = jnp.where(spot >= step, pltpu.roll(q, step, 0), 0.0)
        term = weight * (ahead - behind)
        out = term if out is None else out + term
    return out


def along(q):
    cols = q.shape[1]
    near = pltpu.roll(q, cols - 1, 1) - pltpu.roll(q, 1, 1)
    wide = pltpu.roll(q, cols - 2, 1) - pltpu.roll(q, 2, 1)
    return (8.0 / 12.0) * near - (1.0 / 12.0) * wide


def active_body(early, adj, courant, metric, *refs):
    gains_in = refs[:3]
    if early:
        emit_edges(adj, courant, metric, refs[3], 0)
    summary, active, pivot, lower, upper, sems = refs[-6:]
    levels = adj.shape[1]
    here = lax.axis_index("tile") == 0

    @pl.when(here if early else jnp.logical_not(here))
    def _():
        copies = fetch_all(gains_in, (lower, upper, pivot), sems)

        def one(l, _):
            c0, c1 = courant[0, l], courant[1, l]
            x = adj[2, l]
            active[0, l] = x + across(c0 * x) + along(c1 * x)
            x = adj[4, l]
            active[1, l] = (
                x
                + across(c0 * x + metric[0, l] * adj[0, l])
                + along(c1 * x + metric[1, l] * adj[1, l])
            )
            return 0

        lax.fori_loop(0, levels, one, 0)
        for copy in copies:
            copy.wait()
        states = forward(active, pivot, lower)

        @pl.when(lax.axis_index("lev") == 0)
        def _():
            for k in range(2):
                summary[k] = states[-1][k]

        @pl.when(lax.axis_index("lev") == 1)
        def _():
            state = backward_first(states, upper)
            for k in range(2):
                summary[k] = state[k]
            chain = [at(lower, 0)]
            for l in range(1, levels):
                chain.append(matmul(at(lower, l), chain[-1]))
            total = chain[-1]
            for l in range(levels - 2, -1, -1):
                total = add(matmul(at(upper, l), total), chain[l])
            for k in range(4):
                summary[2 + k] = total[k]


def forward(active, pivot, lower):
    states = []
    for l in range(active.shape[1]):
        fresh = mul(at(pivot, l), at(active, l))
        if states:
            fresh = add(mul(at(lower, l), states[-1]), fresh)
        states.append(fresh)
    return states


def backward_first(states, upper):
    state = states[-1]
    for l in range(len(states) - 2, -1, -1):
        state = add(mul(at(upper, l), state), states[l])
    return state


def add_halo(ref, slot, low, high):
    rows = ref.shape[2]
    near, wide = 8.0 / 12.0, 1.0 / 12.0
    ref[slot, :, 0, :] = ref[slot, :, 0, :] + (wide * low[0] - near * low[1])
    ref[slot, :, 1, :] = ref[slot, :, 1, :] + wide * low[1]
    ref[slot, :, rows - 2, :] = ref[slot, :, rows - 2, :] - wide * high[0]
    ref[slot, :, rows - 1, :] = ref[slot, :, rows - 1, :] + (
        near * high[0] - wide * high[1]
    )


def halo_rows(low, high, field):
    lows = [low[field, r] for r in range(2)]
    highs = [high[field, r] for r in range(2)]
    if field == 4:
        lows = [lows[r] + low[5, r] for r in range(2)]
        highs = [highs[r] + high[5, r] for r in range(2)]
    return lows, highs


def sweep_body(active, pivot, lower, upper, low, high, lowered, mine, edges, held_active):
    levels, rows = active.shape[1:3]
    held_active[...] = active[...]
    for slot, field in ((0, 2), (1, 4)):
        add_halo(held_active, slot, *halo_rows(low, high, field))
    states = forward(held_active, pivot, lower)
    for l in range(levels):
        for k in range(2):
            lowered[k, l] = states[l][k]

    def emit(state):
        for k in range(2):
            mine[k] = state[k]
            for i, row in enumerate(edge_rows(rows)):
                edges[pl.ds(4 * k + i, 1)] = state[k][row : row + 1]

    @pl.when(lax.axis_index("lev") == 0)
    def _():
        emit(states[-1])

    @pl.when(lax.axis_index("lev") == 1)
    def _():
        emit(backward_first(states, upper))


def passive_body(adj, courant, low, high, out, done, sems):
    levels = adj.shape[1]
    copies = []

    def one(l, _):
        c0, c1 = courant[0, l], courant[1, l]
        for slot, field in ((0, 0), (1, 1), (2, 3)):
            x = adj[field, l]
            done[slot, l] = x + across(c0 * x) + along(c1 * x)
        return 0

    lax.fori_loop(0, levels, one, 0)
    for slot, field in ((0, 0), (1, 1), (2, 3)):
        add_halo(done, slot, *halo_rows(low, high, field))
        copies.append(
            pltpu.make_async_copy(done.at[slot], out.at[field], sems.at[slot])
        )
        copies[-1].start()
    for copy in copies:
        copy.wait()


def patched(base, edges, k):
    rows = base.shape[0]
    spot = lax.broadcasted_iota(jnp.int32, base.shape, 0)
    for i, row in enumerate(edge_rows(rows)):
        base = jnp.where(spot == row, edges[pl.ds(4 * k + i, 1)], base)
    return base


def solve_body(lowered, lower, upper, mine, summary, edges, partial, out, solved, sems):
    del partial
    levels = lowered.shape[1]
    other = tuple(patched(summary[k], edges, k) for k in range(2))

    @pl.when(lax.axis_index("lev") == 0)
    def _():
        gain = tuple(summary[2 + k] for k in range(4))
        state = add(mul(gain, (mine[0], mine[1])), other)
        for l in range(levels - 1, -1, -1):
            state = add(mul(at(upper, l), state), at(lowered, l))
            for k in range(2):
                solved[k, l] = state[k]

    @pl.when(lax.axis_index("lev") == 1)
    def _():
        entering = other
        full = []
        for l in range(levels):
            entering = mul(at(lower, l), entering)
            full.append(add(entering, at(lowered, l)))
        state = full[-1]
        for l in range(levels - 1, -1, -1):
            if l < levels - 1:
                state = add(mul(at(upper, l), state), full[l])
            for k in range(2):
                solved[k, l] = state[k]

    copies = [
        pltpu.make_async_copy(solved.at[k], out.at[field], sems.at[k])
        for k, field in ((0, 2), (1, 4))
    ]
    for copy in copies:
        copy.start()
    for copy in copies:
        copy.wait()


def local_pair(adjoint, courant, metric, pivot_inverse, lower_gain, upper_gain):
    fields, levels, rows, cols = adjoint.shape
    tiles = lax.axis_size("tile")
    swap = [(0, 1), (1, 0)]
    ahead, adj, cour, met = pl.pallas_call(
        edges_body,
        name="edges",
        in_specs=[in_hbm()] * 3,
        out_specs=[whole()] * 4,
        out_shape=[
            held((fields + 1, 2, levels, cols)),
            held(adjoint.shape),
            held(courant.shape),
            held(metric.shape),
        ],
        scratch_shapes=[pltpu.SemaphoreType.DMA((3,))],
        compiler_params=params(),
    )(from_hbm(adjoint), from_hbm(courant), from_hbm(metric))
    work = [
        held((6, rows, cols)),
        held((2, levels, rows, cols)),
        held(pivot_inverse.shape),
        held(lower_gain.shape),
        held(upper_gain.shape),
    ]
    given = (
        adj, cour, met,
        from_hbm(lower_gain), from_hbm(upper_gain), from_hbm(pivot_inverse),
    )
    low = lax.ppermute(ahead, "tile", [(i, (i + 1) % tiles) for i in range(tiles)])
    behind, *begun = pl.pallas_call(
        functools.partial(active_body, True),
        name="active_first_tile",
        in_specs=[whole()] * 3 + [in_hbm()] * 3,
        out_specs=[whole()] * (1 + len(work)),
        out_shape=[held(ahead.shape)] + work,
        scratch_shapes=[pltpu.SemaphoreType.DMA((3,))],
        compiler_params=params(),
    )(*given)
    high = lax.ppermute(behind, "tile", [(i, (i - 1) % tiles) for i in range(tiles)])
    summary, active, pivot, lower, upper = pl.pallas_call(
        functools.partial(active_body, False),
        name="active_other_tiles",
        in_specs=[whole()] * 3 + [in_hbm()] * 3 + [whole()] * len(work),
        out_specs=[whole()] * len(work),
        out_shape=work,
        scratch_shapes=[pltpu.SemaphoreType.DMA((3,))],
        input_output_aliases={6 + i: i for i in range(len(work))},
        compiler_params=params(),
    )(*given, *begun)
    bulk = lax.ppermute(summary, "lev", swap)
    lowered, mine, edges = pl.pallas_call(
        sweep_body,
        name="sweep",
        in_specs=[whole()] * 6,
        out_specs=[whole()] * 3,
        out_shape=[
            held((2, levels, rows, cols)),
            held((2, rows, cols)),
            held((8, cols)),
        ],
        scratch_shapes=[pltpu.VMEM((2, levels, rows, cols), F32)],
        compiler_params=params(),
    )(active, pivot, lower, upper, low, high)
    got_edges = lax.ppermute(edges, "lev", swap)
    partial = pl.pallas_call(
        passive_body,
        name="passive",
        in_specs=[whole()] * 4,
        out_specs=pl.BlockSpec(memory_space=pl.ANY),
        out_shape=jax.ShapeDtypeStruct(adjoint.shape, F32),
        scratch_shapes=[
            pltpu.VMEM((3, levels, rows, cols), F32),
            pltpu.SemaphoreType.DMA((3,)),
        ],
        compiler_params=params(),
    )(adj, cour, low, high)
    return pl.pallas_call(
        solve_body,
        name="solve",
        in_specs=[whole()] * 6 + [pl.BlockSpec(memory_space=pl.ANY)],
        out_specs=pl.BlockSpec(memory_space=pl.ANY),
        out_shape=jax.ShapeDtypeStruct(adjoint.shape, F32),
        scratch_shapes=[
            pltpu.VMEM((2, levels, rows, cols), F32),
            pltpu.SemaphoreType.DMA((2,)),
        ],
        input_output_aliases={6: 0},
        compiler_params=params(),
    )(lowered, lower, upper, mine, bulk, got_edges, partial)


LEVEL_UNROLL = 16


def with_halo(block, sides, width):
    for axis, dim in sides:
        count = lax.axis_size(axis)
        forward = [(i, i + 1) for i in range(count - 1)]
        forward.append((count - 1, 0))
        backward = [(target, source) for source, target in forward]
        low = lax.ppermute(
            lax.slice_in_dim(block, block.shape[dim] - width, None, axis=dim), axis, forward
        )
        high = lax.ppermute(lax.slice_in_dim(block, 0, width, axis=dim), axis, backward)
        block = jnp.concatenate([low, block, high], axis=dim)
    return block


def centered_roll(values, axis_id):
    ahead_one = jnp.roll(values, -1, axis_id)
    behind_one = jnp.roll(values, 1, axis_id)
    ahead_two = jnp.roll(values, -2, axis_id)
    behind_two = jnp.roll(values, 2, axis_id)
    return (8.0 * (ahead_one - behind_one) - (ahead_two - behind_two)) / 12.0


def centered_padded(padded):
    ahead_one = padded[:, :, 3:-1, :]
    behind_one = padded[:, :, 1:-3, :]
    ahead_two = padded[:, :, 4:, :]
    behind_two = padded[:, :, :-4, :]
    return (8.0 * (ahead_one - behind_one) - (ahead_two - behind_two)) / 12.0


def mat_vec(system_matrix, vector):
    return jnp.stack(
        [
            system_matrix[0] * vector[0] + system_matrix[1] * vector[1],
            system_matrix[2] * vector[0] + system_matrix[3] * vector[1],
        ]
    )


def chain_run(coupling, forcing, initial, backward):

    def advance(state, inputs):
        fresh = mat_vec(inputs[0], state) + inputs[1]
        return (fresh, fresh)

    final_state, states = lax.scan(
        advance,
        initial,
        (jnp.moveaxis(coupling, 1, 0), jnp.moveaxis(forcing, 1, 0)),
        reverse=backward,
        unroll=min(LEVEL_UNROLL, coupling.shape[1]),
    )
    return jnp.moveaxis(states, 0, 1)


def column_solve(pieces):
    forcing, lower_part, upper_part = pieces
    initial = jnp.zeros((2,) + forcing.shape[2:], jnp.float32)
    lowered = chain_run(lower_part, forcing, initial, False)
    solved = chain_run(upper_part, lowered, initial, True)
    return lax.all_to_all(solved, "lev", split_axis=1, concat_axis=2, tiled=True)


def local_any(adjoint, courant, metric, pivot_inverse, lower_gain, upper_gain):
    weighted = jnp.concatenate([courant[0] * adjoint, (metric[0] * adjoint[0])[None]], 0)
    padded = with_halo(weighted, (("tile", 2),), 2)
    across = centered_padded(padded)
    advected = adjoint + across[:5] + centered_roll(courant[1] * adjoint, 3)
    pressure_field = advected[4] + across[5] + centered_roll(metric[1] * adjoint[1], 2)
    forcing = mat_vec(pivot_inverse, jnp.stack([advected[2], pressure_field]))
    solved = column_solve(
        (
            lax.all_to_all(forcing, "lev", split_axis=2, concat_axis=1, tiled=True),
            lax.all_to_all(lower_gain, "lev", split_axis=2, concat_axis=1, tiled=True),
            lax.all_to_all(upper_gain, "lev", split_axis=2, concat_axis=1, tiled=True),
        )
    )
    return jnp.stack([advected[0], advected[1], solved[0], advected[3], solved[1]])


def solution(mesh):
    placed = (P(None, "lev", "tile", None),) * 6
    pair = mesh.shape["lev"] == 2 and mesh.shape["tile"] % 2 == 0
    return jax.shard_map(
        local_pair if pair else local_any,
        mesh=mesh,
        in_specs=placed,
        out_specs=P(None, "lev", "tile", None),
        check_vma=False,
    )
```

```python
import jax
import jax.numpy as jnp
from jax import lax
from jax.experimental import pallas as pl
from jax.experimental.pallas import tpu as pltpu
from jax.sharding import PartitionSpec as P

F32 = jnp.float32
VMEM_LIMIT = 24 * 1024 * 1024


def held(shape):
    return pltpu.VMEM(shape, F32)


def whole():
    return pl.BlockSpec(memory_space=pltpu.VMEM)


def in_hbm():
    return pl.BlockSpec(memory_space=pltpu.HBM)


def from_hbm(x):
    return pltpu.with_memory_space_constraint(x, pltpu.HBM)


def params():
    return pltpu.CompilerParams(vmem_limit_bytes=VMEM_LIMIT)


def mul(m, v):
    return (m[0] * v[0] + m[1] * v[1], m[2] * v[0] + m[3] * v[1])


def matmul(m, n):
    return (
        m[0] * n[0] + m[1] * n[2],
        m[0] * n[1] + m[1] * n[3],
        m[2] * n[0] + m[3] * n[2],
        m[2] * n[1] + m[3] * n[3],
    )


def add(a, b):
    return tuple(x + y for x, y in zip(a, b, strict=True))


def at(ref, level):
    return tuple(ref[k, level] for k in range(ref.shape[0]))


def emit_edges(adj, courant, metric, out, first):
    for r in range(2):
        row = first + r
        wind = courant[0, :, row, :]
        for k in range(4):
            out[k, r] = wind * adj[k, :, row, :]
        out[4, r] = wind * adj[4, :, row, :] + metric[0, :, row, :] * adj[0, :, row, :]


def fetch_all(sources, targets, sems):
    copies = [
        pltpu.make_async_copy(source, target, sems.at[i])
        for i, (source, target) in enumerate(zip(sources, targets, strict=True))
    ]
    for copy in copies:
        copy.start()
    return copies


def tail_rows(ref):
    return ref.at[:, :, pl.ds(ref.shape[2] - 8, 8)]


def head_rows(ref):
    return ref.at[:, :, pl.ds(0, ref.shape[2] - 8)]


def edges_body(
    adj_in, courant_in, metric_in, ahead, adj, courant, metric, sems
):
    first = lax.axis_index("tile") == 0
    given, targets = (adj_in, courant_in, metric_in), (adj, courant, metric)

    @pl.when(first)
    def _():
        for copy in fetch_all(map(tail_rows, given), map(tail_rows, targets), sems):
            copy.wait()

    @pl.when(jnp.logical_not(first))
    def _():
        for copy in fetch_all(given, targets, sems):
            copy.wait()

    emit_edges(adj, courant, metric, ahead, adj.shape[2] - 2)


def across(q):
    rows = q.shape[0]
    spot = lax.broadcasted_iota(jnp.int32, q.shape, 0)
    out = None
    for step, weight in ((1, 8.0 / 12.0), (2, -1.0 / 12.0)):
        ahead = jnp.where(spot < rows - step, pltpu.roll(q, rows - step, 0), 0.0)
        behind = jnp.where(spot >= step, pltpu.roll(q, step, 0), 0.0)
        term = weight * (ahead - behind)
        out = term if out is None else out + term
    return out


def along(q):
    cols = q.shape[1]
    near = pltpu.roll(q, cols - 1, 1) - pltpu.roll(q, 1, 1)
    wide = pltpu.roll(q, cols - 2, 1) - pltpu.roll(q, 2, 1)
    return (8.0 / 12.0) * near - (1.0 / 12.0) * wide


def passive_base(adj, courant, passive):
    def one(l, _):
        c0, c1 = courant[0, l], courant[1, l]
        for slot, field in ((0, 0), (1, 1), (2, 3)):
            x = adj[field, l]
            passive[slot, l] = x + across(c0 * x) + along(c1 * x)
        return 0

    lax.fori_loop(0, adj.shape[1], one, 0)


def first_tile_body(adj_in, courant_in, metric_in, lower_in, upper_in, pivot_in, *refs):
    behind, adj, courant, metric, *work = refs[3:-2]
    sems, head_sems = refs[-2:]
    first = lax.axis_index("tile") == 0

    @pl.when(first)
    def _():
        heads = fetch_all(
            map(head_rows, (adj_in, courant_in, metric_in)),
            map(head_rows, (adj, courant, metric)),
            head_sems,
        )
        gains = fetch_all((lower_in, upper_in, pivot_in), work[-2:] + work[-3:-2], sems)
        for copy in heads:
            copy.wait()
        active_base(adj, courant, metric, work[1])
        summarise(work, gains)

    emit_edges(adj, courant, metric, behind, 0)


def other_tiles_body(adj, courant, metric, lower_in, upper_in, pivot_in, *refs):
    *work, sems = refs[-6:]

    @pl.when(lax.axis_index("tile") > 0)
    def _():
        gains = fetch_all((lower_in, upper_in, pivot_in), work[-2:] + work[-3:-2], sems)
        active_base(adj, courant, metric, work[1])
        summarise(work, gains)


def active_base(adj, courant, metric, active):
    def one(l, _):
        c0, c1 = courant[0, l], courant[1, l]
        x = adj[2, l]
        active[0, l] = x + across(c0 * x) + along(c1 * x)
        x = adj[4, l]
        active[1, l] = (
            x
            + across(c0 * x + metric[0, l] * adj[0, l])
            + along(c1 * x + metric[1, l] * adj[1, l])
        )
        return 0

    lax.fori_loop(0, adj.shape[1], one, 0)


def summarise(work, gains):
    bulk, active, pivot, lower, upper = work
    levels = active.shape[1]
    for copy in gains:
        copy.wait()
    states = forward(active, pivot, lower)

    rows = active.shape[2]

    def emit(state):
        for k in range(2):
            start = 4 * rows + k * (rows - 8)
            bulk[pl.ds(start, rows - 8)] = state[k][4 : rows - 4]

    @pl.when(lax.axis_index("lev") == 0)
    def _():
        emit(states[-1])

    @pl.when(lax.axis_index("lev") == 1)
    def _():
        emit(backward_first(states, upper))
        chain = [at(lower, 0)]
        for l in range(1, levels):
            chain.append(matmul(at(lower, l), chain[-1]))
        total = chain[-1]
        for l in range(levels - 2, -1, -1):
            total = add(matmul(at(upper, l), total), chain[l])
        for k in range(4):
            bulk[pl.ds(k * rows, rows)] = total[k]


def forward(active, pivot, lower):
    states = []
    for l in range(active.shape[1]):
        fresh = mul(at(pivot, l), at(active, l))
        if states:
            fresh = add(mul(at(lower, l), states[-1]), fresh)
        states.append(fresh)
    return states


def backward_first(states, upper):
    state = states[-1]
    for l in range(len(states) - 2, -1, -1):
        state = add(mul(at(upper, l), state), states[l])
    return state


def add_halo(ref, slot, low, high):
    rows = ref.shape[2]
    near, wide = 8.0 / 12.0, 1.0 / 12.0
    ref[slot, :, 0, :] = ref[slot, :, 0, :] + (wide * low[0] - near * low[1])
    ref[slot, :, 1, :] = ref[slot, :, 1, :] + wide * low[1]
    ref[slot, :, rows - 2, :] = ref[slot, :, rows - 2, :] - wide * high[0]
    ref[slot, :, rows - 1, :] = ref[slot, :, rows - 1, :] + (
        near * high[0] - wide * high[1]
    )


def halo_rows(low, high, field):
    return [[ref[field, r] for r in range(2)] for ref in (low, high)]


def sweep_body(given, pivot, lower, upper, low, high, base, lowered, mine, edges, active, kept):
    del given, base, kept
    levels, rows = active.shape[1:3]
    for slot, field in ((0, 2), (1, 4)):
        add_halo(active, slot, *halo_rows(low, high, field))
    states = forward(active, pivot, lower)
    for l in range(levels):
        for k in range(2):
            lowered[k, l] = states[l][k]

    def emit(state):
        for k in range(2):
            mine[k] = state[k]
            edges[pl.ds(8 * k, 4)] = state[k][:4]
            edges[pl.ds(8 * k + 4, 4)] = state[k][rows - 4 :]

    @pl.when(lax.axis_index("lev") == 0)
    def _():
        emit(states[-1])

    @pl.when(lax.axis_index("lev") == 1)
    def _():
        emit(backward_first(states, upper))


def odd_tiles_body(adj, courant, passive):
    @pl.when(lax.rem(lax.axis_index("tile"), 2) == 1)
    def _():
        passive_base(adj, courant, passive)


def passive_body(adj, courant, base, low, high, out, passive, sems):
    del base

    @pl.when(lax.rem(lax.axis_index("tile"), 2) == 0)
    def _():
        passive_base(adj, courant, passive)

    copies = []
    for slot, field in enumerate((0, 1, 3)):
        add_halo(passive, slot, *halo_rows(low, high, field))
        copies.append(
            pltpu.make_async_copy(passive.at[slot], out.at[field], sems.at[slot])
        )
        copies[-1].start()
    for copy in copies:
        copy.wait()


def solve_body(
    lowered, lower, upper, mine, bulk, edges, partial, out, solved, other, sems
):
    del partial
    levels, rows = lowered.shape[1:3]
    half = levels // 2
    for k in range(2):
        other[k, pl.ds(0, 4)] = edges[pl.ds(8 * k, 4)]
        other[k, pl.ds(4, rows - 8)] = bulk[pl.ds(4 * rows + k * (rows - 8), rows - 8)]
        other[k, pl.ds(rows - 4, 4)] = edges[pl.ds(8 * k + 4, 4)]

    def copies(part):
        span = pl.ds(part * half, half)
        return [
            pltpu.make_async_copy(
                solved.at[k, span], out.at[field, span], sems.at[part, k]
            )
            for k, field in ((0, 2), (1, 4))
        ]

    def descend(state, full):
        for l in range(levels - 1, -1, -1):
            if state is None:
                state = full(l)
            else:
                state = add(mul(at(upper, l), state), full(l))
            for k in range(2):
                solved[k, l] = state[k]
            if l == half or l == 0:
                for copy in copies(l // half):
                    copy.start()

    @pl.when(lax.axis_index("lev") == 0)
    def _():
        gain = tuple(bulk[pl.ds(k * rows, rows)] for k in range(4))
        descend(
            add(mul(gain, (mine[0], mine[1])), (other[0], other[1])),
            lambda l: at(lowered, l),
        )

    @pl.when(lax.axis_index("lev") == 1)
    def _():
        entering = (other[0], other[1])
        full = []
        for l in range(levels):
            entering = mul(at(lower, l), entering)
            full.append(add(entering, at(lowered, l)))
        descend(None, lambda l: full[l])

    for part in range(2):
        for copy in copies(part):
            copy.wait()


def local_pair(adjoint, courant, metric, pivot_inverse, lower_gain, upper_gain):
    fields, levels, rows, cols = adjoint.shape
    tiles = lax.axis_size("tile")
    swap = [(0, 1), (1, 0)]
    forth = [(i, (i + 1) % tiles) for i in range(tiles)]
    back = [(i, (i - 1) % tiles) for i in range(tiles)]
    halo = held((fields, 2, levels, cols))
    inputs = [held(adjoint.shape), held(courant.shape), held(metric.shape)]
    sems = pltpu.SemaphoreType.DMA((3,))
    sources = (from_hbm(adjoint), from_hbm(courant), from_hbm(metric))
    gains = (from_hbm(lower_gain), from_hbm(upper_gain), from_hbm(pivot_inverse))
    ahead, *fetched = pl.pallas_call(
        edges_body,
        name="edges",
        in_specs=[in_hbm()] * 3,
        out_specs=[whole()] * 4,
        out_shape=[halo] + inputs,
        scratch_shapes=[sems],
        compiler_params=params(),
    )(*sources)
    work = [
        held((6 * rows - 16, cols)),
        held((2, levels, rows, cols)),
        held(pivot_inverse.shape),
        held(lower_gain.shape),
        held(upper_gain.shape),
    ]
    low = lax.ppermute(ahead, "tile", forth)
    behind, adj, cour, met, *begun = pl.pallas_call(
        first_tile_body,
        name="first_tile",
        in_specs=[in_hbm()] * 6 + [whole()] * 3,
        out_specs=[whole()] * (4 + len(work)),
        out_shape=[halo] + inputs + work,
        scratch_shapes=[sems, sems],
        input_output_aliases={6 + i: 1 + i for i in range(3)},
        compiler_params=params(),
    )(*sources, *gains, *fetched)
    high = lax.ppermute(behind, "tile", back)
    summary, active, pivot, lower, upper = pl.pallas_call(
        other_tiles_body,
        name="other_tiles",
        in_specs=[whole()] * 3 + [in_hbm()] * 3 + [whole()] * len(work),
        out_specs=[whole()] * len(work),
        out_shape=work,
        scratch_shapes=[sems],
        input_output_aliases={6 + i: i for i in range(len(work))},
        compiler_params=params(),
    )(adj, cour, met, *gains, *begun)
    bulk = lax.ppermute(summary, "lev", swap)
    base = pl.pallas_call(
        odd_tiles_body,
        name="odd_tiles",
        in_specs=[whole()] * 2,
        out_specs=whole(),
        out_shape=held((3, levels, rows, cols)),
        compiler_params=params(),
    )(adj, cour)
    lowered, mine, edges, _, base = pl.pallas_call(
        sweep_body,
        name="sweep",
        in_specs=[whole()] * 7,
        out_specs=[whole()] * 5,
        out_shape=[
            held((2, levels, rows, cols)),
            held((2, rows, cols)),
            held((16, cols)),
            work[1],
            held((3, levels, rows, cols)),
        ],
        input_output_aliases={0: 3, 6: 4},
        compiler_params=params(),
    )(active, pivot, lower, upper, low, high, base)
    got_edges = lax.ppermute(edges, "lev", swap)
    partial, _ = pl.pallas_call(
        passive_body,
        name="passive",
        in_specs=[whole()] * 5,
        out_specs=[pl.BlockSpec(memory_space=pl.ANY), whole()],
        out_shape=[
            jax.ShapeDtypeStruct(adjoint.shape, F32),
            held((3, levels, rows, cols)),
        ],
        scratch_shapes=[sems],
        input_output_aliases={2: 1},
        compiler_params=params(),
    )(adj, cour, base, low, high)
    return pl.pallas_call(
        solve_body,
        name="solve",
        in_specs=[whole()] * 6 + [pl.BlockSpec(memory_space=pl.ANY)],
        out_specs=pl.BlockSpec(memory_space=pl.ANY),
        out_shape=jax.ShapeDtypeStruct(adjoint.shape, F32),
        scratch_shapes=[
            pltpu.VMEM((2, levels, rows, cols), F32),
            pltpu.VMEM((2, rows, cols), F32),
            pltpu.SemaphoreType.DMA((2, 2)),
        ],
        input_output_aliases={6: 0},
        compiler_params=params(),
    )(lowered, lower, upper, mine, bulk, got_edges, partial)


LEVEL_UNROLL = 16


def with_halo(block, sides, width):
    for axis, dim in sides:
        count = lax.axis_size(axis)
        forward = [(i, i + 1) for i in range(count - 1)]
        forward.append((count - 1, 0))
        backward = [(target, source) for source, target in forward]
        low = lax.ppermute(
            lax.slice_in_dim(block, block.shape[dim] - width, None, axis=dim), axis, forward
        )
        high = lax.ppermute(lax.slice_in_dim(block, 0, width, axis=dim), axis, backward)
        block = jnp.concatenate([low, block, high], axis=dim)
    return block


def centered_roll(values, axis_id):
    ahead_one = jnp.roll(values, -1, axis_id)
    behind_one = jnp.roll(values, 1, axis_id)
    ahead_two = jnp.roll(values, -2, axis_id)
    behind_two = jnp.roll(values, 2, axis_id)
    return (8.0 * (ahead_one - behind_one) - (ahead_two - behind_two)) / 12.0


def centered_padded(padded):
    ahead_one = padded[:, :, 3:-1, :]
    behind_one = padded[:, :, 1:-3, :]
    ahead_two = padded[:, :, 4:, :]
    behind_two = padded[:, :, :-4, :]
    return (8.0 * (ahead_one - behind_one) - (ahead_two - behind_two)) / 12.0


def mat_vec(system_matrix, vector):
    return jnp.stack(
        [
            system_matrix[0] * vector[0] + system_matrix[1] * vector[1],
            system_matrix[2] * vector[0] + system_matrix[3] * vector[1],
        ]
    )


def chain_run(coupling, forcing, initial, backward):

    def advance(state, inputs):
        fresh = mat_vec(inputs[0], state) + inputs[1]
        return (fresh, fresh)

    final_state, states = lax.scan(
        advance,
        initial,
        (jnp.moveaxis(coupling, 1, 0), jnp.moveaxis(forcing, 1, 0)),
        reverse=backward,
        unroll=min(LEVEL_UNROLL, coupling.shape[1]),
    )
    return jnp.moveaxis(states, 0, 1)


def column_solve(pieces):
    forcing, lower_part, upper_part = pieces
    initial = jnp.zeros((2,) + forcing.shape[2:], jnp.float32)
    lowered = chain_run(lower_part, forcing, initial, False)
    solved = chain_run(upper_part, lowered, initial, True)
    return lax.all_to_all(solved, "lev", split_axis=1, concat_axis=2, tiled=True)


def local_any(adjoint, courant, metric, pivot_inverse, lower_gain, upper_gain):
    weighted = jnp.concatenate([courant[0] * adjoint, (metric[0] * adjoint[0])[None]], 0)
    padded = with_halo(weighted, (("tile", 2),), 2)
    across = centered_padded(padded)
    advected = adjoint + across[:5] + centered_roll(courant[1] * adjoint, 3)
    pressure_field = advected[4] + across[5] + centered_roll(metric[1] * adjoint[1], 2)
    forcing = mat_vec(pivot_inverse, jnp.stack([advected[2], pressure_field]))
    solved = column_solve(
        (
            lax.all_to_all(forcing, "lev", split_axis=2, concat_axis=1, tiled=True),
            lax.all_to_all(lower_gain, "lev", split_axis=2, concat_axis=1, tiled=True),
            lax.all_to_all(upper_gain, "lev", split_axis=2, concat_axis=1, tiled=True),
        )
    )
    return jnp.stack([advected[0], advected[1], solved[0], advected[3], solved[1]])


def solution(mesh):
    placed = (P(None, "lev", "tile", None),) * 6
    pair = mesh.shape["lev"] == 2 and mesh.shape["tile"] % 2 == 0
    return jax.shard_map(
        local_pair if pair else local_any,
        mesh=mesh,
        in_specs=placed,
        out_specs=P(None, "lev", "tile", None),
        check_vma=False,
    )
```

```python
import jax
import jax.numpy as jnp
from jax import lax
from jax.experimental import pallas as pl
from jax.experimental.pallas import tpu as pltpu
from jax.sharding import PartitionSpec as P

F32 = jnp.float32
VMEM_LIMIT = 24 * 1024 * 1024


def held(shape):
    return pltpu.VMEM(shape, F32)


def whole():
    return pl.BlockSpec(memory_space=pltpu.VMEM)


def in_hbm():
    return pl.BlockSpec(memory_space=pltpu.HBM)


def from_hbm(x):
    return pltpu.with_memory_space_constraint(x, pltpu.HBM)


def params():
    return pltpu.CompilerParams(vmem_limit_bytes=VMEM_LIMIT)


def mul(m, v):
    return (m[0] * v[0] + m[1] * v[1], m[2] * v[0] + m[3] * v[1])


def matmul(m, n):
    return (
        m[0] * n[0] + m[1] * n[2],
        m[0] * n[1] + m[1] * n[3],
        m[2] * n[0] + m[3] * n[2],
        m[2] * n[1] + m[3] * n[3],
    )


def add(a, b):
    return tuple(x + y for x, y in zip(a, b, strict=True))


def at(ref, level):
    return tuple(ref[k, level] for k in range(ref.shape[0]))


def emit_edges(adj, courant, metric, out, first):
    for r in range(2):
        row = first + r
        wind = courant[0, :, row, :]
        for k in range(4):
            out[k, r] = wind * adj[k, :, row, :]
        out[4, r] = wind * adj[4, :, row, :] + metric[0, :, row, :] * adj[0, :, row, :]


def fetch_all(sources, targets, sems, levels_each=2):
    waits = []
    for i, (source, target) in enumerate(zip(sources, targets, strict=True)):
        for k in range(source.shape[0]):
            for l in range(0, source.shape[1], levels_each):
                span = pl.ds(l, min(levels_each, source.shape[1] - l))
                pltpu.make_async_copy(
                    source.at[k, span], target.at[k, span], sems.at[i]
                ).start()
        waits.append(pltpu.make_async_copy(source, target, sems.at[i]))
    return waits


def tail_rows(ref):
    return ref.at[:, :, pl.ds(ref.shape[2] - 8, 8)]


def head_rows(ref):
    return ref.at[:, :, pl.ds(0, ref.shape[2] - 8)]


def is_first_tile():
    return lax.axis_index("tile") == 0


def is_last_tile():
    return lax.axis_index("tile") == lax.axis_size("tile") - 1


def edges_body(
    adj_in, courant_in, metric_in, ahead, adj, courant, metric, sems
):
    given, targets = (adj_in, courant_in, metric_in), (adj, courant, metric)
    across_in = (adj_in, courant_in.at[pl.ds(0, 1)], metric_in.at[pl.ds(0, 1)])
    across_out = (adj, courant.at[pl.ds(0, 1)], metric.at[pl.ds(0, 1)])
    first, last = is_first_tile(), is_last_tile()

    @pl.when(first)
    def _():
        for copy in fetch_all(
            map(tail_rows, across_in), map(tail_rows, across_out), sems
        ):
            copy.wait()

    @pl.when(last)
    def _():
        for copy in fetch_all(across_in, across_out, sems):
            copy.wait()

    @pl.when(jnp.logical_not(jnp.logical_or(first, last)))
    def _():
        for copy in fetch_all(given, targets, sems):
            copy.wait()

    emit_edges(adj, courant, metric, ahead, adj.shape[2] - 2)


def across(q):
    rows = q.shape[0]
    spot = lax.broadcasted_iota(jnp.int32, q.shape, 0)
    out = None
    for step, weight in ((1, 8.0 / 12.0), (2, -1.0 / 12.0)):
        ahead = jnp.where(spot < rows - step, pltpu.roll(q, rows - step, 0), 0.0)
        behind = jnp.where(spot >= step, pltpu.roll(q, step, 0), 0.0)
        term = weight * (ahead - behind)
        out = term if out is None else out + term
    return out


def along(q):
    cols = q.shape[1]
    near = pltpu.roll(q, cols - 1, 1) - pltpu.roll(q, 1, 1)
    wide = pltpu.roll(q, cols - 2, 1) - pltpu.roll(q, 2, 1)
    return (8.0 / 12.0) * near - (1.0 / 12.0) * wide


def passive_base(adj, courant, passive):
    def one(l, _):
        c0, c1 = courant[0, l], courant[1, l]
        for slot, field in ((0, 0), (1, 1), (2, 3)):
            x = adj[field, l]
            passive[slot, l] = x + across(c0 * x) + along(c1 * x)
        return 0

    lax.fori_loop(0, adj.shape[1], one, 0)


def along_planes(courant_in, metric_in, courant, metric):
    second = pl.ds(1, 1)
    return (
        (courant_in.at[second], metric_in.at[second]),
        (courant.at[second], metric.at[second]),
    )


def first_tile_body(adj_in, courant_in, metric_in, lower_in, upper_in, pivot_in, *refs):
    behind, adj, courant, metric, *work = refs[3:-3]
    sems, head_sems, along_sems = refs[-3:]

    @pl.when(is_first_tile())
    def _():
        first = pl.ds(0, 1)
        heads = fetch_all(
            map(head_rows, (adj_in, courant_in.at[first], metric_in.at[first])),
            map(head_rows, (adj, courant.at[first], metric.at[first])),
            head_sems,
        )
        heads += fetch_all(
            *along_planes(courant_in, metric_in, courant, metric), along_sems
        )
        gains = fetch_all((lower_in, upper_in, pivot_in), work[-2:] + work[-3:-2], sems)
        for copy in heads:
            copy.wait()
        active_base(adj, courant, metric, work[1])
        summarise(work, gains)

    emit_edges(adj, courant, metric, behind, 0)


def other_tiles_body(
    courant_in, metric_in, lower_in, upper_in, pivot_in, adj, courant, metric, *refs
):
    courant, metric, *work, sems, along_sems = refs[-9:]

    @pl.when(jnp.logical_not(is_first_tile()))
    def _():
        last = is_last_tile()
        planes = along_planes(courant_in, metric_in, courant, metric)

        @pl.when(last)
        def _():
            fetch_all(*planes, along_sems)

        gains = fetch_all((lower_in, upper_in, pivot_in), work[-2:] + work[-3:-2], sems)

        @pl.when(last)
        def _():
            for i, (source, target) in enumerate(zip(*planes, strict=True)):
                pltpu.make_async_copy(source, target, along_sems.at[i]).wait()

        active_base(adj, courant, metric, work[1])
        summarise(work, gains)


def active_base(adj, courant, metric, active):
    def one(l, _):
        c0, c1 = courant[0, l], courant[1, l]
        x = adj[2, l]
        active[0, l] = x + across(c0 * x) + along(c1 * x)
        x = adj[4, l]
        active[1, l] = (
            x
            + across(c0 * x + metric[0, l] * adj[0, l])
            + along(c1 * x + metric[1, l] * adj[1, l])
        )
        return 0

    lax.fori_loop(0, adj.shape[1], one, 0)


def summarise(work, gains):
    bulk, active, pivot, lower, upper = work
    levels = active.shape[1]
    for copy in gains:
        copy.wait()
    states = forward(active, pivot, lower)

    rows = active.shape[2]

    def emit(state):
        for k in range(2):
            start = 4 * rows + k * (rows - 8)
            bulk[pl.ds(start, rows - 8)] = state[k][4 : rows - 4]

    @pl.when(lax.axis_index("lev") == 0)
    def _():
        emit(states[-1])

    @pl.when(lax.axis_index("lev") == 1)
    def _():
        emit(backward_first(states, upper))
        chain = [at(lower, 0)]
        for l in range(1, levels):
            chain.append(matmul(at(lower, l), chain[-1]))
        total = chain[-1]
        for l in range(levels - 2, -1, -1):
            total = add(matmul(at(upper, l), total), chain[l])
        for k in range(4):
            bulk[pl.ds(k * rows, rows)] = total[k]


def forward(active, pivot, lower):
    states = []
    for l in range(active.shape[1]):
        fresh = mul(at(pivot, l), at(active, l))
        if states:
            fresh = add(mul(at(lower, l), states[-1]), fresh)
        states.append(fresh)
    return states


def backward_first(states, upper):
    state = states[-1]
    for l in range(len(states) - 2, -1, -1):
        state = add(mul(at(upper, l), state), states[l])
    return state


def add_halo(ref, slot, low, high):
    rows = ref.shape[2]
    near, wide = 8.0 / 12.0, 1.0 / 12.0
    ref[slot, :, 0, :] = ref[slot, :, 0, :] + (wide * low[0] - near * low[1])
    ref[slot, :, 1, :] = ref[slot, :, 1, :] + wide * low[1]
    ref[slot, :, rows - 2, :] = ref[slot, :, rows - 2, :] - wide * high[0]
    ref[slot, :, rows - 1, :] = ref[slot, :, rows - 1, :] + (
        near * high[0] - wide * high[1]
    )


def halo_rows(low, high, field):
    return [[ref[field, r] for r in range(2)] for ref in (low, high)]


def sweep_body(given, pivot, lower, upper, low, high, base, lowered, mine, edges, active, kept):
    del given, base, kept
    levels, rows = active.shape[1:3]
    for slot, field in ((0, 2), (1, 4)):
        add_halo(active, slot, *halo_rows(low, high, field))
    states = forward(active, pivot, lower)
    for l in range(levels):
        for k in range(2):
            lowered[k, l] = states[l][k]

    def emit(state):
        for k in range(2):
            mine[k] = state[k]
            edges[pl.ds(8 * k, 4)] = state[k][:4]
            edges[pl.ds(8 * k + 4, 4)] = state[k][rows - 4 :]

    @pl.when(lax.axis_index("lev") == 0)
    def _():
        emit(states[-1])

    @pl.when(lax.axis_index("lev") == 1)
    def _():
        emit(backward_first(states, upper))


def odd_tiles_body(adj, courant, passive):
    @pl.when(lax.rem(lax.axis_index("tile"), 2) == 1)
    def _():
        passive_base(adj, courant, passive)


def passive_body(adj, courant, base, low, high, out, passive, sems):
    del base

    @pl.when(lax.rem(lax.axis_index("tile"), 2) == 0)
    def _():
        passive_base(adj, courant, passive)

    copies = []
    for slot, field in enumerate((0, 1, 3)):
        add_halo(passive, slot, *halo_rows(low, high, field))
        copies.append(
            pltpu.make_async_copy(passive.at[slot], out.at[field], sems.at[slot])
        )
        copies[-1].start()
    for copy in copies:
        copy.wait()


def solve_body(
    lowered, lower, upper, mine, bulk, edges, partial, out, solved, other, sems
):
    del partial
    levels, rows = lowered.shape[1:3]
    for k in range(2):
        other[k, pl.ds(0, 4)] = edges[pl.ds(8 * k, 4)]
        other[k, pl.ds(4, rows - 8)] = bulk[pl.ds(4 * rows + k * (rows - 8), rows - 8)]
        other[k, pl.ds(rows - 4, 4)] = edges[pl.ds(8 * k + 4, 4)]

    def descend(state, full):
        for l in range(levels - 1, -1, -1):
            if state is None:
                state = full(l)
            else:
                state = add(mul(at(upper, l), state), full(l))
            for k, field in ((0, 2), (1, 4)):
                solved[k, l] = state[k]
                pltpu.make_async_copy(
                    solved.at[k, l], out.at[field, l], sems.at[k]
                ).start()

    @pl.when(lax.axis_index("lev") == 0)
    def _():
        gain = tuple(bulk[pl.ds(k * rows, rows)] for k in range(4))
        descend(
            add(mul(gain, (mine[0], mine[1])), (other[0], other[1])),
            lambda l: at(lowered, l),
        )

    @pl.when(lax.axis_index("lev") == 1)
    def _():
        entering = (other[0], other[1])
        full = []
        for l in range(levels):
            entering = mul(at(lower, l), entering)
            full.append(add(entering, at(lowered, l)))
        descend(None, lambda l: full[l])

    for k, field in ((0, 2), (1, 4)):
        pltpu.make_async_copy(solved.at[k], out.at[field], sems.at[k]).wait()


def local_pair(adjoint, courant, metric, pivot_inverse, lower_gain, upper_gain):
    fields, levels, rows, cols = adjoint.shape
    tiles = lax.axis_size("tile")
    swap = [(0, 1), (1, 0)]
    forth = [(i, (i + 1) % tiles) for i in range(tiles)]
    back = [(i, (i - 1) % tiles) for i in range(tiles)]
    halo = held((fields, 2, levels, cols))
    inputs = [held(adjoint.shape), held(courant.shape), held(metric.shape)]
    sems = pltpu.SemaphoreType.DMA((3,))
    sources = (from_hbm(adjoint), from_hbm(courant), from_hbm(metric))
    gains = (from_hbm(lower_gain), from_hbm(upper_gain), from_hbm(pivot_inverse))
    ahead, *fetched = pl.pallas_call(
        edges_body,
        name="edges",
        in_specs=[in_hbm()] * 3,
        out_specs=[whole()] * 4,
        out_shape=[halo] + inputs,
        scratch_shapes=[sems],
        compiler_params=params(),
    )(*sources)
    work = [
        held((6 * rows - 16, cols)),
        held((2, levels, rows, cols)),
        held(pivot_inverse.shape),
        held(lower_gain.shape),
        held(upper_gain.shape),
    ]
    low = lax.ppermute(ahead, "tile", forth)
    behind, adj, cour, met, *begun = pl.pallas_call(
        first_tile_body,
        name="first_tile",
        in_specs=[in_hbm()] * 6 + [whole()] * 3,
        out_specs=[whole()] * (4 + len(work)),
        out_shape=[halo] + inputs + work,
        scratch_shapes=[sems, sems, sems],
        input_output_aliases={6 + i: 1 + i for i in range(3)},
        compiler_params=params(),
    )(*sources, *gains, *fetched)
    high = lax.ppermute(behind, "tile", back)
    cour, met, summary, active, pivot, lower, upper = pl.pallas_call(
        other_tiles_body,
        name="other_tiles",
        in_specs=[in_hbm()] * 5 + [whole()] * (3 + len(work)),
        out_specs=[whole()] * (2 + len(work)),
        out_shape=inputs[1:] + work,
        scratch_shapes=[sems, sems],
        input_output_aliases={6 + i: i for i in range(2 + len(work))},
        compiler_params=params(),
    )(*sources[1:], *gains, adj, cour, met, *begun)
    bulk = lax.ppermute(summary, "lev", swap)
    base = pl.pallas_call(
        odd_tiles_body,
        name="odd_tiles",
        in_specs=[whole()] * 2,
        out_specs=whole(),
        out_shape=held((3, levels, rows, cols)),
        compiler_params=params(),
    )(adj, cour)
    lowered, mine, edges, _, base = pl.pallas_call(
        sweep_body,
        name="sweep",
        in_specs=[whole()] * 7,
        out_specs=[whole()] * 5,
        out_shape=[
            held((2, levels, rows, cols)),
            held((2, rows, cols)),
            held((16, cols)),
            work[1],
            held((3, levels, rows, cols)),
        ],
        input_output_aliases={0: 3, 6: 4},
        compiler_params=params(),
    )(active, pivot, lower, upper, low, high, base)
    got_edges = lax.ppermute(edges, "lev", swap)
    partial, _ = pl.pallas_call(
        passive_body,
        name="passive",
        in_specs=[whole()] * 5,
        out_specs=[pl.BlockSpec(memory_space=pl.ANY), whole()],
        out_shape=[
            jax.ShapeDtypeStruct(adjoint.shape, F32),
            held((3, levels, rows, cols)),
        ],
        scratch_shapes=[sems],
        input_output_aliases={2: 1},
        compiler_params=params(),
    )(adj, cour, base, low, high)
    return pl.pallas_call(
        solve_body,
        name="solve",
        in_specs=[whole()] * 6 + [pl.BlockSpec(memory_space=pl.ANY)],
        out_specs=pl.BlockSpec(memory_space=pl.ANY),
        out_shape=jax.ShapeDtypeStruct(adjoint.shape, F32),
        scratch_shapes=[
            pltpu.VMEM((2, levels, rows, cols), F32),
            pltpu.VMEM((2, rows, cols), F32),
            pltpu.SemaphoreType.DMA((2,)),
        ],
        input_output_aliases={6: 0},
        compiler_params=params(),
    )(lowered, lower, upper, mine, bulk, got_edges, partial)


LEVEL_UNROLL = 16


def with_halo(block, sides, width):
    for axis, dim in sides:
        count = lax.axis_size(axis)
        forward = [(i, i + 1) for i in range(count - 1)]
        forward.append((count - 1, 0))
        backward = [(target, source) for source, target in forward]
        low = lax.ppermute(
            lax.slice_in_dim(block, block.shape[dim] - width, None, axis=dim), axis, forward
        )
        high = lax.ppermute(lax.slice_in_dim(block, 0, width, axis=dim), axis, backward)
        block = jnp.concatenate([low, block, high], axis=dim)
    return block


def centered_roll(values, axis_id):
    ahead_one = jnp.roll(values, -1, axis_id)
    behind_one = jnp.roll(values, 1, axis_id)
    ahead_two = jnp.roll(values, -2, axis_id)
    behind_two = jnp.roll(values, 2, axis_id)
    return (8.0 * (ahead_one - behind_one) - (ahead_two - behind_two)) / 12.0


def centered_padded(padded):
    ahead_one = padded[:, :, 3:-1, :]
    behind_one = padded[:, :, 1:-3, :]
    ahead_two = padded[:, :, 4:, :]
    behind_two = padded[:, :, :-4, :]
    return (8.0 * (ahead_one - behind_one) - (ahead_two - behind_two)) / 12.0


def mat_vec(system_matrix, vector):
    return jnp.stack(
        [
            system_matrix[0] * vector[0] + system_matrix[1] * vector[1],
            system_matrix[2] * vector[0] + system_matrix[3] * vector[1],
        ]
    )


def chain_run(coupling, forcing, initial, backward):

    def advance(state, inputs):
        fresh = mat_vec(inputs[0], state) + inputs[1]
        return (fresh, fresh)

    final_state, states = lax.scan(
        advance,
        initial,
        (jnp.moveaxis(coupling, 1, 0), jnp.moveaxis(forcing, 1, 0)),
        reverse=backward,
        unroll=min(LEVEL_UNROLL, coupling.shape[1]),
    )
    return jnp.moveaxis(states, 0, 1)


def column_solve(pieces):
    forcing, lower_part, upper_part = pieces
    initial = jnp.zeros((2,) + forcing.shape[2:], jnp.float32)
    lowered = chain_run(lower_part, forcing, initial, False)
    solved = chain_run(upper_part, lowered, initial, True)
    return lax.all_to_all(solved, "lev", split_axis=1, concat_axis=2, tiled=True)


def local_any(adjoint, courant, metric, pivot_inverse, lower_gain, upper_gain):
    weighted = jnp.concatenate([courant[0] * adjoint, (metric[0] * adjoint[0])[None]], 0)
    padded = with_halo(weighted, (("tile", 2),), 2)
    across = centered_padded(padded)
    advected = adjoint + across[:5] + centered_roll(courant[1] * adjoint, 3)
    pressure_field = advected[4] + across[5] + centered_roll(metric[1] * adjoint[1], 2)
    forcing = mat_vec(pivot_inverse, jnp.stack([advected[2], pressure_field]))
    solved = column_solve(
        (
            lax.all_to_all(forcing, "lev", split_axis=2, concat_axis=1, tiled=True),
            lax.all_to_all(lower_gain, "lev", split_axis=2, concat_axis=1, tiled=True),
            lax.all_to_all(upper_gain, "lev", split_axis=2, concat_axis=1, tiled=True),
        )
    )
    return jnp.stack([advected[0], advected[1], solved[0], advected[3], solved[1]])


def solution(mesh):
    placed = (P(None, "lev", "tile", None),) * 6
    pair = mesh.shape["lev"] == 2 and mesh.shape["tile"] % 2 == 0
    return jax.shard_map(
        local_pair if pair else local_any,
        mesh=mesh,
        in_specs=placed,
        out_specs=P(None, "lev", "tile", None),
        check_vma=False,
    )
```

```python
import jax
import jax.numpy as jnp
from jax import lax
from jax.experimental import pallas as pl
from jax.experimental.pallas import tpu as pltpu
from jax.sharding import PartitionSpec as P

F32 = jnp.float32
VMEM_LIMIT = 24 * 1024 * 1024


def held(shape):
    return pltpu.VMEM(shape, F32)


def whole():
    return pl.BlockSpec(memory_space=pltpu.VMEM)


def in_hbm():
    return pl.BlockSpec(memory_space=pltpu.HBM)


def from_hbm(x):
    return pltpu.with_memory_space_constraint(x, pltpu.HBM)


def params():
    return pltpu.CompilerParams(vmem_limit_bytes=VMEM_LIMIT)


def mul(m, v):
    return (m[0] * v[0] + m[1] * v[1], m[2] * v[0] + m[3] * v[1])


def matmul(m, n):
    return (
        m[0] * n[0] + m[1] * n[2],
        m[0] * n[1] + m[1] * n[3],
        m[2] * n[0] + m[3] * n[2],
        m[2] * n[1] + m[3] * n[3],
    )


def add(a, b):
    return tuple(x + y for x, y in zip(a, b, strict=True))


def at(ref, level):
    return tuple(ref[k, level] for k in range(ref.shape[0]))


def emit_edges(adj, courant, metric, out, first):
    for r in range(2):
        row = first + r
        wind = courant[0, :, row, :]
        for k in range(4):
            out[k, r] = wind * adj[k, :, row, :]
        out[4, r] = wind * adj[4, :, row, :] + metric[0, :, row, :] * adj[0, :, row, :]


def fetch_all(sources, targets, sems, levels_each=2):
    waits = []
    for i, (source, target) in enumerate(zip(sources, targets, strict=True)):
        parts = source.shape[1] // levels_each

        def start(n, _, i=i, source=source, target=target, parts=parts):
            k, span = n // parts, pl.ds(lax.rem(n, parts) * levels_each, levels_each)
            pltpu.make_async_copy(
                source.at[k, span], target.at[k, span], sems.at[i]
            ).start()
            return 0

        lax.fori_loop(0, source.shape[0] * parts, start, 0)
        waits.append(pltpu.make_async_copy(source, target, sems.at[i]))
    return waits


def tail_rows(ref):
    return ref.at[:, :, pl.ds(ref.shape[2] - 8, 8)]


def head_rows(ref):
    return ref.at[:, :, pl.ds(0, ref.shape[2] - 8)]


def is_first_tile():
    return lax.axis_index("tile") == 0


def is_last_tile():
    return lax.axis_index("tile") == lax.axis_size("tile") - 1


def edges_body(
    adj_in, courant_in, metric_in, ahead, adj, courant, metric, sems
):
    given, targets = (adj_in, courant_in, metric_in), (adj, courant, metric)
    across_in = (adj_in, courant_in.at[pl.ds(0, 1)], metric_in.at[pl.ds(0, 1)])
    across_out = (adj, courant.at[pl.ds(0, 1)], metric.at[pl.ds(0, 1)])
    first, last = is_first_tile(), is_last_tile()

    @pl.when(first)
    def _():
        for copy in fetch_all(
            map(tail_rows, across_in), map(tail_rows, across_out), sems
        ):
            copy.wait()

    @pl.when(last)
    def _():
        for copy in fetch_all(across_in, across_out, sems):
            copy.wait()

    @pl.when(jnp.logical_not(jnp.logical_or(first, last)))
    def _():
        for copy in fetch_all(given, targets, sems):
            copy.wait()

    emit_edges(adj, courant, metric, ahead, adj.shape[2] - 2)


def across(q):
    rows = q.shape[0]
    spot = lax.broadcasted_iota(jnp.int32, q.shape, 0)
    out = None
    for step, weight in ((1, 8.0 / 12.0), (2, -1.0 / 12.0)):
        ahead = jnp.where(spot < rows - step, pltpu.roll(q, rows - step, 0), 0.0)
        behind = jnp.where(spot >= step, pltpu.roll(q, step, 0), 0.0)
        term = weight * (ahead - behind)
        out = term if out is None else out + term
    return out


def along(q):
    cols = q.shape[1]
    near = pltpu.roll(q, cols - 1, 1) - pltpu.roll(q, 1, 1)
    wide = pltpu.roll(q, cols - 2, 1) - pltpu.roll(q, 2, 1)
    return (8.0 / 12.0) * near - (1.0 / 12.0) * wide


def passive_base(adj, courant, passive):
    def one(l, _):
        c0, c1 = courant[0, l], courant[1, l]
        for slot, field in ((0, 0), (1, 1), (2, 3)):
            x = adj[field, l]
            passive[slot, l] = x + across(c0 * x) + along(c1 * x)
        return 0

    lax.fori_loop(0, adj.shape[1], one, 0)


def along_planes(courant_in, metric_in, courant, metric):
    second = pl.ds(1, 1)
    return (
        (courant_in.at[second], metric_in.at[second]),
        (courant.at[second], metric.at[second]),
    )


def first_tile_body(adj_in, courant_in, metric_in, lower_in, upper_in, pivot_in, *refs):
    behind, adj, courant, metric, *work = refs[3:-3]
    sems, head_sems, along_sems = refs[-3:]

    @pl.when(is_first_tile())
    def _():
        first = pl.ds(0, 1)
        heads = fetch_all(
            map(head_rows, (adj_in, courant_in.at[first], metric_in.at[first])),
            map(head_rows, (adj, courant.at[first], metric.at[first])),
            head_sems,
        )
        heads += fetch_all(
            *along_planes(courant_in, metric_in, courant, metric), along_sems
        )
        gains = fetch_all((lower_in, upper_in, pivot_in), work[-2:] + work[-3:-2], sems)
        for copy in heads:
            copy.wait()
        active_base(adj, courant, metric, work[1])
        summarise(work, gains)

    emit_edges(adj, courant, metric, behind, 0)


def other_tiles_body(
    courant_in, metric_in, lower_in, upper_in, pivot_in, adj, courant, metric, *refs
):
    courant, metric, *work, sems, along_sems = refs[-9:]

    @pl.when(jnp.logical_not(is_first_tile()))
    def _():
        last = is_last_tile()
        planes = along_planes(courant_in, metric_in, courant, metric)

        @pl.when(last)
        def _():
            fetch_all(*planes, along_sems)

        gains = fetch_all((lower_in, upper_in, pivot_in), work[-2:] + work[-3:-2], sems)

        @pl.when(last)
        def _():
            for i, (source, target) in enumerate(zip(*planes, strict=True)):
                pltpu.make_async_copy(source, target, along_sems.at[i]).wait()

        active_base(adj, courant, metric, work[1])
        summarise(work, gains)


def active_base(adj, courant, metric, active):
    def one(l, _):
        c0, c1 = courant[0, l], courant[1, l]
        x = adj[2, l]
        active[0, l] = x + across(c0 * x) + along(c1 * x)
        x = adj[4, l]
        active[1, l] = (
            x
            + across(c0 * x + metric[0, l] * adj[0, l])
            + along(c1 * x + metric[1, l] * adj[1, l])
        )
        return 0

    lax.fori_loop(0, adj.shape[1], one, 0)


def summarise(work, gains):
    bulk, active, pivot, lower, upper = work
    levels = active.shape[1]
    for copy in gains:
        copy.wait()
    states = forward(active, pivot, lower)

    rows = active.shape[2]

    def emit(state):
        for k in range(2):
            start = 4 * rows + k * (rows - 8)
            bulk[pl.ds(start, rows - 8)] = state[k][4 : rows - 4]

    @pl.when(lax.axis_index("lev") == 0)
    def _():
        emit(states[-1])

    @pl.when(lax.axis_index("lev") == 1)
    def _():
        emit(backward_first(states, upper))
        chain = [at(lower, 0)]
        for l in range(1, levels):
            chain.append(matmul(at(lower, l), chain[-1]))
        total = chain[-1]
        for l in range(levels - 2, -1, -1):
            total = add(matmul(at(upper, l), total), chain[l])
        for k in range(4):
            bulk[pl.ds(k * rows, rows)] = total[k]


def forward(active, pivot, lower):
    states = []
    for l in range(active.shape[1]):
        fresh = mul(at(pivot, l), at(active, l))
        if states:
            fresh = add(mul(at(lower, l), states[-1]), fresh)
        states.append(fresh)
    return states


def backward_first(states, upper):
    state = states[-1]
    for l in range(len(states) - 2, -1, -1):
        state = add(mul(at(upper, l), state), states[l])
    return state


def add_halo(ref, slot, low, high):
    rows = ref.shape[2]
    near, wide = 8.0 / 12.0, 1.0 / 12.0
    ref[slot, :, 0, :] = ref[slot, :, 0, :] + (wide * low[0] - near * low[1])
    ref[slot, :, 1, :] = ref[slot, :, 1, :] + wide * low[1]
    ref[slot, :, rows - 2, :] = ref[slot, :, rows - 2, :] - wide * high[0]
    ref[slot, :, rows - 1, :] = ref[slot, :, rows - 1, :] + (
        near * high[0] - wide * high[1]
    )


def halo_rows(low, high, field):
    return [[ref[field, r] for r in range(2)] for ref in (low, high)]


def sweep_body(given, pivot, lower, upper, low, high, base, lowered, mine, edges, active, kept):
    del given, base, kept
    levels, rows = active.shape[1:3]
    for slot, field in ((0, 2), (1, 4)):
        add_halo(active, slot, *halo_rows(low, high, field))
    states = forward(active, pivot, lower)
    for l in range(levels):
        for k in range(2):
            lowered[k, l] = states[l][k]

    def emit(state):
        for k in range(2):
            mine[k] = state[k]
            edges[pl.ds(8 * k, 4)] = state[k][:4]
            edges[pl.ds(8 * k + 4, 4)] = state[k][rows - 4 :]

    @pl.when(lax.axis_index("lev") == 0)
    def _():
        emit(states[-1])

    @pl.when(lax.axis_index("lev") == 1)
    def _():
        emit(backward_first(states, upper))


def odd_tiles_body(adj, courant, passive):
    @pl.when(lax.rem(lax.axis_index("tile"), 2) == 1)
    def _():
        passive_base(adj, courant, passive)


def passive_body(adj, courant, base, low, high, out, passive, sems):
    del base

    @pl.when(lax.rem(lax.axis_index("tile"), 2) == 0)
    def _():
        passive_base(adj, courant, passive)

    copies = []
    for slot, field in enumerate((0, 1, 3)):
        add_halo(passive, slot, *halo_rows(low, high, field))
        copies.append(
            pltpu.make_async_copy(passive.at[slot], out.at[field], sems.at[slot])
        )
        copies[-1].start()
    for copy in copies:
        copy.wait()


def solve_body(
    lowered, lower, upper, mine, bulk, edges, partial, out, solved, other, sems
):
    del partial
    levels, rows = lowered.shape[1:3]
    for k in range(2):
        other[k, pl.ds(0, 4)] = edges[pl.ds(8 * k, 4)]
        other[k, pl.ds(4, rows - 8)] = bulk[pl.ds(4 * rows + k * (rows - 8), rows - 8)]
        other[k, pl.ds(rows - 4, 4)] = edges[pl.ds(8 * k + 4, 4)]

    def descend(state, full):
        for l in range(levels - 1, -1, -1):
            if state is None:
                state = full(l)
            else:
                state = add(mul(at(upper, l), state), full(l))
            for k, field in ((0, 2), (1, 4)):
                solved[k, l] = state[k]
                pltpu.make_async_copy(
                    solved.at[k, l], out.at[field, l], sems.at[k]
                ).start()

    @pl.when(lax.axis_index("lev") == 0)
    def _():
        gain = tuple(bulk[pl.ds(k * rows, rows)] for k in range(4))
        descend(
            add(mul(gain, (mine[0], mine[1])), (other[0], other[1])),
            lambda l: at(lowered, l),
        )

    @pl.when(lax.axis_index("lev") == 1)
    def _():
        entering = (other[0], other[1])
        full = []
        for l in range(levels):
            entering = mul(at(lower, l), entering)
            full.append(add(entering, at(lowered, l)))
        descend(None, lambda l: full[l])

    for k, field in ((0, 2), (1, 4)):
        pltpu.make_async_copy(solved.at[k], out.at[field], sems.at[k]).wait()


def local_pair(adjoint, courant, metric, pivot_inverse, lower_gain, upper_gain):
    fields, levels, rows, cols = adjoint.shape
    tiles = lax.axis_size("tile")
    swap = [(0, 1), (1, 0)]
    forth = [(i, (i + 1) % tiles) for i in range(tiles)]
    back = [(i, (i - 1) % tiles) for i in range(tiles)]
    halo = held((fields, 2, levels, cols))
    inputs = [held(adjoint.shape), held(courant.shape), held(metric.shape)]
    sems = pltpu.SemaphoreType.DMA((3,))
    sources = (from_hbm(adjoint), from_hbm(courant), from_hbm(metric))
    gains = (from_hbm(lower_gain), from_hbm(upper_gain), from_hbm(pivot_inverse))
    ahead, *fetched = pl.pallas_call(
        edges_body,
        name="edges",
        in_specs=[in_hbm()] * 3,
        out_specs=[whole()] * 4,
        out_shape=[halo] + inputs,
        scratch_shapes=[sems],
        compiler_params=params(),
    )(*sources)
    work = [
        held((6 * rows - 16, cols)),
        held((2, levels, rows, cols)),
        held(pivot_inverse.shape),
        held(lower_gain.shape),
        held(upper_gain.shape),
    ]
    low = lax.ppermute(ahead, "tile", forth)
    behind, adj, cour, met, *begun = pl.pallas_call(
        first_tile_body,
        name="first_tile",
        in_specs=[in_hbm()] * 6 + [whole()] * 3,
        out_specs=[whole()] * (4 + len(work)),
        out_shape=[halo] + inputs + work,
        scratch_shapes=[sems, sems, sems],
        input_output_aliases={6 + i: 1 + i for i in range(3)},
        compiler_params=params(),
    )(*sources, *gains, *fetched)
    high = lax.ppermute(behind, "tile", back)
    cour, met, summary, active, pivot, lower, upper = pl.pallas_call(
        other_tiles_body,
        name="other_tiles",
        in_specs=[in_hbm()] * 5 + [whole()] * (3 + len(work)),
        out_specs=[whole()] * (2 + len(work)),
        out_shape=inputs[1:] + work,
        scratch_shapes=[sems, sems],
        input_output_aliases={6 + i: i for i in range(2 + len(work))},
        compiler_params=params(),
    )(*sources[1:], *gains, adj, cour, met, *begun)
    bulk = lax.ppermute(summary, "lev", swap)
    base = pl.pallas_call(
        odd_tiles_body,
        name="odd_tiles",
        in_specs=[whole()] * 2,
        out_specs=whole(),
        out_shape=held((3, levels, rows, cols)),
        compiler_params=params(),
    )(adj, cour)
    lowered, mine, edges, _, base = pl.pallas_call(
        sweep_body,
        name="sweep",
        in_specs=[whole()] * 7,
        out_specs=[whole()] * 5,
        out_shape=[
            held((2, levels, rows, cols)),
            held((2, rows, cols)),
            held((16, cols)),
            work[1],
            held((3, levels, rows, cols)),
        ],
        input_output_aliases={0: 3, 6: 4},
        compiler_params=params(),
    )(active, pivot, lower, upper, low, high, base)
    got_edges = lax.ppermute(edges, "lev", swap)
    partial, _ = pl.pallas_call(
        passive_body,
        name="passive",
        in_specs=[whole()] * 5,
        out_specs=[pl.BlockSpec(memory_space=pl.ANY), whole()],
        out_shape=[
            jax.ShapeDtypeStruct(adjoint.shape, F32),
            held((3, levels, rows, cols)),
        ],
        scratch_shapes=[sems],
        input_output_aliases={2: 1},
        compiler_params=params(),
    )(adj, cour, base, low, high)
    return pl.pallas_call(
        solve_body,
        name="solve",
        in_specs=[whole()] * 6 + [pl.BlockSpec(memory_space=pl.ANY)],
        out_specs=pl.BlockSpec(memory_space=pl.ANY),
        out_shape=jax.ShapeDtypeStruct(adjoint.shape, F32),
        scratch_shapes=[
            pltpu.VMEM((2, levels, rows, cols), F32),
            pltpu.VMEM((2, rows, cols), F32),
            pltpu.SemaphoreType.DMA((2,)),
        ],
        input_output_aliases={6: 0},
        compiler_params=params(),
    )(lowered, lower, upper, mine, bulk, got_edges, partial)


LEVEL_UNROLL = 16


def with_halo(block, sides, width):
    for axis, dim in sides:
        count = lax.axis_size(axis)
        forward = [(i, i + 1) for i in range(count - 1)]
        forward.append((count - 1, 0))
        backward = [(target, source) for source, target in forward]
        low = lax.ppermute(
            lax.slice_in_dim(block, block.shape[dim] - width, None, axis=dim), axis, forward
        )
        high = lax.ppermute(lax.slice_in_dim(block, 0, width, axis=dim), axis, backward)
        block = jnp.concatenate([low, block, high], axis=dim)
    return block


def centered_roll(values, axis_id):
    ahead_one = jnp.roll(values, -1, axis_id)
    behind_one = jnp.roll(values, 1, axis_id)
    ahead_two = jnp.roll(values, -2, axis_id)
    behind_two = jnp.roll(values, 2, axis_id)
    return (8.0 * (ahead_one - behind_one) - (ahead_two - behind_two)) / 12.0


def centered_padded(padded):
    ahead_one = padded[:, :, 3:-1, :]
    behind_one = padded[:, :, 1:-3, :]
    ahead_two = padded[:, :, 4:, :]
    behind_two = padded[:, :, :-4, :]
    return (8.0 * (ahead_one - behind_one) - (ahead_two - behind_two)) / 12.0


def mat_vec(system_matrix, vector):
    return jnp.stack(
        [
            system_matrix[0] * vector[0] + system_matrix[1] * vector[1],
            system_matrix[2] * vector[0] + system_matrix[3] * vector[1],
        ]
    )


def chain_run(coupling, forcing, initial, backward):

    def advance(state, inputs):
        fresh = mat_vec(inputs[0], state) + inputs[1]
        return (fresh, fresh)

    final_state, states = lax.scan(
        advance,
        initial,
        (jnp.moveaxis(coupling, 1, 0), jnp.moveaxis(forcing, 1, 0)),
        reverse=backward,
        unroll=min(LEVEL_UNROLL, coupling.shape[1]),
    )
    return jnp.moveaxis(states, 0, 1)


def column_solve(pieces):
    forcing, lower_part, upper_part = pieces
    initial = jnp.zeros((2,) + forcing.shape[2:], jnp.float32)
    lowered = chain_run(lower_part, forcing, initial, False)
    solved = chain_run(upper_part, lowered, initial, True)
    return lax.all_to_all(solved, "lev", split_axis=1, concat_axis=2, tiled=True)


def local_any(adjoint, courant, metric, pivot_inverse, lower_gain, upper_gain):
    weighted = jnp.concatenate([courant[0] * adjoint, (metric[0] * adjoint[0])[None]], 0)
    padded = with_halo(weighted, (("tile", 2),), 2)
    across = centered_padded(padded)
    advected = adjoint + across[:5] + centered_roll(courant[1] * adjoint, 3)
    pressure_field = advected[4] + across[5] + centered_roll(metric[1] * adjoint[1], 2)
    forcing = mat_vec(pivot_inverse, jnp.stack([advected[2], pressure_field]))
    solved = column_solve(
        (
            lax.all_to_all(forcing, "lev", split_axis=2, concat_axis=1, tiled=True),
            lax.all_to_all(lower_gain, "lev", split_axis=2, concat_axis=1, tiled=True),
            lax.all_to_all(upper_gain, "lev", split_axis=2, concat_axis=1, tiled=True),
        )
    )
    return jnp.stack([advected[0], advected[1], solved[0], advected[3], solved[1]])


def solution(mesh):
    placed = (P(None, "lev", "tile", None),) * 6
    pair = mesh.shape["lev"] == 2 and mesh.shape["tile"] % 2 == 0
    return jax.shard_map(
        local_pair if pair else local_any,
        mesh=mesh,
        in_specs=placed,
        out_specs=P(None, "lev", "tile", None),
        check_vma=False,
    )
```

```python
import jax
import jax.numpy as jnp
from jax import lax
from jax.experimental import pallas as pl
from jax.experimental.pallas import tpu as pltpu
from jax.sharding import PartitionSpec as P

F32 = jnp.float32
VMEM_LIMIT = 24 * 1024 * 1024
EDGE_LEVELS = 8


def held(shape):
    return pltpu.VMEM(shape, F32)


def whole():
    return pl.BlockSpec(memory_space=pltpu.VMEM)


def in_hbm():
    return pl.BlockSpec(memory_space=pltpu.HBM)


def from_hbm(x):
    return pltpu.with_memory_space_constraint(x, pltpu.HBM)


def params():
    return pltpu.CompilerParams(vmem_limit_bytes=VMEM_LIMIT)


def mul(m, v):
    return (m[0] * v[0] + m[1] * v[1], m[2] * v[0] + m[3] * v[1])


def matmul(m, n):
    return (
        m[0] * n[0] + m[1] * n[2],
        m[0] * n[1] + m[1] * n[3],
        m[2] * n[0] + m[3] * n[2],
        m[2] * n[1] + m[3] * n[3],
    )


def add(a, b):
    return tuple(x + y for x, y in zip(a, b, strict=True))


def at(ref, level):
    return tuple(ref[k, level] for k in range(ref.shape[0]))


def emit_edges(adj, courant, metric, out, first):
    for r in range(2):
        row = first + r
        wind = courant[0, :, row, :]
        for k in range(4):
            out[k, r] = wind * adj[k, :, row, :]
        out[4, r] = wind * adj[4, :, row, :] + metric[0, :, row, :] * adj[0, :, row, :]


def fetch_all(sources, targets, sems, levels_each=2):
    sources = list(sources)
    levels_each = min(levels_each, sources[0].shape[1])
    pairs = list(zip(sources, targets, strict=True))
    for i, (source, target) in enumerate(pairs):
        parts = source.shape[1] // levels_each

        def start(n, _, i=i, source=source, target=target, parts=parts):
            k, span = n // parts, pl.ds(lax.rem(n, parts) * levels_each, levels_each)
            pltpu.make_async_copy(
                source.at[k, span], target.at[k, span], sems.at[i]
            ).start()
            return 0

        lax.fori_loop(0, source.shape[0] * parts, start, 0)
    return pairs, sems


def wait_all(fetched):
    pairs, sems = fetched
    for i, (source, target) in enumerate(pairs):
        pltpu.make_async_copy(source, target, sems.at[i]).wait()


def rows_of(refs, first):
    return [ref.at[:, :, pl.ds(first, 2)] for ref in refs]


def is_first_tile():
    return lax.axis_index("tile") == 0


def is_last_tile():
    return lax.axis_index("tile") == lax.axis_size("tile") - 1


def edges_body(
    adj_in, courant_in, metric_in, ahead, adj, courant, metric, sems, head_sems
):
    given, targets = (adj_in, courant_in, metric_in), (adj, courant, metric)
    plane = pl.ds(0, 1)
    sent_in = (adj_in, courant_in.at[plane], metric_in.at[plane])
    sent = (adj, courant.at[plane], metric.at[plane])
    rows = adj.shape[2]
    first, last = is_first_tile(), is_last_tile()
    end = jnp.logical_or(first, last)

    def emit():
        emit_edges(adj, courant, metric, ahead, rows - 2)

    @pl.when(end)
    def _():
        tails = fetch_all(
            rows_of(sent_in, rows - 2), rows_of(sent, rows - 2), sems, EDGE_LEVELS
        )

        @pl.when(last)
        def _():
            fetch_all(rows_of(sent_in, 0), rows_of(sent, 0), head_sems, EDGE_LEVELS)

        wait_all(tails)
        emit()

        @pl.when(last)
        def _():
            pairs = list(zip(rows_of(sent_in, 0), rows_of(sent, 0), strict=True))
            wait_all((pairs, head_sems))

    @pl.when(jnp.logical_not(end))
    def _():
        wait_all(fetch_all(given, targets, sems))
        emit()


def across(q):
    rows = q.shape[0]
    spot = lax.broadcasted_iota(jnp.int32, q.shape, 0)
    out = None
    for step, weight in ((1, 8.0 / 12.0), (2, -1.0 / 12.0)):
        ahead = jnp.where(spot < rows - step, pltpu.roll(q, rows - step, 0), 0.0)
        behind = jnp.where(spot >= step, pltpu.roll(q, step, 0), 0.0)
        term = weight * (ahead - behind)
        out = term if out is None else out + term
    return out


def along(q):
    cols = q.shape[1]
    near = pltpu.roll(q, cols - 1, 1) - pltpu.roll(q, 1, 1)
    wide = pltpu.roll(q, cols - 2, 1) - pltpu.roll(q, 2, 1)
    return (8.0 / 12.0) * near - (1.0 / 12.0) * wide


def passive_base(adj, courant, passive):
    def one(l, _):
        c0, c1 = courant[0, l], courant[1, l]
        for slot, field in ((0, 0), (1, 1), (2, 3)):
            x = adj[field, l]
            passive[slot, l] = x + across(c0 * x) + along(c1 * x)
        return 0

    lax.fori_loop(0, adj.shape[1], one, 0)


def first_tile_body(adj_in, courant_in, metric_in, lower_in, upper_in, pivot_in, *refs):
    behind, adj, courant, metric, *work = refs[3:-2]
    sems, gain_sems = refs[-2:]

    @pl.when(is_first_tile())
    def _():
        fields = fetch_all(
            (adj_in, courant_in, metric_in), (adj, courant, metric), sems
        )
        gains = fetch_all(
            (lower_in, upper_in, pivot_in), work[-2:] + work[-3:-2], gain_sems
        )
        wait_all(fields)
        active_base(adj, courant, metric, work[1])
        summarise(work, gains)

    emit_edges(adj, courant, metric, behind, 0)


def other_tiles_body(adj_in, courant_in, metric_in, lower_in, upper_in, pivot_in, *refs):
    adj, courant, metric, *work = refs[-10:-2]
    sems, gain_sems = refs[-2:]

    @pl.when(jnp.logical_not(is_first_tile()))
    def _():
        last = is_last_tile()
        given, targets = (adj_in, courant_in, metric_in), (adj, courant, metric)

        @pl.when(last)
        def _():
            fetch_all(given, targets, sems)

        gains = fetch_all(
            (lower_in, upper_in, pivot_in), work[-2:] + work[-3:-2], gain_sems
        )

        @pl.when(last)
        def _():
            wait_all((list(zip(given, targets, strict=True)), sems))

        active_base(adj, courant, metric, work[1])
        summarise(work, gains)


def active_base(adj, courant, metric, active):
    def one(l, _):
        c0, c1 = courant[0, l], courant[1, l]
        x = adj[2, l]
        active[0, l] = x + across(c0 * x) + along(c1 * x)
        x = adj[4, l]
        active[1, l] = (
            x
            + across(c0 * x + metric[0, l] * adj[0, l])
            + along(c1 * x + metric[1, l] * adj[1, l])
        )
        return 0

    lax.fori_loop(0, adj.shape[1], one, 0)


def summarise(work, gains):
    bulk, active, pivot, lower, upper = work
    levels = active.shape[1]
    wait_all(gains)
    states = forward(active, pivot, lower)

    rows = active.shape[2]

    def emit(state):
        for k in range(2):
            start = 4 * rows + k * (rows - 8)
            bulk[pl.ds(start, rows - 8)] = state[k][4 : rows - 4]

    @pl.when(lax.axis_index("lev") == 0)
    def _():
        emit(states[-1])

    @pl.when(lax.axis_index("lev") == 1)
    def _():
        emit(backward_first(states, upper))
        chain = [at(lower, 0)]
        for l in range(1, levels):
            chain.append(matmul(at(lower, l), chain[-1]))
        total = chain[-1]
        for l in range(levels - 2, -1, -1):
            total = add(matmul(at(upper, l), total), chain[l])
        for k in range(4):
            bulk[pl.ds(k * rows, rows)] = total[k]


def forward(active, pivot, lower):
    states = []
    for l in range(active.shape[1]):
        fresh = mul(at(pivot, l), at(active, l))
        if states:
            fresh = add(mul(at(lower, l), states[-1]), fresh)
        states.append(fresh)
    return states


def backward_first(states, upper):
    state = states[-1]
    for l in range(len(states) - 2, -1, -1):
        state = add(mul(at(upper, l), state), states[l])
    return state


def add_halo(ref, slot, low, high):
    rows = ref.shape[2]
    near, wide = 8.0 / 12.0, 1.0 / 12.0
    ref[slot, :, 0, :] = ref[slot, :, 0, :] + (wide * low[0] - near * low[1])
    ref[slot, :, 1, :] = ref[slot, :, 1, :] + wide * low[1]
    ref[slot, :, rows - 2, :] = ref[slot, :, rows - 2, :] - wide * high[0]
    ref[slot, :, rows - 1, :] = ref[slot, :, rows - 1, :] + (
        near * high[0] - wide * high[1]
    )


def halo_rows(low, high, field):
    return [[ref[field, r] for r in range(2)] for ref in (low, high)]


def sweep_body(given, pivot, lower, upper, low, high, base, lowered, mine, edges, active, kept):
    del given, base, kept
    levels, rows = active.shape[1:3]
    for slot, field in ((0, 2), (1, 4)):
        add_halo(active, slot, *halo_rows(low, high, field))
    states = forward(active, pivot, lower)
    for l in range(levels):
        for k in range(2):
            lowered[k, l] = states[l][k]

    def emit(state):
        for k in range(2):
            mine[k] = state[k]
            edges[pl.ds(8 * k, 4)] = state[k][:4]
            edges[pl.ds(8 * k + 4, 4)] = state[k][rows - 4 :]

    @pl.when(lax.axis_index("lev") == 0)
    def _():
        emit(states[-1])

    @pl.when(lax.axis_index("lev") == 1)
    def _():
        emit(backward_first(states, upper))


def odd_tiles_body(adj, courant, passive):
    @pl.when(lax.rem(lax.axis_index("tile"), 2) == 1)
    def _():
        passive_base(adj, courant, passive)


def passive_body(adj, courant, base, low, high, out, passive, sems):
    del base

    @pl.when(lax.rem(lax.axis_index("tile"), 2) == 0)
    def _():
        passive_base(adj, courant, passive)

    copies = []
    for slot, field in enumerate((0, 1, 3)):
        add_halo(passive, slot, *halo_rows(low, high, field))
        copies.append(
            pltpu.make_async_copy(passive.at[slot], out.at[field], sems.at[slot])
        )
        copies[-1].start()
    for copy in copies:
        copy.wait()


def solve_body(
    lowered, lower, upper, mine, bulk, edges, partial, out, solved, other, sems
):
    del partial
    levels, rows = lowered.shape[1:3]
    for k in range(2):
        other[k, pl.ds(0, 4)] = edges[pl.ds(8 * k, 4)]
        other[k, pl.ds(4, rows - 8)] = bulk[pl.ds(4 * rows + k * (rows - 8), rows - 8)]
        other[k, pl.ds(rows - 4, 4)] = edges[pl.ds(8 * k + 4, 4)]

    def descend(state, full):
        for l in range(levels - 1, -1, -1):
            if state is None:
                state = full(l)
            else:
                state = add(mul(at(upper, l), state), full(l))
            for k, field in ((0, 2), (1, 4)):
                solved[k, l] = state[k]
                pltpu.make_async_copy(
                    solved.at[k, l], out.at[field, l], sems.at[k]
                ).start()

    @pl.when(lax.axis_index("lev") == 0)
    def _():
        gain = tuple(bulk[pl.ds(k * rows, rows)] for k in range(4))
        descend(
            add(mul(gain, (mine[0], mine[1])), (other[0], other[1])),
            lambda l: at(lowered, l),
        )

    @pl.when(lax.axis_index("lev") == 1)
    def _():
        entering = (other[0], other[1])
        full = []
        for l in range(levels):
            entering = mul(at(lower, l), entering)
            full.append(add(entering, at(lowered, l)))
        descend(None, lambda l: full[l])

    for k, field in ((0, 2), (1, 4)):
        pltpu.make_async_copy(solved.at[k], out.at[field], sems.at[k]).wait()


def local_pair(adjoint, courant, metric, pivot_inverse, lower_gain, upper_gain):
    fields, levels, rows, cols = adjoint.shape
    tiles = lax.axis_size("tile")
    swap = [(0, 1), (1, 0)]
    forth = [(i, (i + 1) % tiles) for i in range(tiles)]
    back = [(i, (i - 1) % tiles) for i in range(tiles)]
    halo = held((fields, 2, levels, cols))
    inputs = [held(adjoint.shape), held(courant.shape), held(metric.shape)]
    sems = pltpu.SemaphoreType.DMA((3,))
    sources = (from_hbm(adjoint), from_hbm(courant), from_hbm(metric))
    gains = (from_hbm(lower_gain), from_hbm(upper_gain), from_hbm(pivot_inverse))
    ahead, *fetched = pl.pallas_call(
        edges_body,
        name="edges",
        in_specs=[in_hbm()] * 3,
        out_specs=[whole()] * 4,
        out_shape=[halo] + inputs,
        scratch_shapes=[sems, sems],
        compiler_params=params(),
    )(*sources)
    work = [
        held((6 * rows - 16, cols)),
        held((2, levels, rows, cols)),
        held(pivot_inverse.shape),
        held(lower_gain.shape),
        held(upper_gain.shape),
    ]
    low = lax.ppermute(ahead, "tile", forth)
    behind, adj, cour, met, *begun = pl.pallas_call(
        first_tile_body,
        name="first_tile",
        in_specs=[in_hbm()] * 6 + [whole()] * 3,
        out_specs=[whole()] * (4 + len(work)),
        out_shape=[halo] + inputs + work,
        scratch_shapes=[sems, sems],
        input_output_aliases={6 + i: 1 + i for i in range(3)},
        compiler_params=params(),
    )(*sources, *gains, *fetched)
    high = lax.ppermute(behind, "tile", back)
    adj, cour, met, summary, active, pivot, lower, upper = pl.pallas_call(
        other_tiles_body,
        name="other_tiles",
        in_specs=[in_hbm()] * 6 + [whole()] * (3 + len(work)),
        out_specs=[whole()] * (3 + len(work)),
        out_shape=inputs + work,
        scratch_shapes=[sems, sems],
        input_output_aliases={6 + i: i for i in range(3 + len(work))},
        compiler_params=params(),
    )(*sources, *gains, adj, cour, met, *begun)
    bulk = lax.ppermute(summary, "lev", swap)
    base = pl.pallas_call(
        odd_tiles_body,
        name="odd_tiles",
        in_specs=[whole()] * 2,
        out_specs=whole(),
        out_shape=held((3, levels, rows, cols)),
        compiler_params=params(),
    )(adj, cour)
    lowered, mine, edges, _, base = pl.pallas_call(
        sweep_body,
        name="sweep",
        in_specs=[whole()] * 7,
        out_specs=[whole()] * 5,
        out_shape=[
            held((2, levels, rows, cols)),
            held((2, rows, cols)),
            held((16, cols)),
            work[1],
            held((3, levels, rows, cols)),
        ],
        input_output_aliases={0: 3, 6: 4},
        compiler_params=params(),
    )(active, pivot, lower, upper, low, high, base)
    got_edges = lax.ppermute(edges, "lev", swap)
    partial, _ = pl.pallas_call(
        passive_body,
        name="passive",
        in_specs=[whole()] * 5,
        out_specs=[pl.BlockSpec(memory_space=pl.ANY), whole()],
        out_shape=[
            jax.ShapeDtypeStruct(adjoint.shape, F32),
            held((3, levels, rows, cols)),
        ],
        scratch_shapes=[sems],
        input_output_aliases={2: 1},
        compiler_params=params(),
    )(adj, cour, base, low, high)
    return pl.pallas_call(
        solve_body,
        name="solve",
        in_specs=[whole()] * 6 + [pl.BlockSpec(memory_space=pl.ANY)],
        out_specs=pl.BlockSpec(memory_space=pl.ANY),
        out_shape=jax.ShapeDtypeStruct(adjoint.shape, F32),
        scratch_shapes=[
            pltpu.VMEM((2, levels, rows, cols), F32),
            pltpu.VMEM((2, rows, cols), F32),
            pltpu.SemaphoreType.DMA((2,)),
        ],
        input_output_aliases={6: 0},
        compiler_params=params(),
    )(lowered, lower, upper, mine, bulk, got_edges, partial)


LEVEL_UNROLL = 16


def with_halo(block, sides, width):
    for axis, dim in sides:
        count = lax.axis_size(axis)
        forward = [(i, i + 1) for i in range(count - 1)]
        forward.append((count - 1, 0))
        backward = [(target, source) for source, target in forward]
        low = lax.ppermute(
            lax.slice_in_dim(block, block.shape[dim] - width, None, axis=dim), axis, forward
        )
        high = lax.ppermute(lax.slice_in_dim(block, 0, width, axis=dim), axis, backward)
        block = jnp.concatenate([low, block, high], axis=dim)
    return block


def centered_roll(values, axis_id):
    ahead_one = jnp.roll(values, -1, axis_id)
    behind_one = jnp.roll(values, 1, axis_id)
    ahead_two = jnp.roll(values, -2, axis_id)
    behind_two = jnp.roll(values, 2, axis_id)
    return (8.0 * (ahead_one - behind_one) - (ahead_two - behind_two)) / 12.0


def centered_padded(padded):
    ahead_one = padded[:, :, 3:-1, :]
    behind_one = padded[:, :, 1:-3, :]
    ahead_two = padded[:, :, 4:, :]
    behind_two = padded[:, :, :-4, :]
    return (8.0 * (ahead_one - behind_one) - (ahead_two - behind_two)) / 12.0


def mat_vec(system_matrix, vector):
    return jnp.stack(
        [
            system_matrix[0] * vector[0] + system_matrix[1] * vector[1],
            system_matrix[2] * vector[0] + system_matrix[3] * vector[1],
        ]
    )


def chain_run(coupling, forcing, initial, backward):

    def advance(state, inputs):
        fresh = mat_vec(inputs[0], state) + inputs[1]
        return (fresh, fresh)

    final_state, states = lax.scan(
        advance,
        initial,
        (jnp.moveaxis(coupling, 1, 0), jnp.moveaxis(forcing, 1, 0)),
        reverse=backward,
        unroll=min(LEVEL_UNROLL, coupling.shape[1]),
    )
    return jnp.moveaxis(states, 0, 1)


def column_solve(pieces):
    forcing, lower_part, upper_part = pieces
    initial = jnp.zeros((2,) + forcing.shape[2:], jnp.float32)
    lowered = chain_run(lower_part, forcing, initial, False)
    solved = chain_run(upper_part, lowered, initial, True)
    return lax.all_to_all(solved, "lev", split_axis=1, concat_axis=2, tiled=True)


def local_any(adjoint, courant, metric, pivot_inverse, lower_gain, upper_gain):
    weighted = jnp.concatenate([courant[0] * adjoint, (metric[0] * adjoint[0])[None]], 0)
    padded = with_halo(weighted, (("tile", 2),), 2)
    across = centered_padded(padded)
    advected = adjoint + across[:5] + centered_roll(courant[1] * adjoint, 3)
    pressure_field = advected[4] + across[5] + centered_roll(metric[1] * adjoint[1], 2)
    forcing = mat_vec(pivot_inverse, jnp.stack([advected[2], pressure_field]))
    solved = column_solve(
        (
            lax.all_to_all(forcing, "lev", split_axis=2, concat_axis=1, tiled=True),
            lax.all_to_all(lower_gain, "lev", split_axis=2, concat_axis=1, tiled=True),
            lax.all_to_all(upper_gain, "lev", split_axis=2, concat_axis=1, tiled=True),
        )
    )
    return jnp.stack([advected[0], advected[1], solved[0], advected[3], solved[1]])


def solution(mesh):
    placed = (P(None, "lev", "tile", None),) * 6
    pair = mesh.shape["lev"] == 2 and mesh.shape["tile"] % 2 == 0

    def local(adjoint, *others):
        levels, rows = adjoint.shape[1:3]
        fits = pair and levels % 2 == 0 and rows % 8 == 0 and rows > 8
        return (local_pair if fits else local_any)(adjoint, *others)

    return jax.shard_map(
        local,
        mesh=mesh,
        in_specs=placed,
        out_specs=P(None, "lev", "tile", None),
        check_vma=False,
    )
```

```python
import jax
import jax.numpy as jnp
from jax import lax
from jax.experimental import pallas as pl
from jax.experimental.pallas import tpu as pltpu
from jax.sharding import PartitionSpec as P

F32 = jnp.float32
VMEM_LIMIT = 24 * 1024 * 1024
EDGE_LEVELS = 8


def held(shape):
    return pltpu.VMEM(shape, F32)


def whole():
    return pl.BlockSpec(memory_space=pltpu.VMEM)


def in_hbm():
    return pl.BlockSpec(memory_space=pltpu.HBM)


def from_hbm(x):
    return pltpu.with_memory_space_constraint(x, pltpu.HBM)


def params():
    return pltpu.CompilerParams(vmem_limit_bytes=VMEM_LIMIT)


def mul(m, v):
    return (m[0] * v[0] + m[1] * v[1], m[2] * v[0] + m[3] * v[1])


def matmul(m, n):
    return (
        m[0] * n[0] + m[1] * n[2],
        m[0] * n[1] + m[1] * n[3],
        m[2] * n[0] + m[3] * n[2],
        m[2] * n[1] + m[3] * n[3],
    )


def add(a, b):
    return tuple(x + y for x, y in zip(a, b, strict=True))


def at(ref, level):
    return tuple(ref[k, level] for k in range(ref.shape[0]))


def emit_edges(adj, courant, metric, out, first):
    for r in range(2):
        row = first + r
        wind = courant[0, :, row, :]
        for k in range(4):
            out[k, r] = wind * adj[k, :, row, :]
        out[4, r] = wind * adj[4, :, row, :] + metric[0, :, row, :] * adj[0, :, row, :]


def fetch_all(sources, targets, sems, levels_each=2):
    sources = list(sources)
    levels_each = min(levels_each, sources[0].shape[1])
    pairs = list(zip(sources, targets, strict=True))
    for i, (source, target) in enumerate(pairs):
        parts = source.shape[1] // levels_each

        def start(n, _, i=i, source=source, target=target, parts=parts):
            k, span = n // parts, pl.ds(lax.rem(n, parts) * levels_each, levels_each)
            pltpu.make_async_copy(
                source.at[k, span], target.at[k, span], sems.at[i]
            ).start()
            return 0

        lax.fori_loop(0, source.shape[0] * parts, start, 0)
    return pairs, sems


def wait_all(fetched):
    pairs, sems = fetched
    for i, (source, target) in enumerate(pairs):
        pltpu.make_async_copy(source, target, sems.at[i]).wait()


def rows_of(refs, first):
    return [ref.at[:, :, pl.ds(first, 2)] for ref in refs]


def is_first_tile():
    return lax.axis_index("tile") == 0


def is_first_of_all():
    return jnp.logical_and(is_first_tile(), lax.axis_index("lev") == 0)


def is_last_tile():
    return lax.axis_index("tile") == lax.axis_size("tile") - 1


def edges_body(
    adj_in, courant_in, metric_in, ahead, adj, courant, metric, sems, head_sems
):
    given, targets = (adj_in, courant_in, metric_in), (adj, courant, metric)
    plane = pl.ds(0, 1)
    sent_in = (adj_in, courant_in.at[plane], metric_in.at[plane])
    sent = (adj, courant.at[plane], metric.at[plane])
    rows = adj.shape[2]
    first, last = is_first_tile(), is_last_tile()
    end = jnp.logical_or(first, last)

    def emit():
        emit_edges(adj, courant, metric, ahead, rows - 2)

    @pl.when(end)
    def _():
        tails = fetch_all(
            rows_of(sent_in, rows - 2), rows_of(sent, rows - 2), sems, EDGE_LEVELS
        )

        @pl.when(last)
        def _():
            fetch_all(rows_of(sent_in, 0), rows_of(sent, 0), head_sems, EDGE_LEVELS)

        wait_all(tails)
        emit()

        @pl.when(last)
        def _():
            pairs = list(zip(rows_of(sent_in, 0), rows_of(sent, 0), strict=True))
            wait_all((pairs, head_sems))

    @pl.when(jnp.logical_not(end))
    def _():
        wait_all(fetch_all(given, targets, sems))
        emit()


def across(q):
    rows = q.shape[0]
    spot = lax.broadcasted_iota(jnp.int32, q.shape, 0)
    out = None
    for step, weight in ((1, 8.0 / 12.0), (2, -1.0 / 12.0)):
        ahead = jnp.where(spot < rows - step, pltpu.roll(q, rows - step, 0), 0.0)
        behind = jnp.where(spot >= step, pltpu.roll(q, step, 0), 0.0)
        term = weight * (ahead - behind)
        out = term if out is None else out + term
    return out


def along(q):
    cols = q.shape[1]
    near = pltpu.roll(q, cols - 1, 1) - pltpu.roll(q, 1, 1)
    wide = pltpu.roll(q, cols - 2, 1) - pltpu.roll(q, 2, 1)
    return (8.0 / 12.0) * near - (1.0 / 12.0) * wide


def passive_base(adj, courant, passive):
    def one(l, _):
        c0, c1 = courant[0, l], courant[1, l]
        for slot, field in ((0, 0), (1, 1), (2, 3)):
            x = adj[field, l]
            passive[slot, l] = x + across(c0 * x) + along(c1 * x)
        return 0

    lax.fori_loop(0, adj.shape[1], one, 0)


def first_tile_body(adj_in, courant_in, metric_in, lower_in, upper_in, pivot_in, *refs):
    behind, adj, courant, metric, *work = refs[3:-2]
    sems, gain_sems = refs[-2:]

    @pl.when(is_first_tile())
    def _():
        fields = fetch_all(
            (adj_in, courant_in, metric_in), (adj, courant, metric), sems
        )
        gains = fetch_all(
            (lower_in, upper_in, pivot_in), work[-2:] + work[-3:-2], gain_sems
        )
        wait_all(fields)
        active_base(adj, courant, metric, work[1])
        summarise(work, gains)

    emit_edges(adj, courant, metric, behind, 0)


def other_tiles_body(adj_in, courant_in, metric_in, lower_in, upper_in, pivot_in, *refs):
    passive, adj, courant, metric, *work = refs[-11:-2]
    sems, gain_sems = refs[-2:]

    @pl.when(is_first_of_all())
    def _():
        passive_base(adj, courant, passive)

    @pl.when(jnp.logical_not(is_first_tile()))
    def _():
        last = is_last_tile()
        given, targets = (adj_in, courant_in, metric_in), (adj, courant, metric)

        @pl.when(last)
        def _():
            fetch_all(given, targets, sems)

        gains = fetch_all(
            (lower_in, upper_in, pivot_in), work[-2:] + work[-3:-2], gain_sems
        )

        @pl.when(last)
        def _():
            wait_all((list(zip(given, targets, strict=True)), sems))

        active_base(adj, courant, metric, work[1])
        summarise(work, gains)


def active_base(adj, courant, metric, active):
    def one(l, _):
        c0, c1 = courant[0, l], courant[1, l]
        x = adj[2, l]
        active[0, l] = x + across(c0 * x) + along(c1 * x)
        x = adj[4, l]
        active[1, l] = (
            x
            + across(c0 * x + metric[0, l] * adj[0, l])
            + along(c1 * x + metric[1, l] * adj[1, l])
        )
        return 0

    lax.fori_loop(0, adj.shape[1], one, 0)


def summarise(work, gains):
    bulk, active, pivot, lower, upper = work
    levels = active.shape[1]
    wait_all(gains)
    states = forward(active, pivot, lower)

    rows = active.shape[2]

    def emit(state):
        for k in range(2):
            start = 4 * rows + k * (rows - 4)
            bulk[pl.ds(start, rows - 4)] = state[k][2 : rows - 2]

    @pl.when(lax.axis_index("lev") == 0)
    def _():
        emit(states[-1])

    @pl.when(lax.axis_index("lev") == 1)
    def _():
        emit(backward_first(states, upper))
        chain = [at(lower, 0)]
        for l in range(1, levels):
            chain.append(matmul(at(lower, l), chain[-1]))
        total = chain[-1]
        for l in range(levels - 2, -1, -1):
            total = add(matmul(at(upper, l), total), chain[l])
        for k in range(4):
            bulk[pl.ds(k * rows, rows)] = total[k]


def forward(active, pivot, lower):
    states = []
    for l in range(active.shape[1]):
        fresh = mul(at(pivot, l), at(active, l))
        if states:
            fresh = add(mul(at(lower, l), states[-1]), fresh)
        states.append(fresh)
    return states


def backward_first(states, upper):
    state = states[-1]
    for l in range(len(states) - 2, -1, -1):
        state = add(mul(at(upper, l), state), states[l])
    return state


def add_halo(ref, slot, low, high):
    rows = ref.shape[2]
    near, wide = 8.0 / 12.0, 1.0 / 12.0
    ref[slot, :, 0, :] = ref[slot, :, 0, :] + (wide * low[0] - near * low[1])
    ref[slot, :, 1, :] = ref[slot, :, 1, :] + wide * low[1]
    ref[slot, :, rows - 2, :] = ref[slot, :, rows - 2, :] - wide * high[0]
    ref[slot, :, rows - 1, :] = ref[slot, :, rows - 1, :] + (
        near * high[0] - wide * high[1]
    )


def halo_rows(low, high, field):
    return [[ref[field, r] for r in range(2)] for ref in (low, high)]


def sweep_body(given, pivot, lower, upper, low, high, base, lowered, mine, edges, active, kept):
    del given, base, kept
    levels, rows = active.shape[1:3]
    for slot, field in ((0, 2), (1, 4)):
        add_halo(active, slot, *halo_rows(low, high, field))
    states = forward(active, pivot, lower)
    for l in range(levels):
        for k in range(2):
            lowered[k, l] = states[l][k]

    def emit(state):
        for k in range(2):
            mine[k] = state[k]
            edges[pl.ds(4 * k, 2)] = state[k][:2]
            edges[pl.ds(4 * k + 2, 2)] = state[k][rows - 2 :]

    @pl.when(lax.axis_index("lev") == 0)
    def _():
        emit(states[-1])

    @pl.when(lax.axis_index("lev") == 1)
    def _():
        emit(backward_first(states, upper))


def odd_tiles_body(adj, courant, base, passive):
    del base

    @pl.when(lax.rem(lax.axis_index("tile"), 2) == 1)
    def _():
        passive_base(adj, courant, passive)


def passive_body(adj, courant, base, low, high, out, passive, sems):
    del base

    even = lax.rem(lax.axis_index("tile"), 2) == 0

    @pl.when(jnp.logical_and(even, jnp.logical_not(is_first_of_all())))
    def _():
        passive_base(adj, courant, passive)

    copies = []
    for slot, field in enumerate((0, 1, 3)):
        add_halo(passive, slot, *halo_rows(low, high, field))
        copies.append(
            pltpu.make_async_copy(passive.at[slot], out.at[field], sems.at[slot])
        )
        copies[-1].start()
    for copy in copies:
        copy.wait()


def solve_body(
    lowered, lower, upper, mine, bulk, edges, partial, out, solved, other, sems
):
    del partial
    levels, rows = lowered.shape[1:3]
    for k in range(2):
        other[k, pl.ds(0, 2)] = edges[pl.ds(4 * k, 2)]
        other[k, pl.ds(2, rows - 4)] = bulk[pl.ds(4 * rows + k * (rows - 4), rows - 4)]
        other[k, pl.ds(rows - 2, 2)] = edges[pl.ds(4 * k + 2, 2)]

    def descend(state, full):
        for l in range(levels - 1, -1, -1):
            if state is None:
                state = full(l)
            else:
                state = add(mul(at(upper, l), state), full(l))
            for k, field in ((0, 2), (1, 4)):
                solved[k, l] = state[k]
                pltpu.make_async_copy(
                    solved.at[k, l], out.at[field, l], sems.at[k]
                ).start()

    @pl.when(lax.axis_index("lev") == 0)
    def _():
        gain = tuple(bulk[pl.ds(k * rows, rows)] for k in range(4))
        descend(
            add(mul(gain, (mine[0], mine[1])), (other[0], other[1])),
            lambda l: at(lowered, l),
        )

    @pl.when(lax.axis_index("lev") == 1)
    def _():
        entering = (other[0], other[1])
        full = []
        for l in range(levels):
            entering = mul(at(lower, l), entering)
            full.append(add(entering, at(lowered, l)))
        descend(None, lambda l: full[l])

    for k, field in ((0, 2), (1, 4)):
        pltpu.make_async_copy(solved.at[k], out.at[field], sems.at[k]).wait()


def local_pair(adjoint, courant, metric, pivot_inverse, lower_gain, upper_gain):
    fields, levels, rows, cols = adjoint.shape
    tiles = lax.axis_size("tile")
    swap = [(0, 1), (1, 0)]
    forth = [(i, (i + 1) % tiles) for i in range(tiles)]
    back = [(i, (i - 1) % tiles) for i in range(tiles)]
    halo = held((fields, 2, levels, cols))
    inputs = [held(adjoint.shape), held(courant.shape), held(metric.shape)]
    sems = pltpu.SemaphoreType.DMA((3,))
    sources = (from_hbm(adjoint), from_hbm(courant), from_hbm(metric))
    gains = (from_hbm(lower_gain), from_hbm(upper_gain), from_hbm(pivot_inverse))
    ahead, *fetched = pl.pallas_call(
        edges_body,
        name="edges",
        in_specs=[in_hbm()] * 3,
        out_specs=[whole()] * 4,
        out_shape=[halo] + inputs,
        scratch_shapes=[sems, sems],
        compiler_params=params(),
    )(*sources)
    work = [
        held((6 * rows - 8, cols)),
        held((2, levels, rows, cols)),
        held(pivot_inverse.shape),
        held(lower_gain.shape),
        held(upper_gain.shape),
    ]
    low = lax.ppermute(ahead, "tile", forth)
    behind, adj, cour, met, *begun = pl.pallas_call(
        first_tile_body,
        name="first_tile",
        in_specs=[in_hbm()] * 6 + [whole()] * 3,
        out_specs=[whole()] * (4 + len(work)),
        out_shape=[halo] + inputs + work,
        scratch_shapes=[sems, sems],
        input_output_aliases={6 + i: 1 + i for i in range(3)},
        compiler_params=params(),
    )(*sources, *gains, *fetched)
    high = lax.ppermute(behind, "tile", back)
    base, adj, cour, met, summary, active, pivot, lower, upper = pl.pallas_call(
        other_tiles_body,
        name="other_tiles",
        in_specs=[in_hbm()] * 6 + [whole()] * (3 + len(work)),
        out_specs=[whole()] * (4 + len(work)),
        out_shape=[held((3, levels, rows, cols))] + inputs + work,
        scratch_shapes=[sems, sems],
        input_output_aliases={6 + i: 1 + i for i in range(3 + len(work))},
        compiler_params=params(),
    )(*sources, *gains, adj, cour, met, *begun)
    bulk = lax.ppermute(summary, "lev", swap)
    base = pl.pallas_call(
        odd_tiles_body,
        name="odd_tiles",
        in_specs=[whole()] * 3,
        out_specs=whole(),
        out_shape=held((3, levels, rows, cols)),
        input_output_aliases={2: 0},
        compiler_params=params(),
    )(adj, cour, base)
    lowered, mine, edges, _, base = pl.pallas_call(
        sweep_body,
        name="sweep",
        in_specs=[whole()] * 7,
        out_specs=[whole()] * 5,
        out_shape=[
            held((2, levels, rows, cols)),
            held((2, rows, cols)),
            held((8, cols)),
            work[1],
            held((3, levels, rows, cols)),
        ],
        input_output_aliases={0: 3, 6: 4},
        compiler_params=params(),
    )(active, pivot, lower, upper, low, high, base)
    got_edges = lax.ppermute(edges, "lev", swap)
    partial, _ = pl.pallas_call(
        passive_body,
        name="passive",
        in_specs=[whole()] * 5,
        out_specs=[pl.BlockSpec(memory_space=pl.ANY), whole()],
        out_shape=[
            jax.ShapeDtypeStruct(adjoint.shape, F32),
            held((3, levels, rows, cols)),
        ],
        scratch_shapes=[sems],
        input_output_aliases={2: 1},
        compiler_params=params(),
    )(adj, cour, base, low, high)
    return pl.pallas_call(
        solve_body,
        name="solve",
        in_specs=[whole()] * 6 + [pl.BlockSpec(memory_space=pl.ANY)],
        out_specs=pl.BlockSpec(memory_space=pl.ANY),
        out_shape=jax.ShapeDtypeStruct(adjoint.shape, F32),
        scratch_shapes=[
            pltpu.VMEM((2, levels, rows, cols), F32),
            pltpu.VMEM((2, rows, cols), F32),
            pltpu.SemaphoreType.DMA((2,)),
        ],
        input_output_aliases={6: 0},
        compiler_params=params(),
    )(lowered, lower, upper, mine, bulk, got_edges, partial)


LEVEL_UNROLL = 16


def with_halo(block, sides, width):
    for axis, dim in sides:
        count = lax.axis_size(axis)
        forward = [(i, i + 1) for i in range(count - 1)]
        forward.append((count - 1, 0))
        backward = [(target, source) for source, target in forward]
        low = lax.ppermute(
            lax.slice_in_dim(block, block.shape[dim] - width, None, axis=dim), axis, forward
        )
        high = lax.ppermute(lax.slice_in_dim(block, 0, width, axis=dim), axis, backward)
        block = jnp.concatenate([low, block, high], axis=dim)
    return block


def centered_roll(values, axis_id):
    ahead_one = jnp.roll(values, -1, axis_id)
    behind_one = jnp.roll(values, 1, axis_id)
    ahead_two = jnp.roll(values, -2, axis_id)
    behind_two = jnp.roll(values, 2, axis_id)
    return (8.0 * (ahead_one - behind_one) - (ahead_two - behind_two)) / 12.0


def centered_padded(padded):
    ahead_one = padded[:, :, 3:-1, :]
    behind_one = padded[:, :, 1:-3, :]
    ahead_two = padded[:, :, 4:, :]
    behind_two = padded[:, :, :-4, :]
    return (8.0 * (ahead_one - behind_one) - (ahead_two - behind_two)) / 12.0


def mat_vec(system_matrix, vector):
    return jnp.stack(
        [
            system_matrix[0] * vector[0] + system_matrix[1] * vector[1],
            system_matrix[2] * vector[0] + system_matrix[3] * vector[1],
        ]
    )


def chain_run(coupling, forcing, initial, backward):

    def advance(state, inputs):
        fresh = mat_vec(inputs[0], state) + inputs[1]
        return (fresh, fresh)

    final_state, states = lax.scan(
        advance,
        initial,
        (jnp.moveaxis(coupling, 1, 0), jnp.moveaxis(forcing, 1, 0)),
        reverse=backward,
        unroll=min(LEVEL_UNROLL, coupling.shape[1]),
    )
    return jnp.moveaxis(states, 0, 1)


def column_solve(pieces):
    forcing, lower_part, upper_part = pieces
    initial = jnp.zeros((2,) + forcing.shape[2:], jnp.float32)
    lowered = chain_run(lower_part, forcing, initial, False)
    solved = chain_run(upper_part, lowered, initial, True)
    return lax.all_to_all(solved, "lev", split_axis=1, concat_axis=2, tiled=True)


def local_any(adjoint, courant, metric, pivot_inverse, lower_gain, upper_gain):
    weighted = jnp.concatenate([courant[0] * adjoint, (metric[0] * adjoint[0])[None]], 0)
    padded = with_halo(weighted, (("tile", 2),), 2)
    across = centered_padded(padded)
    advected = adjoint + across[:5] + centered_roll(courant[1] * adjoint, 3)
    pressure_field = advected[4] + across[5] + centered_roll(metric[1] * adjoint[1], 2)
    forcing = mat_vec(pivot_inverse, jnp.stack([advected[2], pressure_field]))
    solved = column_solve(
        (
            lax.all_to_all(forcing, "lev", split_axis=2, concat_axis=1, tiled=True),
            lax.all_to_all(lower_gain, "lev", split_axis=2, concat_axis=1, tiled=True),
            lax.all_to_all(upper_gain, "lev", split_axis=2, concat_axis=1, tiled=True),
        )
    )
    return jnp.stack([advected[0], advected[1], solved[0], advected[3], solved[1]])


def solution(mesh):
    placed = (P(None, "lev", "tile", None),) * 6
    pair = mesh.shape["lev"] == 2 and mesh.shape["tile"] % 2 == 0

    def local(adjoint, *others):
        levels, rows = adjoint.shape[1:3]
        fits = pair and levels % EDGE_LEVELS == 0 and rows % 8 == 0 and rows > 8
        return (local_pair if fits else local_any)(adjoint, *others)

    return jax.shard_map(
        local,
        mesh=mesh,
        in_specs=placed,
        out_specs=P(None, "lev", "tile", None),
        check_vma=False,
    )
```

```python
import jax
import jax.numpy as jnp
from jax import lax
from jax.experimental import pallas as pl
from jax.experimental.pallas import tpu as pltpu
from jax.sharding import PartitionSpec as P

F32 = jnp.float32
VMEM_LIMIT = 24 * 1024 * 1024
EDGE_LEVELS = 8


def held(shape):
    return pltpu.VMEM(shape, F32)


def whole():
    return pl.BlockSpec(memory_space=pltpu.VMEM)


def in_hbm():
    return pl.BlockSpec(memory_space=pltpu.HBM)


def from_hbm(x):
    return pltpu.with_memory_space_constraint(x, pltpu.HBM)


def params():
    return pltpu.CompilerParams(vmem_limit_bytes=VMEM_LIMIT)


def mul(m, v):
    return (m[0] * v[0] + m[1] * v[1], m[2] * v[0] + m[3] * v[1])


def matmul(m, n):
    return (
        m[0] * n[0] + m[1] * n[2],
        m[0] * n[1] + m[1] * n[3],
        m[2] * n[0] + m[3] * n[2],
        m[2] * n[1] + m[3] * n[3],
    )


def add(a, b):
    return tuple(x + y for x, y in zip(a, b, strict=True))


def at(ref, level):
    return tuple(ref[k, level] for k in range(ref.shape[0]))


def emit_edges(adj, courant, metric, out, first):
    for r in range(2):
        row = first + r
        wind = courant[0, :, row, :]
        for k in range(4):
            out[k, r] = wind * adj[k, :, row, :]
        out[4, r] = wind * adj[4, :, row, :] + metric[0, :, row, :] * adj[0, :, row, :]


def fetch_all(sources, targets, sems, levels_each=2):
    levels_each = min(levels_each, sources[0].shape[1])
    for i, (source, target) in enumerate(zip(sources, targets, strict=True)):
        parts = source.shape[1] // levels_each

        def start(n, _, i=i, source=source, target=target, parts=parts):
            k, span = n // parts, pl.ds(lax.rem(n, parts) * levels_each, levels_each)
            pltpu.make_async_copy(
                source.at[k, span], target.at[k, span], sems.at[i]
            ).start()
            return 0

        lax.fori_loop(0, source.shape[0] * parts, start, 0)


def wait_all(sources, targets, sems):
    for i, (source, target) in enumerate(zip(sources, targets, strict=True)):
        pltpu.make_async_copy(source, target, sems.at[i]).wait()


def rows_of(refs, first):
    return [ref.at[:, :, pl.ds(first, 2)] for ref in refs]


def is_first_tile():
    return lax.axis_index("tile") == 0


def is_first_chip(tile):
    return jnp.logical_and(lax.axis_index("tile") == tile, lax.axis_index("lev") == 0)


def is_last_tile():
    return lax.axis_index("tile") == lax.axis_size("tile") - 1


def edges_body(
    adj_in, courant_in, metric_in, ahead, adj, courant, metric, sems, head_sems
):
    given, targets = (adj_in, courant_in, metric_in), (adj, courant, metric)
    plane = pl.ds(0, 1)
    sent_in = (courant_in.at[plane], metric_in.at[plane], adj_in)
    sent = (courant.at[plane], metric.at[plane], adj)
    rows = adj.shape[2]
    first, last = is_first_tile(), is_last_tile()
    end = jnp.logical_or(first, last)

    tails = (rows_of(sent_in, rows - 2), rows_of(sent, rows - 2), sems)
    heads = (rows_of(sent_in, 0), rows_of(sent, 0), head_sems)

    @pl.when(end)
    def _():
        fetch_all(*tails, EDGE_LEVELS)

        @pl.when(last)
        def _():
            fetch_all(*heads, EDGE_LEVELS)

        wait_all(*tails)

    @pl.when(jnp.logical_not(end))
    def _():
        fetch_all(given, targets, sems)
        wait_all(given, targets, sems)

    emit_edges(adj, courant, metric, ahead, rows - 2)

    @pl.when(last)
    def _():
        wait_all(*heads)


def across(q):
    rows = q.shape[0]
    spot = lax.broadcasted_iota(jnp.int32, q.shape, 0)
    out = None
    for step, weight in ((1, 8.0 / 12.0), (2, -1.0 / 12.0)):
        ahead = jnp.where(spot < rows - step, pltpu.roll(q, rows - step, 0), 0.0)
        behind = jnp.where(spot >= step, pltpu.roll(q, step, 0), 0.0)
        term = weight * (ahead - behind)
        out = term if out is None else out + term
    return out


def along(q):
    cols = q.shape[1]
    near = pltpu.roll(q, cols - 1, 1) - pltpu.roll(q, 1, 1)
    wide = pltpu.roll(q, cols - 2, 1) - pltpu.roll(q, 2, 1)
    return (8.0 / 12.0) * near - (1.0 / 12.0) * wide


def passive_base(adj, courant, passive):
    def one(l, _):
        c0, c1 = courant[0, l], courant[1, l]
        for slot, field in ((0, 0), (1, 1), (2, 3)):
            x = adj[field, l]
            passive[slot, l] = x + across(c0 * x) + along(c1 * x)
        return 0

    lax.fori_loop(0, adj.shape[1], one, 0)


def first_tile_body(adj_in, courant_in, metric_in, pivot_in, lower_in, upper_in, *refs):
    behind, passive, adj, courant, metric, *work = refs[3:-2]
    sems, gain_sems = refs[-2:]

    @pl.when(is_first_tile())
    def _():
        fields = ((adj_in, courant_in, metric_in), (adj, courant, metric), sems)
        gains = ((pivot_in, lower_in, upper_in), work[-3:], gain_sems)
        fetch_all(*fields)
        fetch_all(*gains)
        wait_all(*fields)
        active_base(adj, courant, metric, work[1])
        summarise(work, gains)

    @pl.when(is_first_chip(0))
    def _():
        passive_base(adj, courant, passive)

    emit_edges(adj, courant, metric, behind, 0)


def other_tiles_body(adj_in, courant_in, metric_in, pivot_in, lower_in, upper_in, *refs):
    passive, adj, courant, metric, *work = refs[-11:-2]
    sems, gain_sems = refs[-2:]

    @pl.when(is_first_chip(1))
    def _():
        passive_base(adj, courant, passive)

    @pl.when(jnp.logical_not(is_first_tile()))
    def _():
        last = is_last_tile()
        fields = ((adj_in, courant_in, metric_in), (adj, courant, metric), sems)
        gains = ((pivot_in, lower_in, upper_in), work[-3:], gain_sems)

        @pl.when(last)
        def _():
            fetch_all(*fields)

        fetch_all(*gains)

        @pl.when(last)
        def _():
            wait_all(*fields)

        active_base(adj, courant, metric, work[1])
        summarise(work, gains)


def active_base(adj, courant, metric, active):
    def one(l, _):
        c0, c1 = courant[0, l], courant[1, l]
        x = adj[2, l]
        active[0, l] = x + across(c0 * x) + along(c1 * x)
        x = adj[4, l]
        active[1, l] = (
            x
            + across(c0 * x + metric[0, l] * adj[0, l])
            + along(c1 * x + metric[1, l] * adj[1, l])
        )
        return 0

    lax.fori_loop(0, adj.shape[1], one, 0)


def summarise(work, gains):
    bulk, active, pivot, lower, upper = work
    levels = active.shape[1]
    wait_all(*gains)
    states = forward(active, pivot, lower)

    rows = active.shape[2]

    def emit(state):
        for k in range(2):
            start = 4 * rows + k * (rows - 4)
            bulk[pl.ds(start, rows - 4)] = state[k][2 : rows - 2]

    @pl.when(lax.axis_index("lev") == 0)
    def _():
        emit(states[-1])

    @pl.when(lax.axis_index("lev") == 1)
    def _():
        emit(backward_first(states, upper))
        chain = [at(lower, 0)]
        for l in range(1, levels):
            chain.append(matmul(at(lower, l), chain[-1]))
        total = chain[-1]
        for l in range(levels - 2, -1, -1):
            total = add(matmul(at(upper, l), total), chain[l])
        for k in range(4):
            bulk[pl.ds(k * rows, rows)] = total[k]


def forward(active, pivot, lower):
    states = []
    for l in range(active.shape[1]):
        fresh = mul(at(pivot, l), at(active, l))
        if states:
            fresh = add(mul(at(lower, l), states[-1]), fresh)
        states.append(fresh)
    return states


def backward_first(states, upper):
    state = states[-1]
    for l in range(len(states) - 2, -1, -1):
        state = add(mul(at(upper, l), state), states[l])
    return state


def add_halo(ref, slot, low, high):
    rows = ref.shape[2]
    near, wide = 8.0 / 12.0, 1.0 / 12.0
    ref[slot, :, 0, :] = ref[slot, :, 0, :] + (wide * low[0] - near * low[1])
    ref[slot, :, 1, :] = ref[slot, :, 1, :] + wide * low[1]
    ref[slot, :, rows - 2, :] = ref[slot, :, rows - 2, :] - wide * high[0]
    ref[slot, :, rows - 1, :] = ref[slot, :, rows - 1, :] + (
        near * high[0] - wide * high[1]
    )


def halo_rows(low, high, field):
    return [[ref[field, r] for r in range(2)] for ref in (low, high)]


def sweep_body(given, pivot, lower, upper, low, high, base, lowered, mine, edges, active, kept):
    del given, base, kept
    levels, rows = active.shape[1:3]
    for slot, field in ((0, 2), (1, 4)):
        add_halo(active, slot, *halo_rows(low, high, field))
    states = forward(active, pivot, lower)
    for l in range(levels):
        for k in range(2):
            lowered[k, l] = states[l][k]

    def emit(state):
        for k in range(2):
            mine[k] = state[k]
            edges[pl.ds(4 * k, 2)] = state[k][:2]
            edges[pl.ds(4 * k + 2, 2)] = state[k][rows - 2 :]

    @pl.when(lax.axis_index("lev") == 0)
    def _():
        emit(states[-1])

    @pl.when(lax.axis_index("lev") == 1)
    def _():
        emit(backward_first(states, upper))


def odd_tiles_body(adj, courant, base, passive):
    del base

    odd = lax.rem(lax.axis_index("tile"), 2) == 1

    @pl.when(jnp.logical_and(odd, jnp.logical_not(is_first_chip(1))))
    def _():
        passive_base(adj, courant, passive)


def passive_body(adj, courant, base, low, high, out, passive, sems):
    del base

    even = lax.rem(lax.axis_index("tile"), 2) == 0

    @pl.when(jnp.logical_and(even, jnp.logical_not(is_first_chip(0))))
    def _():
        passive_base(adj, courant, passive)

    copies = []
    for slot, field in enumerate((0, 1, 3)):
        add_halo(passive, slot, *halo_rows(low, high, field))
        copies.append(
            pltpu.make_async_copy(passive.at[slot], out.at[field], sems.at[slot])
        )
        copies[-1].start()
    for copy in copies:
        copy.wait()


def solve_body(
    lowered, lower, upper, mine, bulk, edges, partial, out, solved, other, sems
):
    del partial
    levels, rows = lowered.shape[1:3]
    for k in range(2):
        other[k, pl.ds(0, 2)] = edges[pl.ds(4 * k, 2)]
        other[k, pl.ds(2, rows - 4)] = bulk[pl.ds(4 * rows + k * (rows - 4), rows - 4)]
        other[k, pl.ds(rows - 2, 2)] = edges[pl.ds(4 * k + 2, 2)]

    def descend(state, full):
        for l in range(levels - 1, -1, -1):
            if state is None:
                state = full(l)
            else:
                state = add(mul(at(upper, l), state), full(l))
            for k, field in ((0, 2), (1, 4)):
                solved[k, l] = state[k]
                pltpu.make_async_copy(
                    solved.at[k, l], out.at[field, l], sems.at[k]
                ).start()

    @pl.when(lax.axis_index("lev") == 0)
    def _():
        gain = tuple(bulk[pl.ds(k * rows, rows)] for k in range(4))
        descend(
            add(mul(gain, (mine[0], mine[1])), (other[0], other[1])),
            lambda l: at(lowered, l),
        )

    @pl.when(lax.axis_index("lev") == 1)
    def _():
        entering = (other[0], other[1])
        full = []
        for l in range(levels):
            entering = mul(at(lower, l), entering)
            full.append(add(entering, at(lowered, l)))
        descend(None, lambda l: full[l])

    for k, field in ((0, 2), (1, 4)):
        pltpu.make_async_copy(solved.at[k], out.at[field], sems.at[k]).wait()


def local_pair(adjoint, courant, metric, pivot_inverse, lower_gain, upper_gain):
    fields, levels, rows, cols = adjoint.shape
    tiles = lax.axis_size("tile")
    swap = [(0, 1), (1, 0)]
    forth = [(i, (i + 1) % tiles) for i in range(tiles)]
    back = [(i, (i - 1) % tiles) for i in range(tiles)]
    halo = held((fields, 2, levels, cols))
    passive = held((3, levels, rows, cols))
    inputs = [held(adjoint.shape), held(courant.shape), held(metric.shape)]
    sems = pltpu.SemaphoreType.DMA((3,))
    sources = (from_hbm(adjoint), from_hbm(courant), from_hbm(metric))
    gains = (from_hbm(pivot_inverse), from_hbm(lower_gain), from_hbm(upper_gain))
    ahead, *fetched = pl.pallas_call(
        edges_body,
        name="edges",
        in_specs=[in_hbm()] * 3,
        out_specs=[whole()] * 4,
        out_shape=[halo] + inputs,
        scratch_shapes=[sems, sems],
        compiler_params=params(),
    )(*sources)
    work = [
        held((6 * rows - 8, cols)),
        held((2, levels, rows, cols)),
        held(pivot_inverse.shape),
        held(lower_gain.shape),
        held(upper_gain.shape),
    ]
    low = lax.ppermute(ahead, "tile", forth)
    behind, base, adj, cour, met, *begun = pl.pallas_call(
        first_tile_body,
        name="first_tile",
        in_specs=[in_hbm()] * 6 + [whole()] * 3,
        out_specs=[whole()] * (5 + len(work)),
        out_shape=[halo, passive] + inputs + work,
        scratch_shapes=[sems, sems],
        input_output_aliases={6 + i: 2 + i for i in range(3)},
        compiler_params=params(),
    )(*sources, *gains, *fetched)
    high = lax.ppermute(behind, "tile", back)
    base, adj, cour, met, summary, active, pivot, lower, upper = pl.pallas_call(
        other_tiles_body,
        name="other_tiles",
        in_specs=[in_hbm()] * 6 + [whole()] * (4 + len(work)),
        out_specs=[whole()] * (4 + len(work)),
        out_shape=[passive] + inputs + work,
        scratch_shapes=[sems, sems],
        input_output_aliases={6 + i: i for i in range(4 + len(work))},
        compiler_params=params(),
    )(*sources, *gains, base, adj, cour, met, *begun)
    bulk = lax.ppermute(summary, "lev", swap)
    base = pl.pallas_call(
        odd_tiles_body,
        name="odd_tiles",
        in_specs=[whole()] * 3,
        out_specs=whole(),
        out_shape=passive,
        input_output_aliases={2: 0},
        compiler_params=params(),
    )(adj, cour, base)
    lowered, mine, edges, _, base = pl.pallas_call(
        sweep_body,
        name="sweep",
        in_specs=[whole()] * 7,
        out_specs=[whole()] * 5,
        out_shape=[
            held((2, levels, rows, cols)),
            held((2, rows, cols)),
            held((8, cols)),
            work[1],
            passive,
        ],
        input_output_aliases={0: 3, 6: 4},
        compiler_params=params(),
    )(active, pivot, lower, upper, low, high, base)
    got_edges = lax.ppermute(edges, "lev", swap)
    partial, _ = pl.pallas_call(
        passive_body,
        name="passive",
        in_specs=[whole()] * 5,
        out_specs=[pl.BlockSpec(memory_space=pl.ANY), whole()],
        out_shape=[
            jax.ShapeDtypeStruct(adjoint.shape, F32),
            passive,
        ],
        scratch_shapes=[sems],
        input_output_aliases={2: 1},
        compiler_params=params(),
    )(adj, cour, base, low, high)
    return pl.pallas_call(
        solve_body,
        name="solve",
        in_specs=[whole()] * 6 + [pl.BlockSpec(memory_space=pl.ANY)],
        out_specs=pl.BlockSpec(memory_space=pl.ANY),
        out_shape=jax.ShapeDtypeStruct(adjoint.shape, F32),
        scratch_shapes=[
            pltpu.VMEM((2, levels, rows, cols), F32),
            pltpu.VMEM((2, rows, cols), F32),
            pltpu.SemaphoreType.DMA((2,)),
        ],
        input_output_aliases={6: 0},
        compiler_params=params(),
    )(lowered, lower, upper, mine, bulk, got_edges, partial)


LEVEL_UNROLL = 16


def with_halo(block, sides, width):
    for axis, dim in sides:
        count = lax.axis_size(axis)
        forward = [(i, i + 1) for i in range(count - 1)]
        forward.append((count - 1, 0))
        backward = [(target, source) for source, target in forward]
        low = lax.ppermute(
            lax.slice_in_dim(block, block.shape[dim] - width, None, axis=dim), axis, forward
        )
        high = lax.ppermute(lax.slice_in_dim(block, 0, width, axis=dim), axis, backward)
        block = jnp.concatenate([low, block, high], axis=dim)
    return block


def centered_roll(values, axis_id):
    ahead_one = jnp.roll(values, -1, axis_id)
    behind_one = jnp.roll(values, 1, axis_id)
    ahead_two = jnp.roll(values, -2, axis_id)
    behind_two = jnp.roll(values, 2, axis_id)
    return (8.0 * (ahead_one - behind_one) - (ahead_two - behind_two)) / 12.0


def centered_padded(padded):
    ahead_one = padded[:, :, 3:-1, :]
    behind_one = padded[:, :, 1:-3, :]
    ahead_two = padded[:, :, 4:, :]
    behind_two = padded[:, :, :-4, :]
    return (8.0 * (ahead_one - behind_one) - (ahead_two - behind_two)) / 12.0


def mat_vec(system_matrix, vector):
    return jnp.stack(
        [
            system_matrix[0] * vector[0] + system_matrix[1] * vector[1],
            system_matrix[2] * vector[0] + system_matrix[3] * vector[1],
        ]
    )


def chain_run(coupling, forcing, initial, backward):

    def advance(state, inputs):
        fresh = mat_vec(inputs[0], state) + inputs[1]
        return (fresh, fresh)

    final_state, states = lax.scan(
        advance,
        initial,
        (jnp.moveaxis(coupling, 1, 0), jnp.moveaxis(forcing, 1, 0)),
        reverse=backward,
        unroll=min(LEVEL_UNROLL, coupling.shape[1]),
    )
    return jnp.moveaxis(states, 0, 1)


def column_solve(pieces):
    forcing, lower_part, upper_part = pieces
    initial = jnp.zeros((2,) + forcing.shape[2:], jnp.float32)
    lowered = chain_run(lower_part, forcing, initial, False)
    solved = chain_run(upper_part, lowered, initial, True)
    return lax.all_to_all(solved, "lev", split_axis=1, concat_axis=2, tiled=True)


def local_any(adjoint, courant, metric, pivot_inverse, lower_gain, upper_gain):
    weighted = jnp.concatenate([courant[0] * adjoint, (metric[0] * adjoint[0])[None]], 0)
    padded = with_halo(weighted, (("tile", 2),), 2)
    across = centered_padded(padded)
    advected = adjoint + across[:5] + centered_roll(courant[1] * adjoint, 3)
    pressure_field = advected[4] + across[5] + centered_roll(metric[1] * adjoint[1], 2)
    forcing = mat_vec(pivot_inverse, jnp.stack([advected[2], pressure_field]))
    solved = column_solve(
        (
            lax.all_to_all(forcing, "lev", split_axis=2, concat_axis=1, tiled=True),
            lax.all_to_all(lower_gain, "lev", split_axis=2, concat_axis=1, tiled=True),
            lax.all_to_all(upper_gain, "lev", split_axis=2, concat_axis=1, tiled=True),
        )
    )
    return jnp.stack([advected[0], advected[1], solved[0], advected[3], solved[1]])


def solution(mesh):
    placed = (P(None, "lev", "tile", None),) * 6
    pair = mesh.shape["lev"] == 2 and mesh.shape["tile"] % 2 == 0

    def local(adjoint, *others):
        levels, rows = adjoint.shape[1:3]
        fits = pair and levels % EDGE_LEVELS == 0 and rows % 8 == 0 and rows > 8
        return (local_pair if fits else local_any)(adjoint, *others)

    return jax.shard_map(
        local,
        mesh=mesh,
        in_specs=placed,
        out_specs=P(None, "lev", "tile", None),
        check_vma=False,
    )
```

```python
import jax
import jax.numpy as jnp
from jax import lax
from jax.experimental import pallas as pl
from jax.experimental.pallas import tpu as pltpu
from jax.sharding import PartitionSpec as P

F32 = jnp.float32
VMEM_LIMIT = 24 * 1024 * 1024
EDGE_LEVELS = 8


def held(shape):
    return pltpu.VMEM(shape, F32)


def whole():
    return pl.BlockSpec(memory_space=pltpu.VMEM)


def in_hbm():
    return pl.BlockSpec(memory_space=pltpu.HBM)


def from_hbm(x):
    return pltpu.with_memory_space_constraint(x, pltpu.HBM)


def params():
    return pltpu.CompilerParams(vmem_limit_bytes=VMEM_LIMIT)


def mul(m, v):
    return (m[0] * v[0] + m[1] * v[1], m[2] * v[0] + m[3] * v[1])


def matmul(m, n):
    return (
        m[0] * n[0] + m[1] * n[2],
        m[0] * n[1] + m[1] * n[3],
        m[2] * n[0] + m[3] * n[2],
        m[2] * n[1] + m[3] * n[3],
    )


def add(a, b):
    return tuple(x + y for x, y in zip(a, b, strict=True))


def at(ref, level):
    return tuple(ref[k, level] for k in range(ref.shape[0]))


def emit_edges(adj, courant, metric, out, first):
    for r in range(2):
        row = first + r
        wind = courant[0, :, row, :]
        for k in range(4):
            out[k, r] = wind * adj[k, :, row, :]
        out[4, r] = wind * adj[4, :, row, :] + metric[0, :, row, :] * adj[0, :, row, :]


def fetch_all(sources, targets, sems, levels_each=2):
    levels_each = min(levels_each, sources[0].shape[1])
    for i, (source, target) in enumerate(zip(sources, targets, strict=True)):
        parts = source.shape[1] // levels_each

        def start(n, _, i=i, source=source, target=target, parts=parts):
            k, span = n // parts, pl.ds(lax.rem(n, parts) * levels_each, levels_each)
            pltpu.make_async_copy(
                source.at[k, span], target.at[k, span], sems.at[i]
            ).start()
            return 0

        lax.fori_loop(0, source.shape[0] * parts, start, 0)


def wait_all(sources, targets, sems):
    for i, (source, target) in enumerate(zip(sources, targets, strict=True)):
        pltpu.make_async_copy(source, target, sems.at[i]).wait()


def rows_of(refs, first):
    return [ref.at[:, :, pl.ds(first, 2)] for ref in refs]


def is_first_tile():
    return lax.axis_index("tile") == 0


def is_first_chip(tile):
    return jnp.logical_and(lax.axis_index("tile") == tile, lax.axis_index("lev") == 0)


def is_last_tile():
    return lax.axis_index("tile") == lax.axis_size("tile") - 1


def edges_body(
    adj_in, courant_in, metric_in, ahead, adj, courant, metric, sems, head_sems
):
    given, targets = (adj_in, courant_in, metric_in), (adj, courant, metric)
    plane = pl.ds(0, 1)
    sent_in = (courant_in.at[plane], metric_in.at[plane], adj_in)
    sent = (courant.at[plane], metric.at[plane], adj)
    rows = adj.shape[2]
    first, last = is_first_tile(), is_last_tile()
    end = jnp.logical_or(first, last)

    tails = (rows_of(sent_in, rows - 2), rows_of(sent, rows - 2), sems)
    heads = (rows_of(sent_in, 0), rows_of(sent, 0), head_sems)

    @pl.when(end)
    def _():
        fetch_all(*tails, EDGE_LEVELS)

        @pl.when(last)
        def _():
            fetch_all(*heads, EDGE_LEVELS)

        wait_all(*tails)

    @pl.when(jnp.logical_not(end))
    def _():
        fetch_all(given, targets, sems)
        wait_all(given, targets, sems)

    emit_edges(adj, courant, metric, ahead, rows - 2)

    @pl.when(last)
    def _():
        wait_all(*heads)


def across(q):
    rows = q.shape[0]
    spot = lax.broadcasted_iota(jnp.int32, q.shape, 0)
    out = None
    for step, weight in ((1, 8.0 / 12.0), (2, -1.0 / 12.0)):
        ahead = jnp.where(spot < rows - step, pltpu.roll(q, rows - step, 0), 0.0)
        behind = jnp.where(spot >= step, pltpu.roll(q, step, 0), 0.0)
        term = weight * (ahead - behind)
        out = term if out is None else out + term
    return out


def along(q):
    cols = q.shape[1]
    near = pltpu.roll(q, cols - 1, 1) - pltpu.roll(q, 1, 1)
    wide = pltpu.roll(q, cols - 2, 1) - pltpu.roll(q, 2, 1)
    return (8.0 / 12.0) * near - (1.0 / 12.0) * wide


def passive_base(adj, courant, passive):
    def one(l, _):
        c0, c1 = courant[0, l], courant[1, l]
        for slot, field in ((0, 0), (1, 1), (2, 3)):
            x = adj[field, l]
            passive[slot, l] = x + across(c0 * x) + along(c1 * x)
        return 0

    lax.fori_loop(0, adj.shape[1], one, 0)


def first_tile_body(adj_in, courant_in, metric_in, pivot_in, lower_in, upper_in, *refs):
    behind, passive, adj, courant, metric, *work = refs[3:-2]
    sems, gain_sems = refs[-2:]

    @pl.when(is_first_tile())
    def _():
        fields = ((adj_in, courant_in, metric_in), (adj, courant, metric), sems)
        gains = ((pivot_in, lower_in, upper_in), work[-3:], gain_sems)
        fetch_all(*fields)
        fetch_all(*gains)
        wait_all(*fields)
        active_base(adj, courant, metric, work[1])
        summarise(work, gains)

    @pl.when(is_first_chip(0))
    def _():
        passive_base(adj, courant, passive)

    emit_edges(adj, courant, metric, behind, 0)


def other_tiles_body(adj_in, courant_in, metric_in, pivot_in, lower_in, upper_in, *refs):
    passive, adj, courant, metric, *work = refs[-11:-2]
    sems, gain_sems = refs[-2:]

    @pl.when(is_first_chip(1))
    def _():
        passive_base(adj, courant, passive)

    @pl.when(jnp.logical_not(is_first_tile()))
    def _():
        last = is_last_tile()
        fields = ((adj_in, courant_in, metric_in), (adj, courant, metric), sems)
        gains = ((pivot_in, lower_in, upper_in), work[-3:], gain_sems)

        @pl.when(last)
        def _():
            fetch_all(*fields)

        fetch_all(*gains)

        @pl.when(last)
        def _():
            wait_all(*fields)

        active_base(adj, courant, metric, work[1])
        summarise(work, gains)


def active_base(adj, courant, metric, active):
    def one(l, _):
        c0, c1 = courant[0, l], courant[1, l]
        x = adj[2, l]
        active[0, l] = x + across(c0 * x) + along(c1 * x)
        x = adj[4, l]
        active[1, l] = (
            x
            + across(c0 * x + metric[0, l] * adj[0, l])
            + along(c1 * x + metric[1, l] * adj[1, l])
        )
        return 0

    lax.fori_loop(0, adj.shape[1], one, 0)


def summarise(work, gains):
    bulk, active, pivot, lower, upper = work
    levels = active.shape[1]
    wait_all(*gains)
    states = forward(active, pivot, lower)

    rows = active.shape[2]

    def emit(state):
        for k in range(2):
            start = 4 * rows + k * (rows - 4)
            bulk[pl.ds(start, rows - 4)] = state[k][2 : rows - 2]

    @pl.when(lax.axis_index("lev") == 0)
    def _():
        emit(states[-1])

    @pl.when(lax.axis_index("lev") == 1)
    def _():
        emit(backward_first(states, upper))
        chain = [at(lower, 0)]
        for l in range(1, levels):
            chain.append(matmul(at(lower, l), chain[-1]))
        total = chain[-1]
        for l in range(levels - 2, -1, -1):
            total = add(matmul(at(upper, l), total), chain[l])
        for k in range(4):
            bulk[pl.ds(k * rows, rows)] = total[k]


def forward(active, pivot, lower):
    states = []
    for l in range(active.shape[1]):
        fresh = mul(at(pivot, l), at(active, l))
        if states:
            fresh = add(mul(at(lower, l), states[-1]), fresh)
        states.append(fresh)
    return states


def backward_first(states, upper):
    state = states[-1]
    for l in range(len(states) - 2, -1, -1):
        state = add(mul(at(upper, l), state), states[l])
    return state


def add_halo(ref, slot, low, high):
    rows = ref.shape[2]
    near, wide = 8.0 / 12.0, 1.0 / 12.0
    ref[slot, :, 0, :] = ref[slot, :, 0, :] + (wide * low[0] - near * low[1])
    ref[slot, :, 1, :] = ref[slot, :, 1, :] + wide * low[1]
    ref[slot, :, rows - 2, :] = ref[slot, :, rows - 2, :] - wide * high[0]
    ref[slot, :, rows - 1, :] = ref[slot, :, rows - 1, :] + (
        near * high[0] - wide * high[1]
    )


def halo_rows(low, high, field):
    return [[ref[field, r] for r in range(2)] for ref in (low, high)]


def sweep_body(given, pivot, lower, upper, low, high, base, lowered, mine, edges, active, kept):
    del given, base, kept
    levels, rows = active.shape[1:3]
    for slot, field in ((0, 2), (1, 4)):
        add_halo(active, slot, *halo_rows(low, high, field))
    states = forward(active, pivot, lower)
    for l in range(levels):
        for k in range(2):
            lowered[k, l] = states[l][k]

    def emit(state):
        for k in range(2):
            mine[k] = state[k]
            edges[pl.ds(4 * k, 2)] = state[k][:2]
            edges[pl.ds(4 * k + 2, 2)] = state[k][rows - 2 :]

    @pl.when(lax.axis_index("lev") == 0)
    def _():
        emit(states[-1])

    @pl.when(lax.axis_index("lev") == 1)
    def _():
        emit(backward_first(states, upper))


def odd_tiles_body(adj, courant, base, passive):
    del base

    odd = lax.rem(lax.axis_index("tile"), 2) == 1

    @pl.when(jnp.logical_and(odd, jnp.logical_not(is_first_chip(1))))
    def _():
        passive_base(adj, courant, passive)


def passive_body(adj, courant, base, low, high, out, passive, sems):
    del base

    even = lax.rem(lax.axis_index("tile"), 2) == 0

    @pl.when(jnp.logical_and(even, jnp.logical_not(is_first_chip(0))))
    def _():
        passive_base(adj, courant, passive)

    copies = []
    for slot, field in enumerate((0, 1, 3)):
        add_halo(passive, slot, *halo_rows(low, high, field))
        copies.append(
            pltpu.make_async_copy(passive.at[slot], out.at[field], sems.at[slot])
        )
        copies[-1].start()
    for copy in copies:
        copy.wait()


def solve_body(
    lowered, lower, upper, mine, bulk, edges, partial, out, solved, other, sems
):
    del partial
    levels, rows = lowered.shape[1:3]
    for k in range(2):
        other[k, pl.ds(0, 2)] = edges[pl.ds(4 * k, 2)]
        other[k, pl.ds(2, rows - 4)] = bulk[pl.ds(4 * rows + k * (rows - 4), rows - 4)]
        other[k, pl.ds(rows - 2, 2)] = edges[pl.ds(4 * k + 2, 2)]

    half = levels // 2

    def descend(state, full):
        for l in range(levels - 1, -1, -1):
            if state is None:
                state = full(l)
            else:
                state = add(mul(at(upper, l), state), full(l))
            for k, field in ((0, 2), (1, 4)):
                solved[k, l] = state[k]
                if l % half == 0:
                    part = pl.ds(l, half)
                    pltpu.make_async_copy(
                        solved.at[k, part], out.at[field, part], sems.at[k]
                    ).start()

    @pl.when(lax.axis_index("lev") == 0)
    def _():
        gain = tuple(bulk[pl.ds(k * rows, rows)] for k in range(4))
        descend(
            add(mul(gain, (mine[0], mine[1])), (other[0], other[1])),
            lambda l: at(lowered, l),
        )

    @pl.when(lax.axis_index("lev") == 1)
    def _():
        entering = (other[0], other[1])
        full = []
        for l in range(levels):
            entering = mul(at(lower, l), entering)
            full.append(add(entering, at(lowered, l)))
        descend(None, lambda l: full[l])

    for k, field in ((0, 2), (1, 4)):
        pltpu.make_async_copy(solved.at[k], out.at[field], sems.at[k]).wait()


def local_pair(adjoint, courant, metric, pivot_inverse, lower_gain, upper_gain):
    fields, levels, rows, cols = adjoint.shape
    tiles = lax.axis_size("tile")
    swap = [(0, 1), (1, 0)]
    forth = [(i, (i + 1) % tiles) for i in range(tiles)]
    back = [(i, (i - 1) % tiles) for i in range(tiles)]
    halo = held((fields, 2, levels, cols))
    passive = held((3, levels, rows, cols))
    inputs = [held(adjoint.shape), held(courant.shape), held(metric.shape)]
    sems = pltpu.SemaphoreType.DMA((3,))
    sources = (from_hbm(adjoint), from_hbm(courant), from_hbm(metric))
    gains = (from_hbm(pivot_inverse), from_hbm(lower_gain), from_hbm(upper_gain))
    ahead, *fetched = pl.pallas_call(
        edges_body,
        name="edges",
        in_specs=[in_hbm()] * 3,
        out_specs=[whole()] * 4,
        out_shape=[halo] + inputs,
        scratch_shapes=[sems, sems],
        compiler_params=params(),
    )(*sources)
    work = [
        held((6 * rows - 8, cols)),
        held((2, levels, rows, cols)),
        held(pivot_inverse.shape),
        held(lower_gain.shape),
        held(upper_gain.shape),
    ]
    low = lax.ppermute(ahead, "tile", forth)
    behind, base, adj, cour, met, *begun = pl.pallas_call(
        first_tile_body,
        name="first_tile",
        in_specs=[in_hbm()] * 6 + [whole()] * 3,
        out_specs=[whole()] * (5 + len(work)),
        out_shape=[halo, passive] + inputs + work,
        scratch_shapes=[sems, sems],
        input_output_aliases={6 + i: 2 + i for i in range(3)},
        compiler_params=params(),
    )(*sources, *gains, *fetched)
    high = lax.ppermute(behind, "tile", back)
    base, adj, cour, met, summary, active, pivot, lower, upper = pl.pallas_call(
        other_tiles_body,
        name="other_tiles",
        in_specs=[in_hbm()] * 6 + [whole()] * (4 + len(work)),
        out_specs=[whole()] * (4 + len(work)),
        out_shape=[passive] + inputs + work,
        scratch_shapes=[sems, sems],
        input_output_aliases={6 + i: i for i in range(4 + len(work))},
        compiler_params=params(),
    )(*sources, *gains, base, adj, cour, met, *begun)
    bulk = lax.ppermute(summary, "lev", swap)
    base = pl.pallas_call(
        odd_tiles_body,
        name="odd_tiles",
        in_specs=[whole()] * 3,
        out_specs=whole(),
        out_shape=passive,
        input_output_aliases={2: 0},
        compiler_params=params(),
    )(adj, cour, base)
    lowered, mine, edges, _, base = pl.pallas_call(
        sweep_body,
        name="sweep",
        in_specs=[whole()] * 7,
        out_specs=[whole()] * 5,
        out_shape=[
            held((2, levels, rows, cols)),
            held((2, rows, cols)),
            held((8, cols)),
            work[1],
            passive,
        ],
        input_output_aliases={0: 3, 6: 4},
        compiler_params=params(),
    )(active, pivot, lower, upper, low, high, base)
    got_edges = lax.ppermute(edges, "lev", swap)
    partial, _ = pl.pallas_call(
        passive_body,
        name="passive",
        in_specs=[whole()] * 5,
        out_specs=[pl.BlockSpec(memory_space=pl.ANY), whole()],
        out_shape=[
            jax.ShapeDtypeStruct(adjoint.shape, F32),
            passive,
        ],
        scratch_shapes=[sems],
        input_output_aliases={2: 1},
        compiler_params=params(),
    )(adj, cour, base, low, high)
    return pl.pallas_call(
        solve_body,
        name="solve",
        in_specs=[whole()] * 6 + [pl.BlockSpec(memory_space=pl.ANY)],
        out_specs=pl.BlockSpec(memory_space=pl.ANY),
        out_shape=jax.ShapeDtypeStruct(adjoint.shape, F32),
        scratch_shapes=[
            pltpu.VMEM((2, levels, rows, cols), F32),
            pltpu.VMEM((2, rows, cols), F32),
            pltpu.SemaphoreType.DMA((2,)),
        ],
        input_output_aliases={6: 0},
        compiler_params=params(),
    )(lowered, lower, upper, mine, bulk, got_edges, partial)


LEVEL_UNROLL = 16


def with_halo(block, sides, width):
    for axis, dim in sides:
        count = lax.axis_size(axis)
        forward = [(i, i + 1) for i in range(count - 1)]
        forward.append((count - 1, 0))
        backward = [(target, source) for source, target in forward]
        low = lax.ppermute(
            lax.slice_in_dim(block, block.shape[dim] - width, None, axis=dim), axis, forward
        )
        high = lax.ppermute(lax.slice_in_dim(block, 0, width, axis=dim), axis, backward)
        block = jnp.concatenate([low, block, high], axis=dim)
    return block


def centered_roll(values, axis_id):
    ahead_one = jnp.roll(values, -1, axis_id)
    behind_one = jnp.roll(values, 1, axis_id)
    ahead_two = jnp.roll(values, -2, axis_id)
    behind_two = jnp.roll(values, 2, axis_id)
    return (8.0 * (ahead_one - behind_one) - (ahead_two - behind_two)) / 12.0


def centered_padded(padded):
    ahead_one = padded[:, :, 3:-1, :]
    behind_one = padded[:, :, 1:-3, :]
    ahead_two = padded[:, :, 4:, :]
    behind_two = padded[:, :, :-4, :]
    return (8.0 * (ahead_one - behind_one) - (ahead_two - behind_two)) / 12.0


def mat_vec(system_matrix, vector):
    return jnp.stack(
        [
            system_matrix[0] * vector[0] + system_matrix[1] * vector[1],
            system_matrix[2] * vector[0] + system_matrix[3] * vector[1],
        ]
    )


def chain_run(coupling, forcing, initial, backward):

    def advance(state, inputs):
        fresh = mat_vec(inputs[0], state) + inputs[1]
        return (fresh, fresh)

    final_state, states = lax.scan(
        advance,
        initial,
        (jnp.moveaxis(coupling, 1, 0), jnp.moveaxis(forcing, 1, 0)),
        reverse=backward,
        unroll=min(LEVEL_UNROLL, coupling.shape[1]),
    )
    return jnp.moveaxis(states, 0, 1)


def column_solve(pieces):
    forcing, lower_part, upper_part = pieces
    initial = jnp.zeros((2,) + forcing.shape[2:], jnp.float32)
    lowered = chain_run(lower_part, forcing, initial, False)
    solved = chain_run(upper_part, lowered, initial, True)
    return lax.all_to_all(solved, "lev", split_axis=1, concat_axis=2, tiled=True)


def local_any(adjoint, courant, metric, pivot_inverse, lower_gain, upper_gain):
    weighted = jnp.concatenate([courant[0] * adjoint, (metric[0] * adjoint[0])[None]], 0)
    padded = with_halo(weighted, (("tile", 2),), 2)
    across = centered_padded(padded)
    advected = adjoint + across[:5] + centered_roll(courant[1] * adjoint, 3)
    pressure_field = advected[4] + across[5] + centered_roll(metric[1] * adjoint[1], 2)
    forcing = mat_vec(pivot_inverse, jnp.stack([advected[2], pressure_field]))
    solved = column_solve(
        (
            lax.all_to_all(forcing, "lev", split_axis=2, concat_axis=1, tiled=True),
            lax.all_to_all(lower_gain, "lev", split_axis=2, concat_axis=1, tiled=True),
            lax.all_to_all(upper_gain, "lev", split_axis=2, concat_axis=1, tiled=True),
        )
    )
    return jnp.stack([advected[0], advected[1], solved[0], advected[3], solved[1]])


def solution(mesh):
    placed = (P(None, "lev", "tile", None),) * 6
    pair = mesh.shape["lev"] == 2 and mesh.shape["tile"] % 2 == 0

    def local(adjoint, *others):
        levels, rows = adjoint.shape[1:3]
        fits = pair and levels % EDGE_LEVELS == 0 and rows % 8 == 0 and rows > 8
        return (local_pair if fits else local_any)(adjoint, *others)

    return jax.shard_map(
        local,
        mesh=mesh,
        in_specs=placed,
        out_specs=P(None, "lev", "tile", None),
        check_vma=False,
    )
```

```python
import jax
import jax.numpy as jnp
from jax import lax
from jax.experimental import pallas as pl
from jax.experimental.pallas import tpu as pltpu
from jax.sharding import PartitionSpec as P

F32 = jnp.float32
VMEM_LIMIT = 24 * 1024 * 1024
EDGE_LEVELS = 8


def held(shape):
    return pltpu.VMEM(shape, F32)


def whole():
    return pl.BlockSpec(memory_space=pltpu.VMEM)


def in_hbm():
    return pl.BlockSpec(memory_space=pltpu.HBM)


def from_hbm(x):
    return pltpu.with_memory_space_constraint(x, pltpu.HBM)


def params():
    return pltpu.CompilerParams(vmem_limit_bytes=VMEM_LIMIT)


def mul(m, v):
    return (m[0] * v[0] + m[1] * v[1], m[2] * v[0] + m[3] * v[1])


def matmul(m, n):
    return (
        m[0] * n[0] + m[1] * n[2],
        m[0] * n[1] + m[1] * n[3],
        m[2] * n[0] + m[3] * n[2],
        m[2] * n[1] + m[3] * n[3],
    )


def add(a, b):
    return tuple(x + y for x, y in zip(a, b, strict=True))


def at(ref, level):
    return tuple(ref[k, level] for k in range(ref.shape[0]))


def emit_edges(adj, courant, metric, out, first):
    for r in range(2):
        row = first + r
        wind = courant[0, :, row, :]
        for k in range(4):
            out[k, r] = wind * adj[k, :, row, :]
        out[4, r] = wind * adj[4, :, row, :] + metric[0, :, row, :] * adj[0, :, row, :]


def fetch_all(sources, targets, sems, levels_each=2):
    levels_each = min(levels_each, sources[0].shape[1])
    for i, (source, target) in enumerate(zip(sources, targets, strict=True)):
        parts = source.shape[1] // levels_each

        def start(n, _, i=i, source=source, target=target, parts=parts):
            k, span = n // parts, pl.ds(lax.rem(n, parts) * levels_each, levels_each)
            pltpu.make_async_copy(
                source.at[k, span], target.at[k, span], sems.at[i]
            ).start()
            return 0

        lax.fori_loop(0, source.shape[0] * parts, start, 0)


def wait_all(sources, targets, sems):
    for i, (source, target) in enumerate(zip(sources, targets, strict=True)):
        pltpu.make_async_copy(source, target, sems.at[i]).wait()


def rows_of(refs, first):
    return [ref.at[:, :, pl.ds(first, 2)] for ref in refs]


def is_first_tile():
    return lax.axis_index("tile") == 0


def is_first_chip(tile):
    return jnp.logical_and(lax.axis_index("tile") == tile, lax.axis_index("lev") == 0)


def is_last_tile():
    return lax.axis_index("tile") == lax.axis_size("tile") - 1


def edges_body(
    adj_in, courant_in, metric_in, ahead, adj, courant, metric, sems, head_sems
):
    given, targets = (adj_in, courant_in, metric_in), (adj, courant, metric)
    plane = pl.ds(0, 1)
    sent_in = (courant_in.at[plane], metric_in.at[plane], adj_in)
    sent = (courant.at[plane], metric.at[plane], adj)
    rows = adj.shape[2]
    first, last = is_first_tile(), is_last_tile()
    end = jnp.logical_or(first, last)

    tails = (rows_of(sent_in, rows - 2), rows_of(sent, rows - 2), sems)
    heads = (rows_of(sent_in, 0), rows_of(sent, 0), head_sems)

    @pl.when(end)
    def _():
        fetch_all(*tails, EDGE_LEVELS)

        @pl.when(last)
        def _():
            fetch_all(*heads, EDGE_LEVELS)

        wait_all(*tails)

    @pl.when(jnp.logical_not(end))
    def _():
        fetch_all(given, targets, sems)
        wait_all(given, targets, sems)

    emit_edges(adj, courant, metric, ahead, rows - 2)

    @pl.when(last)
    def _():
        wait_all(*heads)


def across(q):
    rows = q.shape[0]
    spot = lax.broadcasted_iota(jnp.int32, q.shape, 0)
    out = None
    for step, weight in ((1, 8.0 / 12.0), (2, -1.0 / 12.0)):
        ahead = jnp.where(spot < rows - step, pltpu.roll(q, rows - step, 0), 0.0)
        behind = jnp.where(spot >= step, pltpu.roll(q, step, 0), 0.0)
        term = weight * (ahead - behind)
        out = term if out is None else out + term
    return out


def along(q):
    cols = q.shape[1]
    near = pltpu.roll(q, cols - 1, 1) - pltpu.roll(q, 1, 1)
    wide = pltpu.roll(q, cols - 2, 1) - pltpu.roll(q, 2, 1)
    return (8.0 / 12.0) * near - (1.0 / 12.0) * wide


def passive_base(adj, courant, passive):
    def one(l, _):
        c0, c1 = courant[0, l], courant[1, l]
        for slot, field in ((0, 0), (1, 1), (2, 3)):
            x = adj[field, l]
            passive[slot, l] = x + across(c0 * x) + along(c1 * x)
        return 0

    lax.fori_loop(0, adj.shape[1], one, 0)


def first_tile_body(adj_in, courant_in, metric_in, pivot_in, lower_in, upper_in, *refs):
    behind, passive, adj, courant, metric, *work = refs[3:-2]
    sems, gain_sems = refs[-2:]

    @pl.when(is_first_tile())
    def _():
        fields = ((adj_in, courant_in, metric_in), (adj, courant, metric), sems)
        gains = ((pivot_in, lower_in, upper_in), work[-3:], gain_sems)
        fetch_all(*fields)
        fetch_all(*gains)
        wait_all(*fields)
        active_base(adj, courant, metric, work[1])
        summarise(work, gains)

    @pl.when(is_first_chip(0))
    def _():
        passive_base(adj, courant, passive)

    emit_edges(adj, courant, metric, behind, 0)


def other_tiles_body(adj_in, courant_in, metric_in, pivot_in, lower_in, upper_in, *refs):
    passive, adj, courant, metric, *work = refs[-13:-2]
    sems, gain_sems = refs[-2:]

    @pl.when(is_first_chip(1))
    def _():
        passive_base(adj, courant, passive)

    @pl.when(jnp.logical_not(is_first_tile()))
    def _():
        last = is_last_tile()
        fields = ((adj_in, courant_in, metric_in), (adj, courant, metric), sems)
        gains = ((pivot_in, lower_in, upper_in), work[-3:], gain_sems)

        @pl.when(last)
        def _():
            fetch_all(*fields)

        fetch_all(*gains)

        @pl.when(last)
        def _():
            wait_all(*fields)

        active_base(adj, courant, metric, work[1])
        summarise(work, gains)


def active_base(adj, courant, metric, active):
    def one(l, _):
        c0, c1 = courant[0, l], courant[1, l]
        x = adj[2, l]
        active[0, l] = x + across(c0 * x) + along(c1 * x)
        x = adj[4, l]
        active[1, l] = (
            x
            + across(c0 * x + metric[0, l] * adj[0, l])
            + along(c1 * x + metric[1, l] * adj[1, l])
        )
        return 0

    lax.fori_loop(0, adj.shape[1], one, 0)


def summarise(work, gains):
    bulk, active, response, ends, pivot, lower, upper = work
    levels, rows = active.shape[1:3]
    wait_all(*gains)
    states = forward(active, pivot, lower)
    one, none = jnp.ones_like(states[0][0]), jnp.zeros_like(states[0][0])
    identity = (one, none, none, one)

    def emit(state):
        for k in range(2):
            ends[k] = state[k]
            start = 4 * rows + k * (rows - 4)
            bulk[pl.ds(start, rows - 4)] = state[k][2 : rows - 2]

    def respond(l, reach):
        gain = matmul(reach, at(pivot, l))
        for k in range(4):
            for i, row in enumerate(edge_rows(rows)):
                response[k, i, pl.ds(l, 1)] = gain[k][row : row + 1]

    @pl.when(lax.axis_index("lev") == 0)
    def _():
        emit(states[-1])
        reach = identity
        for l in range(levels - 1, -1, -1):
            if l < levels - 1:
                reach = matmul(reach, at(lower, l + 1))
            respond(l, reach)

    @pl.when(lax.axis_index("lev") == 1)
    def _():
        emit(backward_first(states, upper))
        chain = [identity]
        for l in range(levels - 1):
            chain.append(matmul(chain[-1], at(upper, l)))
        reach = chain[-1]
        for l in range(levels - 1, -1, -1):
            if l < levels - 1:
                reach = add(chain[l], matmul(reach, at(lower, l + 1)))
            respond(l, reach)
        total = matmul(reach, at(lower, 0))
        for k in range(4):
            bulk[pl.ds(k * rows, rows)] = total[k]


def edge_rows(rows):
    return (0, 1, rows - 2, rows - 1)


def forward(active, pivot, lower):
    states = []
    for l in range(active.shape[1]):
        fresh = mul(at(pivot, l), at(active, l))
        if states:
            fresh = add(mul(at(lower, l), states[-1]), fresh)
        states.append(fresh)
    return states


def backward_first(states, upper):
    state = states[-1]
    for l in range(len(states) - 2, -1, -1):
        state = add(mul(at(upper, l), state), states[l])
    return state


def halo_parts(low, high):
    near, wide = 8.0 / 12.0, 1.0 / 12.0
    return (
        wide * low[0] - near * low[1],
        wide * low[1],
        -wide * high[0],
        near * high[0] - wide * high[1],
    )


def add_halo(ref, slot, low, high):
    parts = halo_parts(low, high)
    for part, row in zip(parts, edge_rows(ref.shape[2]), strict=True):
        ref[slot, :, row, :] = ref[slot, :, row, :] + part


def halo_rows(low, high, field):
    return [[ref[field, r] for r in range(2)] for ref in (low, high)]


def couple_body(low, high, response, ends, base, edges, kept):
    del base, kept
    rows = ends.shape[1]
    parts = [halo_parts(*halo_rows(low, high, field)) for field in (2, 4)]
    for i, row in enumerate(edge_rows(rows)):
        for k in range(2):
            change = (
                response[2 * k, i] * parts[0][i] + response[2 * k + 1, i] * parts[1][i]
            )
            edges[pl.ds(4 * k + i, 1)] = ends[k, pl.ds(row, 1)] + jnp.sum(
                change, axis=0, keepdims=True
            )


def sweep(active, pivot, lower, low, high, lowered, mine):
    for slot, field in ((0, 2), (1, 4)):
        add_halo(active, slot, *halo_rows(low, high, field))
    states = forward(active, pivot, lower)
    for k in range(2):
        for l in range(active.shape[1]):
            lowered[k, l] = states[l][k]
        mine[k] = states[-1][k]


def odd_tiles_body(adj, courant, base, passive):
    del base

    odd = lax.rem(lax.axis_index("tile"), 2) == 1

    @pl.when(jnp.logical_and(odd, jnp.logical_not(is_first_chip(1))))
    def _():
        passive_base(adj, courant, passive)


def passive_body(
    adj, courant, pivot, lower, low, high, base, given,
    out, lowered, mine, passive, active, sems,
):
    del base, given

    even = lax.rem(lax.axis_index("tile"), 2) == 0

    @pl.when(jnp.logical_and(even, jnp.logical_not(is_first_chip(0))))
    def _():
        passive_base(adj, courant, passive)

    copies = []
    for slot, field in enumerate((0, 1, 3)):
        add_halo(passive, slot, *halo_rows(low, high, field))
        copies.append(
            pltpu.make_async_copy(passive.at[slot], out.at[field], sems.at[slot])
        )
        copies[-1].start()
    sweep(active, pivot, lower, low, high, lowered, mine)
    for copy in copies:
        copy.wait()


def solve_body(
    lowered, lower, upper, mine, bulk, edges, partial, out, solved, other, sems
):
    del partial
    levels, rows = lowered.shape[1:3]
    for k in range(2):
        other[k, pl.ds(0, 2)] = edges[pl.ds(4 * k, 2)]
        other[k, pl.ds(2, rows - 4)] = bulk[pl.ds(4 * rows + k * (rows - 4), rows - 4)]
        other[k, pl.ds(rows - 2, 2)] = edges[pl.ds(4 * k + 2, 2)]

    half = levels // 2

    def descend(state, full):
        for l in range(levels - 1, -1, -1):
            if state is None:
                state = full(l)
            else:
                state = add(mul(at(upper, l), state), full(l))
            for k, field in ((0, 2), (1, 4)):
                solved[k, l] = state[k]
                if l % half == 0:
                    part = pl.ds(l, half)
                    pltpu.make_async_copy(
                        solved.at[k, part], out.at[field, part], sems.at[k]
                    ).start()

    @pl.when(lax.axis_index("lev") == 0)
    def _():
        gain = tuple(bulk[pl.ds(k * rows, rows)] for k in range(4))
        descend(
            add(mul(gain, (mine[0], mine[1])), (other[0], other[1])),
            lambda l: at(lowered, l),
        )

    @pl.when(lax.axis_index("lev") == 1)
    def _():
        entering = (other[0], other[1])
        full = []
        for l in range(levels):
            entering = mul(at(lower, l), entering)
            full.append(add(entering, at(lowered, l)))
        descend(None, lambda l: full[l])

    for k, field in ((0, 2), (1, 4)):
        pltpu.make_async_copy(solved.at[k], out.at[field], sems.at[k]).wait()


def local_pair(adjoint, courant, metric, pivot_inverse, lower_gain, upper_gain):
    fields, levels, rows, cols = adjoint.shape
    tiles = lax.axis_size("tile")
    swap = [(0, 1), (1, 0)]
    forth = [(i, (i + 1) % tiles) for i in range(tiles)]
    back = [(i, (i - 1) % tiles) for i in range(tiles)]
    halo = held((fields, 2, levels, cols))
    passive = held((3, levels, rows, cols))
    inputs = [held(adjoint.shape), held(courant.shape), held(metric.shape)]
    sems = pltpu.SemaphoreType.DMA((3,))
    sources = (from_hbm(adjoint), from_hbm(courant), from_hbm(metric))
    gains = (from_hbm(pivot_inverse), from_hbm(lower_gain), from_hbm(upper_gain))
    ahead, *fetched = pl.pallas_call(
        edges_body,
        name="edges",
        in_specs=[in_hbm()] * 3,
        out_specs=[whole()] * 4,
        out_shape=[halo] + inputs,
        scratch_shapes=[sems, sems],
        compiler_params=params(),
    )(*sources)
    work = [
        held((6 * rows - 8, cols)),
        held((2, levels, rows, cols)),
        held((4, 4, levels, cols)),
        held((2, rows, cols)),
        held(pivot_inverse.shape),
        held(lower_gain.shape),
        held(upper_gain.shape),
    ]
    low = lax.ppermute(ahead, "tile", forth)
    behind, base, adj, cour, met, *begun = pl.pallas_call(
        first_tile_body,
        name="first_tile",
        in_specs=[in_hbm()] * 6 + [whole()] * 3,
        out_specs=[whole()] * (5 + len(work)),
        out_shape=[halo, passive] + inputs + work,
        scratch_shapes=[sems, sems],
        input_output_aliases={6 + i: 2 + i for i in range(3)},
        compiler_params=params(),
    )(*sources, *gains, *fetched)
    high = lax.ppermute(behind, "tile", back)
    base, adj, cour, met, summary, active, response, ends, pivot, lower, upper = pl.pallas_call(
        other_tiles_body,
        name="other_tiles",
        in_specs=[in_hbm()] * 6 + [whole()] * (4 + len(work)),
        out_specs=[whole()] * (4 + len(work)),
        out_shape=[passive] + inputs + work,
        scratch_shapes=[sems, sems],
        input_output_aliases={6 + i: i for i in range(4 + len(work))},
        compiler_params=params(),
    )(*sources, *gains, base, adj, cour, met, *begun)
    bulk = lax.ppermute(summary, "lev", swap)
    base = pl.pallas_call(
        odd_tiles_body,
        name="odd_tiles",
        in_specs=[whole()] * 3,
        out_specs=whole(),
        out_shape=passive,
        input_output_aliases={2: 0},
        compiler_params=params(),
    )(adj, cour, base)
    edges, base = pl.pallas_call(
        couple_body,
        name="couple",
        in_specs=[whole()] * 5,
        out_specs=[whole()] * 2,
        out_shape=[held((8, cols)), passive],
        input_output_aliases={4: 1},
        compiler_params=params(),
    )(low, high, response, ends, base)
    got_edges = lax.ppermute(edges, "lev", swap)
    partial, lowered, mine, *_ = pl.pallas_call(
        passive_body,
        name="passive",
        in_specs=[whole()] * 8,
        out_specs=[pl.BlockSpec(memory_space=pl.ANY)] + [whole()] * 4,
        out_shape=[
            jax.ShapeDtypeStruct(adjoint.shape, F32),
            held((2, levels, rows, cols)),
            held((2, rows, cols)),
            passive,
            work[1],
        ],
        scratch_shapes=[sems],
        input_output_aliases={6: 3, 7: 4},
        compiler_params=params(),
    )(adj, cour, pivot, lower, low, high, base, active)
    return pl.pallas_call(
        solve_body,
        name="solve",
        in_specs=[whole()] * 6 + [pl.BlockSpec(memory_space=pl.ANY)],
        out_specs=pl.BlockSpec(memory_space=pl.ANY),
        out_shape=jax.ShapeDtypeStruct(adjoint.shape, F32),
        scratch_shapes=[
            pltpu.VMEM((2, levels, rows, cols), F32),
            pltpu.VMEM((2, rows, cols), F32),
            pltpu.SemaphoreType.DMA((2,)),
        ],
        input_output_aliases={6: 0},
        compiler_params=params(),
    )(lowered, lower, upper, mine, bulk, got_edges, partial)


LEVEL_UNROLL = 16


def with_halo(block, sides, width):
    for axis, dim in sides:
        count = lax.axis_size(axis)
        forward = [(i, i + 1) for i in range(count - 1)]
        forward.append((count - 1, 0))
        backward = [(target, source) for source, target in forward]
        low = lax.ppermute(
            lax.slice_in_dim(block, block.shape[dim] - width, None, axis=dim), axis, forward
        )
        high = lax.ppermute(lax.slice_in_dim(block, 0, width, axis=dim), axis, backward)
        block = jnp.concatenate([low, block, high], axis=dim)
    return block


def centered_roll(values, axis_id):
    ahead_one = jnp.roll(values, -1, axis_id)
    behind_one = jnp.roll(values, 1, axis_id)
    ahead_two = jnp.roll(values, -2, axis_id)
    behind_two = jnp.roll(values, 2, axis_id)
    return (8.0 * (ahead_one - behind_one) - (ahead_two - behind_two)) / 12.0


def centered_padded(padded):
    ahead_one = padded[:, :, 3:-1, :]
    behind_one = padded[:, :, 1:-3, :]
    ahead_two = padded[:, :, 4:, :]
    behind_two = padded[:, :, :-4, :]
    return (8.0 * (ahead_one - behind_one) - (ahead_two - behind_two)) / 12.0


def mat_vec(system_matrix, vector):
    return jnp.stack(
        [
            system_matrix[0] * vector[0] + system_matrix[1] * vector[1],
            system_matrix[2] * vector[0] + system_matrix[3] * vector[1],
        ]
    )


def chain_run(coupling, forcing, initial, backward):

    def advance(state, inputs):
        fresh = mat_vec(inputs[0], state) + inputs[1]
        return (fresh, fresh)

    final_state, states = lax.scan(
        advance,
        initial,
        (jnp.moveaxis(coupling, 1, 0), jnp.moveaxis(forcing, 1, 0)),
        reverse=backward,
        unroll=min(LEVEL_UNROLL, coupling.shape[1]),
    )
    return jnp.moveaxis(states, 0, 1)


def column_solve(pieces):
    forcing, lower_part, upper_part = pieces
    initial = jnp.zeros((2,) + forcing.shape[2:], jnp.float32)
    lowered = chain_run(lower_part, forcing, initial, False)
    solved = chain_run(upper_part, lowered, initial, True)
    return lax.all_to_all(solved, "lev", split_axis=1, concat_axis=2, tiled=True)


def local_any(adjoint, courant, metric, pivot_inverse, lower_gain, upper_gain):
    weighted = jnp.concatenate([courant[0] * adjoint, (metric[0] * adjoint[0])[None]], 0)
    padded = with_halo(weighted, (("tile", 2),), 2)
    across = centered_padded(padded)
    advected = adjoint + across[:5] + centered_roll(courant[1] * adjoint, 3)
    pressure_field = advected[4] + across[5] + centered_roll(metric[1] * adjoint[1], 2)
    forcing = mat_vec(pivot_inverse, jnp.stack([advected[2], pressure_field]))
    solved = column_solve(
        (
            lax.all_to_all(forcing, "lev", split_axis=2, concat_axis=1, tiled=True),
            lax.all_to_all(lower_gain, "lev", split_axis=2, concat_axis=1, tiled=True),
            lax.all_to_all(upper_gain, "lev", split_axis=2, concat_axis=1, tiled=True),
        )
    )
    return jnp.stack([advected[0], advected[1], solved[0], advected[3], solved[1]])


def solution(mesh):
    placed = (P(None, "lev", "tile", None),) * 6
    pair = mesh.shape["lev"] == 2 and mesh.shape["tile"] % 2 == 0

    def local(adjoint, *others):
        levels, rows = adjoint.shape[1:3]
        fits = pair and levels % EDGE_LEVELS == 0 and rows % 8 == 0 and rows > 8
        return (local_pair if fits else local_any)(adjoint, *others)

    return jax.shard_map(
        local,
        mesh=mesh,
        in_specs=placed,
        out_specs=P(None, "lev", "tile", None),
        check_vma=False,
    )
```

```python
import jax
import jax.numpy as jnp
from jax import lax
from jax.experimental import pallas as pl
from jax.experimental.pallas import tpu as pltpu
from jax.sharding import PartitionSpec as P

F32 = jnp.float32
VMEM_LIMIT = 24 * 1024 * 1024
EDGE_LEVELS = 8


def held(shape):
    return pltpu.VMEM(shape, F32)


def whole():
    return pl.BlockSpec(memory_space=pltpu.VMEM)


def in_hbm():
    return pl.BlockSpec(memory_space=pltpu.HBM)


def from_hbm(x):
    return pltpu.with_memory_space_constraint(x, pltpu.HBM)


def params():
    return pltpu.CompilerParams(vmem_limit_bytes=VMEM_LIMIT)


def mul(m, v):
    return (m[0] * v[0] + m[1] * v[1], m[2] * v[0] + m[3] * v[1])


def matmul(m, n):
    return (
        m[0] * n[0] + m[1] * n[2],
        m[0] * n[1] + m[1] * n[3],
        m[2] * n[0] + m[3] * n[2],
        m[2] * n[1] + m[3] * n[3],
    )


def add(a, b):
    return tuple(x + y for x, y in zip(a, b, strict=True))


def at(ref, level):
    return tuple(ref[k, level] for k in range(ref.shape[0]))


def emit_edges(adj, courant, metric, out, first):
    for r in range(2):
        row = first + r
        wind = courant[0, :, row, :]
        for k in range(4):
            out[k, r] = wind * adj[k, :, row, :]
        out[4, r] = wind * adj[4, :, row, :] + metric[0, :, row, :] * adj[0, :, row, :]


def fetch_all(sources, targets, sems, levels_each=2):
    levels_each = min(levels_each, sources[0].shape[1])
    for i, (source, target) in enumerate(zip(sources, targets, strict=True)):
        parts = source.shape[1] // levels_each

        def start(n, _, i=i, source=source, target=target, parts=parts):
            k, span = n // parts, pl.ds(lax.rem(n, parts) * levels_each, levels_each)
            pltpu.make_async_copy(
                source.at[k, span], target.at[k, span], sems.at[i]
            ).start()
            return 0

        lax.fori_loop(0, source.shape[0] * parts, start, 0)


def wait_all(sources, targets, sems):
    for i, (source, target) in enumerate(zip(sources, targets, strict=True)):
        pltpu.make_async_copy(source, target, sems.at[i]).wait()


def rows_of(refs, first):
    return [ref.at[:, :, pl.ds(first, 2)] for ref in refs]


def copy_rows(refs, first, dense, sem):
    plane = 0
    for ref, count in refs:
        for r in range(2):
            pltpu.make_async_copy(
                ref.at[pl.ds(0, count), :, first + r],
                dense.at[pl.ds(plane, count), r],
                sem,
            ).start()
        plane += count


def emit_dense(dense, out):
    for r in range(2):
        wind = dense[5, r]
        for k in range(4):
            out[k, r] = wind * dense[k, r]
        out[4, r] = wind * dense[4, r] + dense[6, r] * dense[0, r]


def is_first_tile():
    return lax.axis_index("tile") == 0


def is_first_chip(tile):
    return jnp.logical_and(lax.axis_index("tile") == tile, lax.axis_index("lev") == 0)


def is_last_tile():
    return lax.axis_index("tile") == lax.axis_size("tile") - 1


def edges_body(
    adj_in, courant_in, metric_in, ahead, heads, adj, courant, metric,
    tails, sems, tail_sem, head_sem,
):
    given, targets = (adj_in, courant_in, metric_in), (adj, courant, metric)
    sent = ((adj_in, 5), (courant_in, 1), (metric_in, 1))
    rows = adj.shape[2]
    first, last = is_first_tile(), is_last_tile()
    end = jnp.logical_or(first, last)

    @pl.when(first)
    def _():
        copy_rows(sent, rows - 2, tails, tail_sem)
        pltpu.make_async_copy(tails, tails, tail_sem).wait()
        emit_dense(tails, ahead)

    @pl.when(last)
    def _():
        plane = pl.ds(0, 1)
        rows_in = rows_of((adj_in, courant_in.at[plane], metric_in.at[plane]), rows - 2)
        rows_out = rows_of((adj, courant.at[plane], metric.at[plane]), rows - 2)
        fetch_all(rows_in, rows_out, sems, EDGE_LEVELS)
        copy_rows(sent, 0, heads, head_sem)
        wait_all(rows_in, rows_out, sems)
        emit_edges(adj, courant, metric, ahead, rows - 2)
        pltpu.make_async_copy(heads, heads, head_sem).wait()

    @pl.when(jnp.logical_not(end))
    def _():
        fetch_all(given, targets, sems)
        wait_all(given, targets, sems)
        emit_edges(adj, courant, metric, ahead, rows - 2)


def across(q):
    rows = q.shape[0]
    spot = lax.broadcasted_iota(jnp.int32, q.shape, 0)
    out = None
    for step, weight in ((1, 8.0 / 12.0), (2, -1.0 / 12.0)):
        ahead = jnp.where(spot < rows - step, pltpu.roll(q, rows - step, 0), 0.0)
        behind = jnp.where(spot >= step, pltpu.roll(q, step, 0), 0.0)
        term = weight * (ahead - behind)
        out = term if out is None else out + term
    return out


def along(q):
    cols = q.shape[1]
    near = pltpu.roll(q, cols - 1, 1) - pltpu.roll(q, 1, 1)
    wide = pltpu.roll(q, cols - 2, 1) - pltpu.roll(q, 2, 1)
    return (8.0 / 12.0) * near - (1.0 / 12.0) * wide


def passive_base(adj, courant, passive):
    def one(l, _):
        c0, c1 = courant[0, l], courant[1, l]
        for slot, field in ((0, 0), (1, 1), (2, 3)):
            x = adj[field, l]
            passive[slot, l] = x + across(c0 * x) + along(c1 * x)
        return 0

    lax.fori_loop(0, adj.shape[1], one, 0)


def first_tile_body(
    adj_in, courant_in, metric_in, pivot_in, lower_in, upper_in, heads, *refs
):
    behind, passive, adj, courant, metric, *work = refs[3:-2]
    sems, gain_sems = refs[-2:]

    @pl.when(is_first_tile())
    def _():
        fields = ((adj_in, courant_in, metric_in), (adj, courant, metric), sems)
        gains = ((pivot_in, lower_in, upper_in), work[-3:], gain_sems)
        fetch_all(*fields)
        fetch_all(*gains)
        wait_all(*fields)
        active_base(adj, courant, metric, work[1])
        summarise(work, gains)

    @pl.when(is_first_chip(0))
    def _():
        passive_base(adj, courant, passive)

    last = is_last_tile()

    @pl.when(last)
    def _():
        emit_dense(heads, behind)

    @pl.when(jnp.logical_not(last))
    def _():
        emit_edges(adj, courant, metric, behind, 0)


def other_tiles_body(adj_in, courant_in, metric_in, pivot_in, lower_in, upper_in, *refs):
    passive, adj, courant, metric, *work = refs[-13:-2]
    sems, gain_sems = refs[-2:]

    @pl.when(jnp.logical_not(is_first_tile()))
    def _():
        last = is_last_tile()

        @pl.when(is_first_chip(1))
        def _():
            passive_base(adj, courant, passive)

        fields = ((adj_in, courant_in, metric_in), (adj, courant, metric), sems)
        gains = ((pivot_in, lower_in, upper_in), work[-3:], gain_sems)

        @pl.when(last)
        def _():
            fetch_all(*fields)

        fetch_all(*gains)

        @pl.when(last)
        def _():
            wait_all(*fields)

        active_base(adj, courant, metric, work[1])
        summarise(work, gains)


def active_base(adj, courant, metric, active):
    def one(l, _):
        c0, c1 = courant[0, l], courant[1, l]
        x = adj[2, l]
        active[0, l] = x + across(c0 * x) + along(c1 * x)
        x = adj[4, l]
        active[1, l] = (
            x
            + across(c0 * x + metric[0, l] * adj[0, l])
            + along(c1 * x + metric[1, l] * adj[1, l])
        )
        return 0

    lax.fori_loop(0, adj.shape[1], one, 0)


def summarise(work, gains):
    bulk, active, response, ends, pivot, lower, upper = work
    levels, rows = active.shape[1:3]
    wait_all(*gains)
    states = forward(active, pivot, lower)
    one, none = jnp.ones_like(states[0][0]), jnp.zeros_like(states[0][0])
    identity = (one, none, none, one)

    def emit(state):
        for k in range(2):
            ends[k] = state[k]
            start = 4 * rows + k * (rows - 4)
            bulk[pl.ds(start, rows - 4)] = state[k][2 : rows - 2]

    def respond(l, reach):
        gain = matmul(reach, at(pivot, l))
        for k in range(4):
            for i, row in enumerate(edge_rows(rows)):
                response[k, i, pl.ds(l, 1)] = gain[k][row : row + 1]

    @pl.when(lax.axis_index("lev") == 0)
    def _():
        emit(states[-1])
        reach = identity
        for l in range(levels - 1, -1, -1):
            if l < levels - 1:
                reach = matmul(reach, at(lower, l + 1))
            respond(l, reach)

    @pl.when(lax.axis_index("lev") == 1)
    def _():
        emit(backward_first(states, upper))
        chain = [identity]
        for l in range(levels - 1):
            chain.append(matmul(chain[-1], at(upper, l)))
        reach = chain[-1]
        for l in range(levels - 1, -1, -1):
            if l < levels - 1:
                reach = add(chain[l], matmul(reach, at(lower, l + 1)))
            respond(l, reach)
        total = matmul(reach, at(lower, 0))
        for k in range(4):
            bulk[pl.ds(k * rows, rows)] = total[k]


def edge_rows(rows):
    return (0, 1, rows - 2, rows - 1)


def forward(active, pivot, lower):
    states = []
    for l in range(active.shape[1]):
        fresh = mul(at(pivot, l), at(active, l))
        if states:
            fresh = add(mul(at(lower, l), states[-1]), fresh)
        states.append(fresh)
    return states


def backward_first(states, upper):
    state = states[-1]
    for l in range(len(states) - 2, -1, -1):
        state = add(mul(at(upper, l), state), states[l])
    return state


def halo_parts(low, high):
    near, wide = 8.0 / 12.0, 1.0 / 12.0
    return (
        wide * low[0] - near * low[1],
        wide * low[1],
        -wide * high[0],
        near * high[0] - wide * high[1],
    )


def add_halo(ref, slot, low, high):
    parts = halo_parts(low, high)
    for part, row in zip(parts, edge_rows(ref.shape[2]), strict=True):
        ref[slot, :, row, :] = ref[slot, :, row, :] + part


def halo_rows(low, high, field):
    return [[ref[field, r] for r in range(2)] for ref in (low, high)]


def couple_body(low, high, response, ends, base, edges, kept):
    del base, kept
    rows = ends.shape[1]
    parts = [halo_parts(*halo_rows(low, high, field)) for field in (2, 4)]
    for i, row in enumerate(edge_rows(rows)):
        for k in range(2):
            change = (
                response[2 * k, i] * parts[0][i] + response[2 * k + 1, i] * parts[1][i]
            )
            edges[pl.ds(4 * k + i, 1)] = ends[k, pl.ds(row, 1)] + jnp.sum(
                change, axis=0, keepdims=True
            )


def sweep(active, pivot, lower, low, high, lowered, mine):
    for slot, field in ((0, 2), (1, 4)):
        add_halo(active, slot, *halo_rows(low, high, field))
    states = forward(active, pivot, lower)
    for k in range(2):
        for l in range(active.shape[1]):
            lowered[k, l] = states[l][k]
        mine[k] = states[-1][k]


def odd_tiles_body(adj, courant, base, passive):
    del base

    odd = lax.rem(lax.axis_index("tile"), 2) == 1

    @pl.when(jnp.logical_and(odd, jnp.logical_not(is_first_chip(1))))
    def _():
        passive_base(adj, courant, passive)


def passive_body(
    adj, courant, pivot, lower, low, high, base, given,
    out, lowered, mine, passive, active, sems,
):
    del base, given

    even = lax.rem(lax.axis_index("tile"), 2) == 0

    @pl.when(jnp.logical_and(even, jnp.logical_not(is_first_chip(0))))
    def _():
        passive_base(adj, courant, passive)

    copies = []
    for slot, field in enumerate((0, 1, 3)):
        add_halo(passive, slot, *halo_rows(low, high, field))
        copies.append(
            pltpu.make_async_copy(passive.at[slot], out.at[field], sems.at[slot])
        )
        copies[-1].start()
    sweep(active, pivot, lower, low, high, lowered, mine)
    for copy in copies:
        copy.wait()


def solve_body(
    lowered, lower, upper, mine, bulk, edges, partial, out, solved, other, sems
):
    del partial
    levels, rows = lowered.shape[1:3]
    for k in range(2):
        other[k, pl.ds(0, 2)] = edges[pl.ds(4 * k, 2)]
        other[k, pl.ds(2, rows - 4)] = bulk[pl.ds(4 * rows + k * (rows - 4), rows - 4)]
        other[k, pl.ds(rows - 2, 2)] = edges[pl.ds(4 * k + 2, 2)]

    half = levels // 2

    def descend(state, full):
        for l in range(levels - 1, -1, -1):
            if state is None:
                state = full(l)
            else:
                state = add(mul(at(upper, l), state), full(l))
            for k, field in ((0, 2), (1, 4)):
                solved[k, l] = state[k]
                if l % half == 0:
                    part = pl.ds(l, half)
                    pltpu.make_async_copy(
                        solved.at[k, part], out.at[field, part], sems.at[k]
                    ).start()

    @pl.when(lax.axis_index("lev") == 0)
    def _():
        gain = tuple(bulk[pl.ds(k * rows, rows)] for k in range(4))
        descend(
            add(mul(gain, (mine[0], mine[1])), (other[0], other[1])),
            lambda l: at(lowered, l),
        )

    @pl.when(lax.axis_index("lev") == 1)
    def _():
        entering = (other[0], other[1])
        full = []
        for l in range(levels):
            entering = mul(at(lower, l), entering)
            full.append(add(entering, at(lowered, l)))
        descend(None, lambda l: full[l])

    for k, field in ((0, 2), (1, 4)):
        pltpu.make_async_copy(solved.at[k], out.at[field], sems.at[k]).wait()


def local_pair(adjoint, courant, metric, pivot_inverse, lower_gain, upper_gain):
    fields, levels, rows, cols = adjoint.shape
    tiles = lax.axis_size("tile")
    swap = [(0, 1), (1, 0)]
    forth = [(i, (i + 1) % tiles) for i in range(tiles)]
    back = [(i, (i - 1) % tiles) for i in range(tiles)]
    halo = held((fields, 2, levels, cols))
    passive = held((3, levels, rows, cols))
    inputs = [held(adjoint.shape), held(courant.shape), held(metric.shape)]
    sems = pltpu.SemaphoreType.DMA((3,))
    sources = (from_hbm(adjoint), from_hbm(courant), from_hbm(metric))
    gains = (from_hbm(pivot_inverse), from_hbm(lower_gain), from_hbm(upper_gain))
    dense = held((fields + 2, 2, levels, cols))
    ahead, heads, *fetched = pl.pallas_call(
        edges_body,
        name="edges",
        in_specs=[in_hbm()] * 3,
        out_specs=[whole()] * 5,
        out_shape=[halo, dense] + inputs,
        scratch_shapes=[
            dense,
            sems,
            pltpu.SemaphoreType.DMA(()),
            pltpu.SemaphoreType.DMA(()),
        ],
        compiler_params=params(),
    )(*sources)
    work = [
        held((6 * rows - 8, cols)),
        held((2, levels, rows, cols)),
        held((4, 4, levels, cols)),
        held((2, rows, cols)),
        held(pivot_inverse.shape),
        held(lower_gain.shape),
        held(upper_gain.shape),
    ]
    low = lax.ppermute(ahead, "tile", forth)
    behind, base, adj, cour, met, *begun = pl.pallas_call(
        first_tile_body,
        name="first_tile",
        in_specs=[in_hbm()] * 6 + [whole()] * 4,
        out_specs=[whole()] * (5 + len(work)),
        out_shape=[halo, passive] + inputs + work,
        scratch_shapes=[sems, sems],
        input_output_aliases={7 + i: 2 + i for i in range(3)},
        compiler_params=params(),
    )(*sources, *gains, heads, *fetched)
    high = lax.ppermute(behind, "tile", back)
    base, adj, cour, met, summary, active, response, ends, pivot, lower, upper = pl.pallas_call(
        other_tiles_body,
        name="other_tiles",
        in_specs=[in_hbm()] * 6 + [whole()] * (4 + len(work)),
        out_specs=[whole()] * (4 + len(work)),
        out_shape=[passive] + inputs + work,
        scratch_shapes=[sems, sems],
        input_output_aliases={6 + i: i for i in range(4 + len(work))},
        compiler_params=params(),
    )(*sources, *gains, base, adj, cour, met, *begun)
    bulk = lax.ppermute(summary, "lev", swap)
    base = pl.pallas_call(
        odd_tiles_body,
        name="odd_tiles",
        in_specs=[whole()] * 3,
        out_specs=whole(),
        out_shape=passive,
        input_output_aliases={2: 0},
        compiler_params=params(),
    )(adj, cour, base)
    edges, base = pl.pallas_call(
        couple_body,
        name="couple",
        in_specs=[whole()] * 5,
        out_specs=[whole()] * 2,
        out_shape=[held((8, cols)), passive],
        input_output_aliases={4: 1},
        compiler_params=params(),
    )(low, high, response, ends, base)
    got_edges = lax.ppermute(edges, "lev", swap)
    partial, lowered, mine, *_ = pl.pallas_call(
        passive_body,
        name="passive",
        in_specs=[whole()] * 8,
        out_specs=[pl.BlockSpec(memory_space=pl.ANY)] + [whole()] * 4,
        out_shape=[
            jax.ShapeDtypeStruct(adjoint.shape, F32),
            held((2, levels, rows, cols)),
            held((2, rows, cols)),
            passive,
            work[1],
        ],
        scratch_shapes=[sems],
        input_output_aliases={6: 3, 7: 4},
        compiler_params=params(),
    )(adj, cour, pivot, lower, low, high, base, active)
    return pl.pallas_call(
        solve_body,
        name="solve",
        in_specs=[whole()] * 6 + [pl.BlockSpec(memory_space=pl.ANY)],
        out_specs=pl.BlockSpec(memory_space=pl.ANY),
        out_shape=jax.ShapeDtypeStruct(adjoint.shape, F32),
        scratch_shapes=[
            pltpu.VMEM((2, levels, rows, cols), F32),
            pltpu.VMEM((2, rows, cols), F32),
            pltpu.SemaphoreType.DMA((2,)),
        ],
        input_output_aliases={6: 0},
        compiler_params=params(),
    )(lowered, lower, upper, mine, bulk, got_edges, partial)


LEVEL_UNROLL = 16


def with_halo(block, sides, width):
    for axis, dim in sides:
        count = lax.axis_size(axis)
        forward = [(i, i + 1) for i in range(count - 1)]
        forward.append((count - 1, 0))
        backward = [(target, source) for source, target in forward]
        low = lax.ppermute(
            lax.slice_in_dim(block, block.shape[dim] - width, None, axis=dim), axis, forward
        )
        high = lax.ppermute(lax.slice_in_dim(block, 0, width, axis=dim), axis, backward)
        block = jnp.concatenate([low, block, high], axis=dim)
    return block


def centered_roll(values, axis_id):
    ahead_one = jnp.roll(values, -1, axis_id)
    behind_one = jnp.roll(values, 1, axis_id)
    ahead_two = jnp.roll(values, -2, axis_id)
    behind_two = jnp.roll(values, 2, axis_id)
    return (8.0 * (ahead_one - behind_one) - (ahead_two - behind_two)) / 12.0


def centered_padded(padded):
    ahead_one = padded[:, :, 3:-1, :]
    behind_one = padded[:, :, 1:-3, :]
    ahead_two = padded[:, :, 4:, :]
    behind_two = padded[:, :, :-4, :]
    return (8.0 * (ahead_one - behind_one) - (ahead_two - behind_two)) / 12.0


def mat_vec(system_matrix, vector):
    return jnp.stack(
        [
            system_matrix[0] * vector[0] + system_matrix[1] * vector[1],
            system_matrix[2] * vector[0] + system_matrix[3] * vector[1],
        ]
    )


def chain_run(coupling, forcing, initial, backward):

    def advance(state, inputs):
        fresh = mat_vec(inputs[0], state) + inputs[1]
        return (fresh, fresh)

    final_state, states = lax.scan(
        advance,
        initial,
        (jnp.moveaxis(coupling, 1, 0), jnp.moveaxis(forcing, 1, 0)),
        reverse=backward,
        unroll=min(LEVEL_UNROLL, coupling.shape[1]),
    )
    return jnp.moveaxis(states, 0, 1)


def column_solve(pieces):
    forcing, lower_part, upper_part = pieces
    initial = jnp.zeros((2,) + forcing.shape[2:], jnp.float32)
    lowered = chain_run(lower_part, forcing, initial, False)
    solved = chain_run(upper_part, lowered, initial, True)
    return lax.all_to_all(solved, "lev", split_axis=1, concat_axis=2, tiled=True)


def local_any(adjoint, courant, metric, pivot_inverse, lower_gain, upper_gain):
    weighted = jnp.concatenate([courant[0] * adjoint, (metric[0] * adjoint[0])[None]], 0)
    padded = with_halo(weighted, (("tile", 2),), 2)
    across = centered_padded(padded)
    advected = adjoint + across[:5] + centered_roll(courant[1] * adjoint, 3)
    pressure_field = advected[4] + across[5] + centered_roll(metric[1] * adjoint[1], 2)
    forcing = mat_vec(pivot_inverse, jnp.stack([advected[2], pressure_field]))
    solved = column_solve(
        (
            lax.all_to_all(forcing, "lev", split_axis=2, concat_axis=1, tiled=True),
            lax.all_to_all(lower_gain, "lev", split_axis=2, concat_axis=1, tiled=True),
            lax.all_to_all(upper_gain, "lev", split_axis=2, concat_axis=1, tiled=True),
        )
    )
    return jnp.stack([advected[0], advected[1], solved[0], advected[3], solved[1]])


def solution(mesh):
    placed = (P(None, "lev", "tile", None),) * 6
    pair = mesh.shape["lev"] == 2 and mesh.shape["tile"] % 2 == 0

    def local(adjoint, *others):
        levels, rows = adjoint.shape[1:3]
        fits = pair and levels % EDGE_LEVELS == 0 and rows % 8 == 0 and rows > 8
        return (local_pair if fits else local_any)(adjoint, *others)

    return jax.shard_map(
        local,
        mesh=mesh,
        in_specs=placed,
        out_specs=P(None, "lev", "tile", None),
        check_vma=False,
    )
```

```python
import jax
import jax.numpy as jnp
from jax import lax
from jax.experimental import pallas as pl
from jax.experimental.pallas import tpu as pltpu
from jax.sharding import PartitionSpec as P

F32 = jnp.float32
VMEM_LIMIT = 24 * 1024 * 1024
EDGE_LEVELS = 8


def held(shape):
    return pltpu.VMEM(shape, F32)


def whole():
    return pl.BlockSpec(memory_space=pltpu.VMEM)


def in_hbm():
    return pl.BlockSpec(memory_space=pltpu.HBM)


def from_hbm(x):
    return pltpu.with_memory_space_constraint(x, pltpu.HBM)


def params():
    return pltpu.CompilerParams(vmem_limit_bytes=VMEM_LIMIT)


def mul(m, v):
    return (m[0] * v[0] + m[1] * v[1], m[2] * v[0] + m[3] * v[1])


def matmul(m, n):
    return (
        m[0] * n[0] + m[1] * n[2],
        m[0] * n[1] + m[1] * n[3],
        m[2] * n[0] + m[3] * n[2],
        m[2] * n[1] + m[3] * n[3],
    )


def add(a, b):
    return tuple(x + y for x, y in zip(a, b, strict=True))


def at(ref, level):
    return tuple(ref[k, level] for k in range(ref.shape[0]))


def emit_edges(adj, courant, metric, out, first):
    for r in range(2):
        row = first + r
        wind = courant[0, :, row, :]
        for k in range(4):
            out[k, r] = wind * adj[k, :, row, :]
        out[4, r] = wind * adj[4, :, row, :] + metric[0, :, row, :] * adj[0, :, row, :]


def fetch_all(sources, targets, sems, levels_each=2):
    levels_each = min(levels_each, sources[0].shape[1])
    for i, (source, target) in enumerate(zip(sources, targets, strict=True)):
        parts = source.shape[1] // levels_each

        def start(n, _, i=i, source=source, target=target, parts=parts):
            k, span = n // parts, pl.ds(lax.rem(n, parts) * levels_each, levels_each)
            pltpu.make_async_copy(
                source.at[k, span], target.at[k, span], sems.at[i]
            ).start()
            return 0

        lax.fori_loop(0, source.shape[0] * parts, start, 0)


def wait_all(sources, targets, sems):
    for i, (source, target) in enumerate(zip(sources, targets, strict=True)):
        pltpu.make_async_copy(source, target, sems.at[i]).wait()


def rows_of(refs, first):
    return [ref.at[:, :, pl.ds(first, 2)] for ref in refs]


def is_first_tile():
    return lax.axis_index("tile") == 0


def is_first_chip(tile):
    return jnp.logical_and(lax.axis_index("tile") == tile, lax.axis_index("lev") == 0)


def is_last_tile():
    return lax.axis_index("tile") == lax.axis_size("tile") - 1


def edges_body(
    adj_in, courant_in, metric_in, ahead, adj, courant, metric, sems, head_sems
):
    given, targets = (adj_in, courant_in, metric_in), (adj, courant, metric)
    plane = pl.ds(0, 1)
    sent_in = (courant_in.at[plane], metric_in.at[plane], adj_in)
    sent = (courant.at[plane], metric.at[plane], adj)
    rows = adj.shape[2]
    first, last = is_first_tile(), is_last_tile()
    end = jnp.logical_or(first, last)

    tails = (rows_of(sent_in, rows - 2), rows_of(sent, rows - 2), sems)
    heads = (rows_of(sent_in, 0), rows_of(sent, 0), head_sems)

    @pl.when(end)
    def _():
        fetch_all(*tails, EDGE_LEVELS)

        @pl.when(last)
        def _():
            fetch_all(*heads, EDGE_LEVELS)

        wait_all(*tails)

    @pl.when(jnp.logical_not(end))
    def _():
        fetch_all(given, targets, sems)
        wait_all(given, targets, sems)

    emit_edges(adj, courant, metric, ahead, rows - 2)

    @pl.when(last)
    def _():
        wait_all(*heads)


def across(q):
    rows = q.shape[0]
    spot = lax.broadcasted_iota(jnp.int32, q.shape, 0)
    out = None
    for step, weight in ((1, 8.0 / 12.0), (2, -1.0 / 12.0)):
        ahead = jnp.where(spot < rows - step, pltpu.roll(q, rows - step, 0), 0.0)
        behind = jnp.where(spot >= step, pltpu.roll(q, step, 0), 0.0)
        term = weight * (ahead - behind)
        out = term if out is None else out + term
    return out


def along(q):
    cols = q.shape[1]
    near = pltpu.roll(q, cols - 1, 1) - pltpu.roll(q, 1, 1)
    wide = pltpu.roll(q, cols - 2, 1) - pltpu.roll(q, 2, 1)
    return (8.0 / 12.0) * near - (1.0 / 12.0) * wide


def passive_base(adj, courant, passive):
    def one(l, _):
        c0, c1 = courant[0, l], courant[1, l]
        for slot, field in ((0, 0), (1, 1), (2, 3)):
            x = adj[field, l]
            passive[slot, l] = x + across(c0 * x) + along(c1 * x)
        return 0

    lax.fori_loop(0, adj.shape[1], one, 0)


def first_tile_body(adj_in, courant_in, metric_in, pivot_in, lower_in, upper_in, *refs):
    behind, passive, adj, courant, metric, *work = refs[3:-2]
    sems, gain_sems = refs[-2:]

    @pl.when(is_first_tile())
    def _():
        fields = ((adj_in, courant_in, metric_in), (adj, courant, metric), sems)
        gains = ((pivot_in, lower_in, upper_in), work[-3:], gain_sems)
        fetch_all(*fields)
        fetch_all(*gains)
        wait_all(*fields)
        active_base(adj, courant, metric, work[1])
        summarise(work, gains)

    @pl.when(is_first_chip(0))
    def _():
        passive_base(adj, courant, passive)

    emit_edges(adj, courant, metric, behind, 0)


def other_tiles_body(adj_in, courant_in, metric_in, pivot_in, lower_in, upper_in, *refs):
    passive, adj, courant, metric, *work = refs[-13:-2]
    sems, gain_sems = refs[-2:]

    @pl.when(jnp.logical_not(is_first_tile()))
    def _():
        last = is_last_tile()

        @pl.when(is_first_chip(1))
        def _():
            passive_base(adj, courant, passive)

        fields = ((adj_in, courant_in, metric_in), (adj, courant, metric), sems)
        gains = ((pivot_in, lower_in, upper_in), work[-3:], gain_sems)

        @pl.when(last)
        def _():
            fetch_all(*fields)

        fetch_all(*gains)

        @pl.when(last)
        def _():
            wait_all(*fields)

        active_base(adj, courant, metric, work[1])
        summarise(work, gains)


def active_base(adj, courant, metric, active):
    def one(l, _):
        c0, c1 = courant[0, l], courant[1, l]
        x = adj[2, l]
        active[0, l] = x + across(c0 * x) + along(c1 * x)
        x = adj[4, l]
        active[1, l] = (
            x
            + across(c0 * x + metric[0, l] * adj[0, l])
            + along(c1 * x + metric[1, l] * adj[1, l])
        )
        return 0

    lax.fori_loop(0, adj.shape[1], one, 0)


def summarise(work, gains):
    bulk, active, response, ends, pivot, lower, upper = work
    levels, rows = active.shape[1:3]
    wait_all(*gains)
    states = forward(active, pivot, lower)

    def emit(state):
        for k in range(2):
            ends[k] = state[k]
            start = 4 * rows + k * (rows - 4)
            bulk[pl.ds(start, rows - 4)] = state[k][2 : rows - 2]

    def respond(l, reach):
        gain = at(pivot, l) if reach is None else matmul(reach, at(pivot, l))
        for k in range(4):
            for i, row in enumerate(edge_rows(rows)):
                response[k, i, pl.ds(l, 1)] = gain[k][row : row + 1]

    @pl.when(lax.axis_index("lev") == 0)
    def _():
        emit(states[-1])
        reach = None
        for l in range(levels - 1, -1, -1):
            if l < levels - 1:
                step = at(lower, l + 1)
                reach = step if reach is None else matmul(reach, step)
            respond(l, reach)

    @pl.when(lax.axis_index("lev") == 1)
    def _():
        emit(backward_first(states, upper))
        chain = [None, at(upper, 0)]
        for l in range(1, levels - 1):
            chain.append(matmul(chain[-1], at(upper, l)))
        reach = chain[-1]
        for l in range(levels - 1, -1, -1):
            if l < levels - 1:
                reach = matmul(reach, at(lower, l + 1))
                if l > 0:
                    reach = add(chain[l], reach)
                else:
                    reach = (reach[0] + 1.0, reach[1], reach[2], reach[3] + 1.0)
            respond(l, reach)
        total = matmul(reach, at(lower, 0))
        for k in range(4):
            bulk[pl.ds(k * rows, rows)] = total[k]


def edge_rows(rows):
    return (0, 1, rows - 2, rows - 1)


def forward(active, pivot, lower):
    states = []
    for l in range(active.shape[1]):
        fresh = mul(at(pivot, l), at(active, l))
        if states:
            fresh = add(mul(at(lower, l), states[-1]), fresh)
        states.append(fresh)
    return states


def backward_first(states, upper):
    state = states[-1]
    for l in range(len(states) - 2, -1, -1):
        state = add(mul(at(upper, l), state), states[l])
    return state


def halo_parts(low, high):
    near, wide = 8.0 / 12.0, 1.0 / 12.0
    return (
        wide * low[0] - near * low[1],
        wide * low[1],
        -wide * high[0],
        near * high[0] - wide * high[1],
    )


def add_halo(ref, slot, low, high):
    parts = halo_parts(low, high)
    for part, row in zip(parts, edge_rows(ref.shape[2]), strict=True):
        ref[slot, :, row, :] = ref[slot, :, row, :] + part


def halo_rows(low, high, field):
    return [[ref[field, r] for r in range(2)] for ref in (low, high)]


def couple_body(low, high, response, ends, base, edges, kept):
    del base, kept
    rows = ends.shape[1]
    parts = [halo_parts(*halo_rows(low, high, field)) for field in (2, 4)]
    for i, row in enumerate(edge_rows(rows)):
        for k in range(2):
            change = (
                response[2 * k, i] * parts[0][i] + response[2 * k + 1, i] * parts[1][i]
            )
            edges[pl.ds(4 * k + i, 1)] = ends[k, pl.ds(row, 1)] + jnp.sum(
                change, axis=0, keepdims=True
            )


def sweep(active, pivot, lower, low, high, lowered, mine):
    for slot, field in ((0, 2), (1, 4)):
        add_halo(active, slot, *halo_rows(low, high, field))
    states = forward(active, pivot, lower)
    for k in range(2):
        for l in range(active.shape[1]):
            lowered[k, l] = states[l][k]
        mine[k] = states[-1][k]


def odd_tiles_body(adj, courant, base, passive):
    del base

    odd = lax.rem(lax.axis_index("tile"), 2) == 1

    @pl.when(jnp.logical_and(odd, jnp.logical_not(is_first_chip(1))))
    def _():
        passive_base(adj, courant, passive)


def passive_body(
    adj, courant, pivot, lower, low, high, base, given,
    out, lowered, mine, passive, active, sems,
):
    del base, given

    even = lax.rem(lax.axis_index("tile"), 2) == 0

    @pl.when(jnp.logical_and(even, jnp.logical_not(is_first_chip(0))))
    def _():
        passive_base(adj, courant, passive)

    copies = []
    for slot, field in enumerate((0, 1, 3)):
        add_halo(passive, slot, *halo_rows(low, high, field))
        copies.append(
            pltpu.make_async_copy(passive.at[slot], out.at[field], sems.at[slot])
        )
        copies[-1].start()
    sweep(active, pivot, lower, low, high, lowered, mine)
    for copy in copies:
        copy.wait()


def solve_body(
    lowered, lower, upper, mine, bulk, edges, partial, out, solved, other, sems
):
    del partial
    levels, rows = lowered.shape[1:3]
    for k in range(2):
        other[k, pl.ds(0, 2)] = edges[pl.ds(4 * k, 2)]
        other[k, pl.ds(2, rows - 4)] = bulk[pl.ds(4 * rows + k * (rows - 4), rows - 4)]
        other[k, pl.ds(rows - 2, 2)] = edges[pl.ds(4 * k + 2, 2)]

    half = levels // 2

    def descend(state, full):
        for l in range(levels - 1, -1, -1):
            if state is None:
                state = full(l)
            else:
                state = add(mul(at(upper, l), state), full(l))
            for k, field in ((0, 2), (1, 4)):
                solved[k, l] = state[k]
                if l % half == 0:
                    part = pl.ds(l, half)
                    pltpu.make_async_copy(
                        solved.at[k, part], out.at[field, part], sems.at[k]
                    ).start()

    @pl.when(lax.axis_index("lev") == 0)
    def _():
        gain = tuple(bulk[pl.ds(k * rows, rows)] for k in range(4))
        descend(
            add(mul(gain, (mine[0], mine[1])), (other[0], other[1])),
            lambda l: at(lowered, l),
        )

    @pl.when(lax.axis_index("lev") == 1)
    def _():
        entering = (other[0], other[1])
        full = []
        for l in range(levels):
            entering = mul(at(lower, l), entering)
            full.append(add(entering, at(lowered, l)))
        descend(None, lambda l: full[l])

    for k, field in ((0, 2), (1, 4)):
        pltpu.make_async_copy(solved.at[k], out.at[field], sems.at[k]).wait()


def local_pair(adjoint, courant, metric, pivot_inverse, lower_gain, upper_gain):
    fields, levels, rows, cols = adjoint.shape
    tiles = lax.axis_size("tile")
    swap = [(0, 1), (1, 0)]
    forth = [(i, (i + 1) % tiles) for i in range(tiles)]
    back = [(i, (i - 1) % tiles) for i in range(tiles)]
    halo = held((fields, 2, levels, cols))
    passive = held((3, levels, rows, cols))
    inputs = [held(adjoint.shape), held(courant.shape), held(metric.shape)]
    sems = pltpu.SemaphoreType.DMA((3,))
    sources = (from_hbm(adjoint), from_hbm(courant), from_hbm(metric))
    gains = (from_hbm(pivot_inverse), from_hbm(lower_gain), from_hbm(upper_gain))
    ahead, *fetched = pl.pallas_call(
        edges_body,
        name="edges",
        in_specs=[in_hbm()] * 3,
        out_specs=[whole()] * 4,
        out_shape=[halo] + inputs,
        scratch_shapes=[sems, sems],
        compiler_params=params(),
    )(*sources)
    work = [
        held((6 * rows - 8, cols)),
        held((2, levels, rows, cols)),
        held((4, 4, levels, cols)),
        held((2, rows, cols)),
        held(pivot_inverse.shape),
        held(lower_gain.shape),
        held(upper_gain.shape),
    ]
    low = lax.ppermute(ahead, "tile", forth)
    behind, base, adj, cour, met, *begun = pl.pallas_call(
        first_tile_body,
        name="first_tile",
        in_specs=[in_hbm()] * 6 + [whole()] * 3,
        out_specs=[whole()] * (5 + len(work)),
        out_shape=[halo, passive] + inputs + work,
        scratch_shapes=[sems, sems],
        input_output_aliases={6 + i: 2 + i for i in range(3)},
        compiler_params=params(),
    )(*sources, *gains, *fetched)
    high = lax.ppermute(behind, "tile", back)
    base, adj, cour, met, summary, active, response, ends, pivot, lower, upper = pl.pallas_call(
        other_tiles_body,
        name="other_tiles",
        in_specs=[in_hbm()] * 6 + [whole()] * (4 + len(work)),
        out_specs=[whole()] * (4 + len(work)),
        out_shape=[passive] + inputs + work,
        scratch_shapes=[sems, sems],
        input_output_aliases={6 + i: i for i in range(4 + len(work))},
        compiler_params=params(),
    )(*sources, *gains, base, adj, cour, met, *begun)
    bulk = lax.ppermute(summary, "lev", swap)
    base = pl.pallas_call(
        odd_tiles_body,
        name="odd_tiles",
        in_specs=[whole()] * 3,
        out_specs=whole(),
        out_shape=passive,
        input_output_aliases={2: 0},
        compiler_params=params(),
    )(adj, cour, base)
    edges, base = pl.pallas_call(
        couple_body,
        name="couple",
        in_specs=[whole()] * 5,
        out_specs=[whole()] * 2,
        out_shape=[held((8, cols)), passive],
        input_output_aliases={4: 1},
        compiler_params=params(),
    )(low, high, response, ends, base)
    got_edges = lax.ppermute(edges, "lev", swap)
    partial, lowered, mine, *_ = pl.pallas_call(
        passive_body,
        name="passive",
        in_specs=[whole()] * 8,
        out_specs=[pl.BlockSpec(memory_space=pl.ANY)] + [whole()] * 4,
        out_shape=[
            jax.ShapeDtypeStruct(adjoint.shape, F32),
            held((2, levels, rows, cols)),
            held((2, rows, cols)),
            passive,
            work[1],
        ],
        scratch_shapes=[sems],
        input_output_aliases={6: 3, 7: 4},
        compiler_params=params(),
    )(adj, cour, pivot, lower, low, high, base, active)
    return pl.pallas_call(
        solve_body,
        name="solve",
        in_specs=[whole()] * 6 + [pl.BlockSpec(memory_space=pl.ANY)],
        out_specs=pl.BlockSpec(memory_space=pl.ANY),
        out_shape=jax.ShapeDtypeStruct(adjoint.shape, F32),
        scratch_shapes=[
            pltpu.VMEM((2, levels, rows, cols), F32),
            pltpu.VMEM((2, rows, cols), F32),
            pltpu.SemaphoreType.DMA((2,)),
        ],
        input_output_aliases={6: 0},
        compiler_params=params(),
    )(lowered, lower, upper, mine, bulk, got_edges, partial)


LEVEL_UNROLL = 16


def with_halo(block, sides, width):
    for axis, dim in sides:
        count = lax.axis_size(axis)
        forward = [(i, i + 1) for i in range(count - 1)]
        forward.append((count - 1, 0))
        backward = [(target, source) for source, target in forward]
        low = lax.ppermute(
            lax.slice_in_dim(block, block.shape[dim] - width, None, axis=dim), axis, forward
        )
        high = lax.ppermute(lax.slice_in_dim(block, 0, width, axis=dim), axis, backward)
        block = jnp.concatenate([low, block, high], axis=dim)
    return block


def centered_roll(values, axis_id):
    ahead_one = jnp.roll(values, -1, axis_id)
    behind_one = jnp.roll(values, 1, axis_id)
    ahead_two = jnp.roll(values, -2, axis_id)
    behind_two = jnp.roll(values, 2, axis_id)
    return (8.0 * (ahead_one - behind_one) - (ahead_two - behind_two)) / 12.0


def centered_padded(padded):
    ahead_one = padded[:, :, 3:-1, :]
    behind_one = padded[:, :, 1:-3, :]
    ahead_two = padded[:, :, 4:, :]
    behind_two = padded[:, :, :-4, :]
    return (8.0 * (ahead_one - behind_one) - (ahead_two - behind_two)) / 12.0


def mat_vec(system_matrix, vector):
    return jnp.stack(
        [
            system_matrix[0] * vector[0] + system_matrix[1] * vector[1],
            system_matrix[2] * vector[0] + system_matrix[3] * vector[1],
        ]
    )


def chain_run(coupling, forcing, initial, backward):

    def advance(state, inputs):
        fresh = mat_vec(inputs[0], state) + inputs[1]
        return (fresh, fresh)

    final_state, states = lax.scan(
        advance,
        initial,
        (jnp.moveaxis(coupling, 1, 0), jnp.moveaxis(forcing, 1, 0)),
        reverse=backward,
        unroll=min(LEVEL_UNROLL, coupling.shape[1]),
    )
    return jnp.moveaxis(states, 0, 1)


def column_solve(pieces):
    forcing, lower_part, upper_part = pieces
    initial = jnp.zeros((2,) + forcing.shape[2:], jnp.float32)
    lowered = chain_run(lower_part, forcing, initial, False)
    solved = chain_run(upper_part, lowered, initial, True)
    return lax.all_to_all(solved, "lev", split_axis=1, concat_axis=2, tiled=True)


def local_any(adjoint, courant, metric, pivot_inverse, lower_gain, upper_gain):
    weighted = jnp.concatenate([courant[0] * adjoint, (metric[0] * adjoint[0])[None]], 0)
    padded = with_halo(weighted, (("tile", 2),), 2)
    across = centered_padded(padded)
    advected = adjoint + across[:5] + centered_roll(courant[1] * adjoint, 3)
    pressure_field = advected[4] + across[5] + centered_roll(metric[1] * adjoint[1], 2)
    forcing = mat_vec(pivot_inverse, jnp.stack([advected[2], pressure_field]))
    solved = column_solve(
        (
            lax.all_to_all(forcing, "lev", split_axis=2, concat_axis=1, tiled=True),
            lax.all_to_all(lower_gain, "lev", split_axis=2, concat_axis=1, tiled=True),
            lax.all_to_all(upper_gain, "lev", split_axis=2, concat_axis=1, tiled=True),
        )
    )
    return jnp.stack([advected[0], advected[1], solved[0], advected[3], solved[1]])


def solution(mesh):
    placed = (P(None, "lev", "tile", None),) * 6
    pair = mesh.shape["lev"] == 2 and mesh.shape["tile"] % 2 == 0

    def local(adjoint, *others):
        levels, rows = adjoint.shape[1:3]
        fits = pair and levels % EDGE_LEVELS == 0 and rows % 8 == 0 and rows > 8
        return (local_pair if fits else local_any)(adjoint, *others)

    return jax.shard_map(
        local,
        mesh=mesh,
        in_specs=placed,
        out_specs=P(None, "lev", "tile", None),
        check_vma=False,
    )
```

```python
import jax
import jax.numpy as jnp
from jax import lax
from jax.experimental import pallas as pl
from jax.experimental.pallas import tpu as pltpu
from jax.sharding import PartitionSpec as P

F32 = jnp.float32
VMEM_LIMIT = 24 * 1024 * 1024
EDGE_LEVELS = 8


def held(shape):
    return pltpu.VMEM(shape, F32)


def whole():
    return pl.BlockSpec(memory_space=pltpu.VMEM)


def in_hbm():
    return pl.BlockSpec(memory_space=pltpu.HBM)


def from_hbm(x):
    return pltpu.with_memory_space_constraint(x, pltpu.HBM)


def params():
    return pltpu.CompilerParams(vmem_limit_bytes=VMEM_LIMIT)


def mul(m, v):
    return (m[0] * v[0] + m[1] * v[1], m[2] * v[0] + m[3] * v[1])


def matmul(m, n):
    return (
        m[0] * n[0] + m[1] * n[2],
        m[0] * n[1] + m[1] * n[3],
        m[2] * n[0] + m[3] * n[2],
        m[2] * n[1] + m[3] * n[3],
    )


def add(a, b):
    return tuple(x + y for x, y in zip(a, b, strict=True))


def at(ref, level):
    return tuple(ref[k, level] for k in range(ref.shape[0]))


def emit_edges(adj, courant, metric, out, first):
    for r in range(2):
        row = first + r
        wind = courant[0, :, row, :]
        for k in range(4):
            out[k, r] = wind * adj[k, :, row, :]
        out[4, r] = wind * adj[4, :, row, :] + metric[0, :, row, :] * adj[0, :, row, :]


def fetch_all(sources, targets, sems, levels_each=2):
    levels_each = min(levels_each, sources[0].shape[1])
    for i, (source, target) in enumerate(zip(sources, targets, strict=True)):
        parts = source.shape[1] // levels_each

        def start(n, _, i=i, source=source, target=target, parts=parts):
            k, span = n // parts, pl.ds(lax.rem(n, parts) * levels_each, levels_each)
            pltpu.make_async_copy(
                source.at[k, span], target.at[k, span], sems.at[i]
            ).start()
            return 0

        lax.fori_loop(0, source.shape[0] * parts, start, 0)


def wait_all(sources, targets, sems):
    for i, (source, target) in enumerate(zip(sources, targets, strict=True)):
        pltpu.make_async_copy(source, target, sems.at[i]).wait()


def rows_of(refs, first):
    return [ref.at[:, :, pl.ds(first, 2)] for ref in refs]


def is_first_tile():
    return lax.axis_index("tile") == 0


def is_first_chip(tile):
    return jnp.logical_and(lax.axis_index("tile") == tile, lax.axis_index("lev") == 0)


def is_last_tile():
    return lax.axis_index("tile") == lax.axis_size("tile") - 1


def edges_body(
    adj_in, courant_in, metric_in, ahead, adj, courant, metric, sems, head_sems
):
    given, targets = (adj_in, courant_in, metric_in), (adj, courant, metric)
    plane = pl.ds(0, 1)
    sent_in = (courant_in.at[plane], metric_in.at[plane], adj_in)
    sent = (courant.at[plane], metric.at[plane], adj)
    rows = adj.shape[2]
    first, last = is_first_tile(), is_last_tile()
    end = jnp.logical_or(first, last)

    tails = (rows_of(sent_in, rows - 2), rows_of(sent, rows - 2), sems)
    heads = (rows_of(sent_in, 0), rows_of(sent, 0), head_sems)

    @pl.when(end)
    def _():
        fetch_all(*tails, EDGE_LEVELS)

        @pl.when(last)
        def _():
            fetch_all(*heads, EDGE_LEVELS)

        wait_all(*tails)

    @pl.when(jnp.logical_not(end))
    def _():
        fetch_all(given, targets, sems)
        wait_all(given, targets, sems)

    emit_edges(adj, courant, metric, ahead, rows - 2)

    @pl.when(last)
    def _():
        wait_all(*heads)


def across(q):
    rows = q.shape[0]
    spot = lax.broadcasted_iota(jnp.int32, q.shape, 0)
    out = None
    for step, weight in ((1, 8.0 / 12.0), (2, -1.0 / 12.0)):
        ahead = jnp.where(spot < rows - step, pltpu.roll(q, rows - step, 0), 0.0)
        behind = jnp.where(spot >= step, pltpu.roll(q, step, 0), 0.0)
        term = weight * (ahead - behind)
        out = term if out is None else out + term
    return out


def along(q):
    cols = q.shape[1]
    near = pltpu.roll(q, cols - 1, 1) - pltpu.roll(q, 1, 1)
    wide = pltpu.roll(q, cols - 2, 1) - pltpu.roll(q, 2, 1)
    return (8.0 / 12.0) * near - (1.0 / 12.0) * wide


def passive_base(adj, courant, passive):
    def one(l, _):
        c0, c1 = courant[0, l], courant[1, l]
        for slot, field in ((0, 0), (1, 1), (2, 3)):
            x = adj[field, l]
            passive[slot, l] = x + across(c0 * x) + along(c1 * x)
        return 0

    lax.fori_loop(0, adj.shape[1], one, 0)


def first_tile_body(adj_in, courant_in, metric_in, pivot_in, lower_in, upper_in, *refs):
    behind, passive, adj, courant, metric, *work = refs[3:-2]
    sems, gain_sems = refs[-2:]

    @pl.when(is_first_tile())
    def _():
        fields = ((adj_in, courant_in, metric_in), (adj, courant, metric), sems)
        gains = ((pivot_in, lower_in, upper_in), work[-3:], gain_sems)
        fetch_all(*fields)
        fetch_all(*gains)
        wait_all(*fields)
        active_base(adj, courant, metric, work[1])
        summarise(work, gains)

    @pl.when(is_first_chip(0))
    def _():
        passive_base(adj, courant, passive)

    emit_edges(adj, courant, metric, behind, 0)


def other_tiles_body(adj_in, courant_in, metric_in, pivot_in, lower_in, upper_in, *refs):
    passive, adj, courant, metric, *work = refs[-13:-2]
    sems, gain_sems = refs[-2:]

    @pl.when(is_first_chip(1))
    def _():
        passive_base(adj, courant, passive)

    @pl.when(jnp.logical_not(is_first_tile()))
    def _():
        last = is_last_tile()
        fields = ((adj_in, courant_in, metric_in), (adj, courant, metric), sems)
        gains = ((pivot_in, lower_in, upper_in), work[-3:], gain_sems)

        @pl.when(last)
        def _():
            fetch_all(*fields)

        fetch_all(*gains)

        @pl.when(last)
        def _():
            wait_all(*fields)

        active_base(adj, courant, metric, work[1])
        summarise(work, gains)


def active_base(adj, courant, metric, active):
    def one(l, _):
        c0, c1 = courant[0, l], courant[1, l]
        x = adj[2, l]
        active[0, l] = x + across(c0 * x) + along(c1 * x)
        x = adj[4, l]
        active[1, l] = (
            x
            + across(c0 * x + metric[0, l] * adj[0, l])
            + along(c1 * x + metric[1, l] * adj[1, l])
        )
        return 0

    lax.fori_loop(0, adj.shape[1], one, 0)


def summarise(work, gains):
    bulk, active, response, ends, pivot, lower, upper = work
    levels, rows = active.shape[1:3]
    wait_all(*gains)
    states = forward(active, pivot, lower)
    one, none = jnp.ones_like(states[0][0]), jnp.zeros_like(states[0][0])
    identity = (one, none, none, one)

    def emit(state):
        for k in range(2):
            ends[k] = state[k]
            start = 4 * rows + k * (rows - 4)
            bulk[pl.ds(start, rows - 4)] = state[k][2 : rows - 2]

    def respond(l, reach):
        gain = matmul(reach, at(pivot, l))
        for k in range(4):
            for i, row in enumerate(edge_rows(rows)):
                response[k, i, pl.ds(l, 1)] = gain[k][row : row + 1]

    @pl.when(lax.axis_index("lev") == 0)
    def _():
        emit(states[-1])
        reach = identity
        for l in range(levels - 1, -1, -1):
            if l < levels - 1:
                reach = matmul(reach, at(lower, l + 1))
            respond(l, reach)

    @pl.when(lax.axis_index("lev") == 1)
    def _():
        emit(backward_first(states, upper))
        chain = [identity]
        for l in range(levels - 1):
            chain.append(matmul(chain[-1], at(upper, l)))
        reach = chain[-1]
        for l in range(levels - 1, -1, -1):
            if l < levels - 1:
                reach = add(chain[l], matmul(reach, at(lower, l + 1)))
            respond(l, reach)
        total = matmul(reach, at(lower, 0))
        for k in range(4):
            bulk[pl.ds(k * rows, rows)] = total[k]


def edge_rows(rows):
    return (0, 1, rows - 2, rows - 1)


def forward(active, pivot, lower):
    states = []
    for l in range(active.shape[1]):
        fresh = mul(at(pivot, l), at(active, l))
        if states:
            fresh = add(mul(at(lower, l), states[-1]), fresh)
        states.append(fresh)
    return states


def backward_first(states, upper):
    state = states[-1]
    for l in range(len(states) - 2, -1, -1):
        state = add(mul(at(upper, l), state), states[l])
    return state


def halo_parts(low, high):
    near, wide = 8.0 / 12.0, 1.0 / 12.0
    return (
        wide * low[0] - near * low[1],
        wide * low[1],
        -wide * high[0],
        near * high[0] - wide * high[1],
    )


def add_halo(ref, slot, low, high):
    parts = halo_parts(low, high)
    for part, row in zip(parts, edge_rows(ref.shape[2]), strict=True):
        ref[slot, :, row, :] = ref[slot, :, row, :] + part


def halo_rows(low, high, field):
    return [[ref[field, r] for r in range(2)] for ref in (low, high)]


def couple_body(low, high, response, ends, base, edges, kept):
    del base, kept
    rows = ends.shape[1]
    parts = [halo_parts(*halo_rows(low, high, field)) for field in (2, 4)]
    for i, row in enumerate(edge_rows(rows)):
        for k in range(2):
            change = (
                response[2 * k, i] * parts[0][i] + response[2 * k + 1, i] * parts[1][i]
            )
            edges[pl.ds(4 * k + i, 1)] = ends[k, pl.ds(row, 1)] + jnp.sum(
                change, axis=0, keepdims=True
            )


def sweep(active, pivot, lower, low, high, lowered, mine):
    for slot, field in ((0, 2), (1, 4)):
        add_halo(active, slot, *halo_rows(low, high, field))
    states = forward(active, pivot, lower)
    for k in range(2):
        for l in range(active.shape[1]):
            lowered[k, l] = states[l][k]
        mine[k] = states[-1][k]


def odd_tiles_body(adj, courant, base, passive):
    del base

    odd = lax.rem(lax.axis_index("tile"), 2) == 1

    @pl.when(jnp.logical_and(odd, jnp.logical_not(is_first_chip(1))))
    def _():
        passive_base(adj, courant, passive)


def passive_body(
    adj, courant, pivot, lower, low, high, base, given,
    out, lowered, mine, passive, active, sems,
):
    del base, given

    even = lax.rem(lax.axis_index("tile"), 2) == 0

    @pl.when(jnp.logical_and(even, jnp.logical_not(is_first_chip(0))))
    def _():
        passive_base(adj, courant, passive)

    copies = []
    for slot, field in enumerate((0, 1, 3)):
        add_halo(passive, slot, *halo_rows(low, high, field))
        copies.append(
            pltpu.make_async_copy(passive.at[slot], out.at[field], sems.at[slot])
        )
        copies[-1].start()
    sweep(active, pivot, lower, low, high, lowered, mine)
    for copy in copies:
        copy.wait()


def solve_body(
    lowered, lower, upper, mine, bulk, edges, partial, out, solved, other, sems
):
    del partial
    levels, rows = lowered.shape[1:3]
    for k in range(2):
        other[k, pl.ds(0, 2)] = edges[pl.ds(4 * k, 2)]
        other[k, pl.ds(2, rows - 4)] = bulk[pl.ds(4 * rows + k * (rows - 4), rows - 4)]
        other[k, pl.ds(rows - 2, 2)] = edges[pl.ds(4 * k + 2, 2)]

    def descend(state, full):
        for l in range(levels - 1, -1, -1):
            if state is None:
                state = full(l)
            else:
                state = add(mul(at(upper, l), state), full(l))
            for k, field in ((0, 2), (1, 4)):
                solved[k, l] = state[k]
                if l == 0:
                    part = pl.ds(0, levels)
                    pltpu.make_async_copy(
                        solved.at[k, part], out.at[field, part], sems.at[k]
                    ).start()

    @pl.when(lax.axis_index("lev") == 0)
    def _():
        gain = tuple(bulk[pl.ds(k * rows, rows)] for k in range(4))
        descend(
            add(mul(gain, (mine[0], mine[1])), (other[0], other[1])),
            lambda l: at(lowered, l),
        )

    @pl.when(lax.axis_index("lev") == 1)
    def _():
        entering = (other[0], other[1])
        full = []
        for l in range(levels):
            entering = mul(at(lower, l), entering)
            full.append(add(entering, at(lowered, l)))
        descend(None, lambda l: full[l])

    for k, field in ((0, 2), (1, 4)):
        pltpu.make_async_copy(solved.at[k], out.at[field], sems.at[k]).wait()


def local_pair(adjoint, courant, metric, pivot_inverse, lower_gain, upper_gain):
    fields, levels, rows, cols = adjoint.shape
    tiles = lax.axis_size("tile")
    swap = [(0, 1), (1, 0)]
    forth = [(i, (i + 1) % tiles) for i in range(tiles)]
    back = [(i, (i - 1) % tiles) for i in range(tiles)]
    halo = held((fields, 2, levels, cols))
    passive = held((3, levels, rows, cols))
    inputs = [held(adjoint.shape), held(courant.shape), held(metric.shape)]
    sems = pltpu.SemaphoreType.DMA((3,))
    sources = (from_hbm(adjoint), from_hbm(courant), from_hbm(metric))
    gains = (from_hbm(pivot_inverse), from_hbm(lower_gain), from_hbm(upper_gain))
    ahead, *fetched = pl.pallas_call(
        edges_body,
        name="edges",
        in_specs=[in_hbm()] * 3,
        out_specs=[whole()] * 4,
        out_shape=[halo] + inputs,
        scratch_shapes=[sems, sems],
        compiler_params=params(),
    )(*sources)
    work = [
        held((6 * rows - 8, cols)),
        held((2, levels, rows, cols)),
        held((4, 4, levels, cols)),
        held((2, rows, cols)),
        held(pivot_inverse.shape),
        held(lower_gain.shape),
        held(upper_gain.shape),
    ]
    low = lax.ppermute(ahead, "tile", forth)
    behind, base, adj, cour, met, *begun = pl.pallas_call(
        first_tile_body,
        name="first_tile",
        in_specs=[in_hbm()] * 6 + [whole()] * 3,
        out_specs=[whole()] * (5 + len(work)),
        out_shape=[halo, passive] + inputs + work,
        scratch_shapes=[sems, sems],
        input_output_aliases={6 + i: 2 + i for i in range(3)},
        compiler_params=params(),
    )(*sources, *gains, *fetched)
    high = lax.ppermute(behind, "tile", back)
    base, adj, cour, met, summary, active, response, ends, pivot, lower, upper = pl.pallas_call(
        other_tiles_body,
        name="other_tiles",
        in_specs=[in_hbm()] * 6 + [whole()] * (4 + len(work)),
        out_specs=[whole()] * (4 + len(work)),
        out_shape=[passive] + inputs + work,
        scratch_shapes=[sems, sems],
        input_output_aliases={6 + i: i for i in range(4 + len(work))},
        compiler_params=params(),
    )(*sources, *gains, base, adj, cour, met, *begun)
    bulk = lax.ppermute(summary, "lev", swap)
    base = pl.pallas_call(
        odd_tiles_body,
        name="odd_tiles",
        in_specs=[whole()] * 3,
        out_specs=whole(),
        out_shape=passive,
        input_output_aliases={2: 0},
        compiler_params=params(),
    )(adj, cour, base)
    edges, base = pl.pallas_call(
        couple_body,
        name="couple",
        in_specs=[whole()] * 5,
        out_specs=[whole()] * 2,
        out_shape=[held((8, cols)), passive],
        input_output_aliases={4: 1},
        compiler_params=params(),
    )(low, high, response, ends, base)
    got_edges = lax.ppermute(edges, "lev", swap)
    partial, lowered, mine, *_ = pl.pallas_call(
        passive_body,
        name="passive",
        in_specs=[whole()] * 8,
        out_specs=[pl.BlockSpec(memory_space=pl.ANY)] + [whole()] * 4,
        out_shape=[
            jax.ShapeDtypeStruct(adjoint.shape, F32),
            held((2, levels, rows, cols)),
            held((2, rows, cols)),
            passive,
            work[1],
        ],
        scratch_shapes=[sems],
        input_output_aliases={6: 3, 7: 4},
        compiler_params=params(),
    )(adj, cour, pivot, lower, low, high, base, active)
    return pl.pallas_call(
        solve_body,
        name="solve",
        in_specs=[whole()] * 6 + [pl.BlockSpec(memory_space=pl.ANY)],
        out_specs=pl.BlockSpec(memory_space=pl.ANY),
        out_shape=jax.ShapeDtypeStruct(adjoint.shape, F32),
        scratch_shapes=[
            pltpu.VMEM((2, levels, rows, cols), F32),
            pltpu.VMEM((2, rows, cols), F32),
            pltpu.SemaphoreType.DMA((2,)),
        ],
        input_output_aliases={6: 0},
        compiler_params=params(),
    )(lowered, lower, upper, mine, bulk, got_edges, partial)


LEVEL_UNROLL = 16


def with_halo(block, sides, width):
    for axis, dim in sides:
        count = lax.axis_size(axis)
        forward = [(i, i + 1) for i in range(count - 1)]
        forward.append((count - 1, 0))
        backward = [(target, source) for source, target in forward]
        low = lax.ppermute(
            lax.slice_in_dim(block, block.shape[dim] - width, None, axis=dim), axis, forward
        )
        high = lax.ppermute(lax.slice_in_dim(block, 0, width, axis=dim), axis, backward)
        block = jnp.concatenate([low, block, high], axis=dim)
    return block


def centered_roll(values, axis_id):
    ahead_one = jnp.roll(values, -1, axis_id)
    behind_one = jnp.roll(values, 1, axis_id)
    ahead_two = jnp.roll(values, -2, axis_id)
    behind_two = jnp.roll(values, 2, axis_id)
    return (8.0 * (ahead_one - behind_one) - (ahead_two - behind_two)) / 12.0


def centered_padded(padded):
    ahead_one = padded[:, :, 3:-1, :]
    behind_one = padded[:, :, 1:-3, :]
    ahead_two = padded[:, :, 4:, :]
    behind_two = padded[:, :, :-4, :]
    return (8.0 * (ahead_one - behind_one) - (ahead_two - behind_two)) / 12.0


def mat_vec(system_matrix, vector):
    return jnp.stack(
        [
            system_matrix[0] * vector[0] + system_matrix[1] * vector[1],
            system_matrix[2] * vector[0] + system_matrix[3] * vector[1],
        ]
    )


def chain_run(coupling, forcing, initial, backward):

    def advance(state, inputs):
        fresh = mat_vec(inputs[0], state) + inputs[1]
        return (fresh, fresh)

    final_state, states = lax.scan(
        advance,
        initial,
        (jnp.moveaxis(coupling, 1, 0), jnp.moveaxis(forcing, 1, 0)),
        reverse=backward,
        unroll=min(LEVEL_UNROLL, coupling.shape[1]),
    )
    return jnp.moveaxis(states, 0, 1)


def column_solve(pieces):
    forcing, lower_part, upper_part = pieces
    initial = jnp.zeros((2,) + forcing.shape[2:], jnp.float32)
    lowered = chain_run(lower_part, forcing, initial, False)
    solved = chain_run(upper_part, lowered, initial, True)
    return lax.all_to_all(solved, "lev", split_axis=1, concat_axis=2, tiled=True)


def local_any(adjoint, courant, metric, pivot_inverse, lower_gain, upper_gain):
    weighted = jnp.concatenate([courant[0] * adjoint, (metric[0] * adjoint[0])[None]], 0)
    padded = with_halo(weighted, (("tile", 2),), 2)
    across = centered_padded(padded)
    advected = adjoint + across[:5] + centered_roll(courant[1] * adjoint, 3)
    pressure_field = advected[4] + across[5] + centered_roll(metric[1] * adjoint[1], 2)
    forcing = mat_vec(pivot_inverse, jnp.stack([advected[2], pressure_field]))
    solved = column_solve(
        (
            lax.all_to_all(forcing, "lev", split_axis=2, concat_axis=1, tiled=True),
            lax.all_to_all(lower_gain, "lev", split_axis=2, concat_axis=1, tiled=True),
            lax.all_to_all(upper_gain, "lev", split_axis=2, concat_axis=1, tiled=True),
        )
    )
    return jnp.stack([advected[0], advected[1], solved[0], advected[3], solved[1]])


def solution(mesh):
    placed = (P(None, "lev", "tile", None),) * 6
    pair = mesh.shape["lev"] == 2 and mesh.shape["tile"] % 2 == 0

    def local(adjoint, *others):
        levels, rows = adjoint.shape[1:3]
        fits = pair and levels % EDGE_LEVELS == 0 and rows % 8 == 0 and rows > 8
        return (local_pair if fits else local_any)(adjoint, *others)

    return jax.shard_map(
        local,
        mesh=mesh,
        in_specs=placed,
        out_specs=P(None, "lev", "tile", None),
        check_vma=False,
    )
```
